32 devices in a mesh: grp: 2 (over y), pts: 4 (over z), spec: 2 (over x), cpl: 2 (over core).
Axes of the slice: x: 2, y: 2, z: 4, core: 2. Of those that a mesh axis runs over, the one named last changes fastest.
Arguments:
- spec_deck: float32 [32, 36, 16384], P('spec', 'cpl', ('grp', 'pts')), parts along dimension 2, may hold values from 0 to 1, as said below
- wind_deck: float32 [2, 16384], P(None, ('grp', 'pts')), parts along dimension 1, may hold values from -24 to 24
- cell_sea: int32 [256, 128], P('grp'), parts along dimension 0, may hold values from -1 to 8191, as said below
- atm_order: int32 [16384], P(('grp', 'pts', 'spec')), parts along dimension 0, may hold values from 0 to 8191, as said below
- ocean_order: int32 [16384], P(('grp', 'pts', 'spec')), parts along dimension 0, may hold values from 0 to 8191, as said below
Outputs:
- spec_out: float32 [32, 36, 16384], P('spec', 'cpl', ('grp', 'pts')), parts along dimension 2
- stress_atm: float32 [2, 16384], P('cpl', ('grp', 'pts', 'spec')), parts along dimension 1
- stokes_ocn: float32 [2, 16384], P('cpl', ('grp', 'pts', 'spec')), parts along dimension 1
The draws below stay inside these ranges and needn't reach their ends.
There are 2 independent parts, one for each index of `grp`. The reference program is written for one: setup_inputs(seed, part) draws one part's arguments, and reference() takes and returns one part's arrays. A program takes and returns all parts, laid end to end along the dimension named above; each array names one. Nothing has to cross between parts.
Inputs may be any that keep to these rules, and one draw needn't show every extreme that they name: `cell_sea`: -1 marks land. Sea cells carry the numbers 0 to 8191 in row-major order, each once. Every grid row holds 32 or more sea cells, and some row exactly 32. In every draw some block of 32 rows starting at a multiple of 32 is all sea. `spec_deck`: spectral densities. `atm_order`: each sea point once. In every aligned block of 1024 rows, exactly 256 rows name sea points s of each value of s mod 4. `ocean_order`: each sea point once. In every aligned block of 1024 rows, exactly 256 rows name sea points s of each value of s mod 4.
All inputs are finite; a program needn't handle non-finite values.
Results may differ from the reference program's by a relative error of at most 0.00002.
Values sent between devices are 32-bit elements; how exact they have to be, the bound alone decides.
No kernel may reach another device: no remote copies, remote signals or barrier semaphores. Data moves between devices by JAX's collectives and lax.ppermute only.
A program may use at most 192 MiB of HBM per device.

```python
import math
import jax
import jax.numpy as jnp
from jax import lax

NF = 32
ND = 36
NSUB = 1
TX = 32
NY = 128
OWNERS = 4
NX = 128
SEA_DEV = 2048
NSEA = 8192
ROWS_DEV = 1024


def draw_cell_sea(key, part):
    key = jax.random.fold_in(key, 5)
    key_full, key_bias, key_score, key_rank, key_strip, key_line = jax.random.split(key, 6)
    full_strip = jax.random.randint(key_full, (), 0, OWNERS)
    strip_bias = jax.random.randint(key_bias, (OWNERS,), 0, 4)
    lean_strip = (full_strip + 1 + jax.random.randint(key_strip, (), 0, OWNERS - 1)) % OWNERS
    lean_row = lean_strip * TX + jax.random.randint(key_line, (), 0, TX)
    row_index = jnp.arange(NX)
    row_strip = row_index // TX
    column_score = jax.random.randint(key_rank, (NX, NY), 0, 1 << 16)
    column_order = jnp.argsort(column_score, axis=1, stable=True)
    column_rank = jnp.argsort(column_order, axis=1, stable=True)
    forced = column_rank < NY // 4
    scores = jax.random.randint(key_score, (NX, NY), 0, 4096) + (strip_bias[row_strip] * 1024)[:, None] + jnp.where(row_strip == full_strip, 16384, 0)[:, None] + jnp.where(forced, 32768, 0)
    scores = jnp.where((row_index[:, None] == lean_row) & jnp.logical_not(forced), -1, scores)
    ranked = jnp.argsort(-scores.reshape(-1), stable=True)
    is_sea = jnp.zeros((NX * NY,), jnp.int32).at[ranked[:NSEA]].set(1)
    sea_number = jnp.cumsum(is_sea) - 1
    return jnp.where(is_sea == 1, sea_number, -1).reshape(NX, NY).astype(jnp.int32)


def block_rows(key):
    key_slots, key_mix = jax.random.split(key, 2)
    blocks = NSEA // ROWS_DEV
    per_owner = ROWS_DEV // OWNERS
    slot_score = jax.random.randint(key_slots, (OWNERS, SEA_DEV), 0, 1 << 20)
    slots = jnp.argsort(slot_score, axis=1, stable=True).astype(jnp.int32)
    points = slots * OWNERS + jnp.arange(OWNERS, dtype=jnp.int32)[:, None]
    points = points.reshape(OWNERS, blocks, per_owner).transpose(1, 0, 2).reshape(blocks, ROWS_DEV)
    mix_score = jax.random.randint(key_mix, (blocks, ROWS_DEV), 0, 1 << 20)
    mixing = jnp.argsort(mix_score, axis=1, stable=True)
    return jnp.take_along_axis(points, mixing, axis=1).reshape(NSEA).astype(jnp.int32)


def draw_atm_order(key, part):
    key = jax.random.fold_in(key, 21)
    return block_rows(key)


def draw_ocean_order(key, part):
    key = jax.random.fold_in(key, 33)
    return block_rows(key)


def draw_spec_deck(key, part):
    key = jax.random.fold_in(key, 9)
    key_base, key_freq, key_dir = jax.random.split(key, 3)
    base_level = jnp.exp(jax.random.uniform(key_base, (NF, ND, NSEA), jnp.float32, math.log(0.05), 0.0))
    freq_scale = jnp.exp(jax.random.uniform(key_freq, (NF, 1, 1), jnp.float32, math.log(0.1), 0.0))
    dir_scale = jnp.exp(jax.random.uniform(key_dir, (1, ND, 1), jnp.float32, math.log(0.1), 0.0))
    return (base_level * freq_scale * dir_scale).astype(jnp.float32)


def shard_levels(rng, extent, shards, low, largest):
    gain = 1.0
    for position, parts in shards:
        heights = jax.random.uniform(jax.random.fold_in(jax.random.fold_in(rng, 6), position), (parts,), jnp.float32, low / len(shards), largest / len(shards))
        gain = gain * jnp.repeat(jnp.exp(heights), extent[position] // parts).reshape((-1,) + (1,) * (len(extent) - 1 - position))
    return gain


def noise(rng, dims, deviation, reach, pieces=(), kind=jnp.bfloat16):
    result = deviation * jax.random.normal(rng, dims, jnp.float32)
    if pieces:
        result = result * shard_levels(rng, dims, pieces, -0.22, 0.18)
    return jnp.clip(result, -reach, reach).astype(kind)


def setup_inputs(seed: int = 0, part: int = 0) -> dict:
    key_list = jax.random.split(jax.random.key(seed), 6)
    part_keys = jax.random.split(jax.random.fold_in(key_list[5], part), 6)
    spec_deck = draw_spec_deck(jax.random.fold_in(jax.random.fold_in(key_list[5], part), 71), part)
    wind_deck = noise(part_keys[1], (2, NSEA), 8.0, 24.0, ((1, 4),), jnp.float32)
    cell_sea = draw_cell_sea(jax.random.fold_in(jax.random.fold_in(key_list[5], part), 71), part)
    atm_order = draw_atm_order(jax.random.fold_in(jax.random.fold_in(key_list[5], part), 71), part)
    ocean_order = draw_ocean_order(jax.random.fold_in(jax.random.fold_in(key_list[5], part), 71), part)
    return {"spec_deck": spec_deck, "wind_deck": wind_deck, "cell_sea": cell_sea, "atm_order": atm_order, "ocean_order": ocean_order}


COURANT_MAX = 0.68
BASE_FREQ = 0.035
GRAVITY = 9.81
GROWTH_RATE = 0.02
SLOPE_REF = 0.09
STRESS_GAIN = 64.0
STOKES_GAIN = 64.0

def upwind(extended, mask_rows, courant_east, courant_north):
    middle = extended[:, :, 1:-1]
    prior_row = extended[:, :, :-2]
    next_row = extended[:, :, 2:]
    side_pad = jnp.pad(middle, ((0, 0), (0, 0), (0, 0), (1, 1)))
    prior_col = side_pad[..., :-2]
    next_col = side_pad[..., 2:]
    advanced = middle - jnp.maximum(courant_east, 0.0) * (middle - prior_row) - jnp.maximum(-courant_east, 0.0) * (middle - next_row) - jnp.maximum(courant_north, 0.0) * (middle - prior_col) - jnp.maximum(-courant_north, 0.0) * (middle - next_col)
    return advanced * mask_rows

def reference(spec_deck, wind_deck, cell_sea, atm_order, ocean_order):
    flat_map = cell_sea.reshape(-1)
    is_sea = flat_map >= 0
    safe_index = jnp.maximum(flat_map, 0)
    deck_col = safe_index % OWNERS * SEA_DEV + safe_index // OWNERS
    grid_field = jnp.take(spec_deck, deck_col, axis=2) * is_sea.astype(jnp.float32)
    grid_field = grid_field.reshape(NF, ND, NX, NY)
    freq_index = jnp.arange(NF).astype(jnp.float32)
    angles = 2.0 * math.pi * (jnp.arange(ND).astype(jnp.float32) + 0.5) / ND
    dir_cosine = jnp.cos(angles)
    dir_sine = jnp.sin(angles)
    speeds = COURANT_MAX * jnp.power(1.1, -freq_index)
    courant_east = (speeds[:, None] * dir_cosine[None, :])[:, :, None, None]
    courant_north = (speeds[:, None] * dir_sine[None, :])[:, :, None, None]
    sea_field = is_sea.astype(jnp.float32).reshape(NX, NY)
    for substep in range(NSUB):
        extended = jnp.pad(grid_field, ((0, 0), (0, 0), (1, 1), (0, 0)))
        grid_field = upwind(extended, sea_field, courant_east, courant_north)
    grid_field = grid_field.reshape(NF, ND, NX * NY)
    cell_of_point = jnp.zeros((NSEA,), jnp.int32).at[jnp.where(is_sea, flat_map, NSEA)].set(jnp.arange(NX * NY, dtype=jnp.int32), mode='drop')
    slot_all = jnp.arange(NSEA, dtype=jnp.int32)
    sea_of_slot = slot_all % SEA_DEV * OWNERS + slot_all // SEA_DEV
    propagated = jnp.take(grid_field, cell_of_point[sea_of_slot], axis=2)
    sigma_freq = 2.0 * math.pi * BASE_FREQ * jnp.power(1.1, freq_index)
    phase_speed = GRAVITY / sigma_freq
    slope_weight = jnp.power(1.1, 0.4 * freq_index)
    slope_total = lax.optimization_barrier(jnp.sum(propagated * slope_weight[:, None, None], axis=(0, 1))) / (SLOPE_REF * NF * ND)
    wind_along = wind_deck[0][None, None, :] * dir_cosine[None, :, None] + wind_deck[1][None, None, :] * dir_sine[None, :, None]
    growth = GROWTH_RATE * sigma_freq[:, None, None] * jnp.maximum(wind_along / phase_speed[:, None, None] - 1.0, 0.0)
    sigma_top = 2.0 * math.pi * BASE_FREQ * 1.1 ** (NF - 1)
    damping = (sigma_freq / sigma_top)[:, None, None] * (slope_total * slope_total)[None, None, :]
    updated = propagated * jnp.exp(growth - damping)
    lifted = growth * propagated
    drift_part = updated * jnp.power(1.1, 2.0 * (freq_index - (NF - 1)))[:, None, None]
    stress_scale = STRESS_GAIN / NF
    stokes_scale = STOKES_GAIN / math.sqrt(NF * ND)
    coupled = jnp.stack([stress_scale * lax.optimization_barrier(jnp.sum(lifted * dir_cosine[None, :, None], axis=(0, 1))), stress_scale * lax.optimization_barrier(jnp.sum(lifted * dir_sine[None, :, None], axis=(0, 1))), stokes_scale * lax.optimization_barrier(jnp.sum(drift_part * dir_cosine[None, :, None], axis=(0, 1))), stokes_scale * lax.optimization_barrier(jnp.sum(drift_part * dir_sine[None, :, None], axis=(0, 1)))])
    atm_col = atm_order % OWNERS * SEA_DEV + atm_order // OWNERS
    ocean_col = ocean_order % OWNERS * SEA_DEV + ocean_order // OWNERS
    stress_atm = jnp.take(coupled[0:2], atm_col, axis=1)
    stokes_ocn = jnp.take(coupled[2:4], ocean_col, axis=1)
    return (updated, stress_atm, stokes_ocn)
```

```python
import functools
import math

import jax
import jax.numpy as jnp
from jax import lax
from jax.experimental import pallas as pl
from jax.experimental.pallas import tpu as pltpu
from jax.sharding import PartitionSpec as P

COURANT_MAX = 0.68
BASE_FREQ = 0.035
GRAVITY = 9.81
GROWTH_RATE = 0.02
SLOPE_REF = 0.09
STRESS_GAIN = 64.0
STOKES_GAIN = 64.0
LANES = 128
F32 = jnp.float32
BF16 = jnp.bfloat16
I32 = jnp.int32
WHOLE = pl.BlockSpec(memory_space=pltpu.VMEM)
SCALARS = pl.BlockSpec(memory_space=pltpu.SMEM)


def passed_along(shard, axis, by):
    devices = lax.axis_size(axis)
    pairs = [(i, i + by) for i in range(devices) if 0 <= i + by < devices]
    return lax.ppermute(shard, axis, pairs)


def upwind(extended, mask_rows, courant_east, courant_north):
    middle = extended[:, :, 1:-1]
    prior_row = extended[:, :, :-2]
    next_row = extended[:, :, 2:]
    side_pad = jnp.pad(middle, ((0, 0), (0, 0), (0, 0), (1, 1)))
    prior_col = side_pad[..., :-2]
    next_col = side_pad[..., 2:]
    advanced = (
        middle
        - jnp.maximum(courant_east, 0.0) * (middle - prior_row)
        - jnp.maximum(-courant_east, 0.0) * (middle - next_row)
        - jnp.maximum(courant_north, 0.0) * (middle - prior_col)
        - jnp.maximum(-courant_north, 0.0) * (middle - next_col)
    )
    return advanced * mask_rows


def general(spec_deck, wind_deck, cell_sea, atm_order, ocean_order):
    owners = lax.axis_size("pts")
    spec_groups = lax.axis_size("spec")
    cpl_groups = lax.axis_size("cpl")
    my_pts = lax.axis_index("pts")
    my_spec = lax.axis_index("spec")
    my_cpl = lax.axis_index("cpl")
    freq_local, dirs_local, slots_local = spec_deck.shape
    grid_rows, grid_cols = cell_sea.shape
    freq_count = freq_local * spec_groups
    dir_count = dirs_local * cpl_groups
    sea_mask = cell_sea >= 0
    row_counts = jnp.sum(sea_mask.astype(jnp.int32), axis=1)
    before_row = jnp.concatenate([jnp.zeros((1,), jnp.int32), jnp.cumsum(row_counts)])
    tile_freq = my_spec * freq_local + jnp.arange(freq_local)
    height = 2 * (grid_rows // owners)
    capacity = (slots_local + grid_cols) // owners + 1
    targets = jnp.arange(owners + 1, dtype=jnp.int32) * slots_local
    row_starts = jnp.sum((before_row[None, :] < targets[:, None]).astype(jnp.int32), axis=1)
    width_cells = height * grid_cols
    bounds = jnp.take(before_row, row_starts)
    starts = bounds[:-1]
    my_row = jnp.take(row_starts, my_pts)
    my_height = jnp.take(row_starts, my_pts + 1) - my_row
    first_slot = -((jnp.arange(owners, dtype=jnp.int32)[None, :] - starts[:, None]) // owners)
    slot_range = jnp.arange(capacity, dtype=jnp.int32)
    own_first = jnp.take(first_slot, my_pts, axis=1)
    picked = jnp.clip(own_first[:, None] + slot_range[None, :], 0, slots_local - 1).reshape(-1)
    outgoing = jnp.take(spec_deck, picked, axis=2)
    arrived = lax.all_to_all(outgoing, "pts", split_axis=2, concat_axis=2, tiled=True)
    freq_here = arrived.shape[0]
    padded_map = jnp.concatenate([cell_sea, jnp.full((height, grid_cols), -1, jnp.int32)], axis=0)
    strip_map = lax.dynamic_slice_in_dim(padded_map, my_row, height, 0)
    row_valid = jnp.arange(height) < my_height
    strip_sea = ((strip_map >= 0) & row_valid[:, None]).reshape(-1)
    strip_map = strip_map.reshape(-1)
    safe_index = jnp.maximum(strip_map, 0)
    source = safe_index % owners
    strip_first = jnp.take(first_slot, my_pts, axis=0)
    where_from = jnp.where(
        strip_sea, source * capacity + safe_index // owners - jnp.take(strip_first, source), 0
    )
    wave_field = jnp.take(arrived, where_from, axis=2) * strip_sea.astype(jnp.float32)
    wave_field = wave_field.reshape(freq_here, dirs_local, height, grid_cols)
    freq_index = tile_freq.astype(jnp.float32)
    dir_index = (my_cpl * dirs_local + jnp.arange(dirs_local)).astype(jnp.float32)
    angles = 2.0 * math.pi * (dir_index + 0.5) / dir_count
    dir_cosine = jnp.cos(angles)
    dir_sine = jnp.sin(angles)
    speeds = COURANT_MAX * jnp.power(1.1, -freq_index)
    courant_east = (speeds[:, None] * dir_cosine[None, :])[:, :, None, None]
    courant_north = (speeds[:, None] * dir_sine[None, :])[:, :, None, None]
    strip_mask = strip_sea.astype(jnp.float32).reshape(height, grid_cols)
    last_row = lax.dynamic_slice_in_dim(wave_field, my_height - 1, 1, 2)
    from_above = passed_along(last_row, "pts", 1)
    from_below = passed_along(wave_field[:, :, :1], "pts", -1)
    extended = jnp.concatenate([from_above, wave_field, jnp.zeros_like(from_below)], axis=2)
    extended = lax.dynamic_update_slice_in_dim(extended, from_below, my_height + 1, 2)
    wave_field = upwind(extended, strip_mask, courant_east, courant_north)
    flat_field = wave_field.reshape(freq_here, dirs_local, width_cells)
    strip_start = jnp.take(starts, my_pts)
    inverse = (
        jnp.zeros((width_cells,), jnp.int32)
        .at[jnp.where(strip_sea, strip_map - strip_start, width_cells)]
        .set(jnp.arange(width_cells, dtype=jnp.int32), mode="drop")
    )
    wanted = (strip_first[:, None] + slot_range[None, :]) * owners + jnp.arange(
        owners, dtype=jnp.int32
    )[:, None]
    cells_out = jnp.take(inverse, jnp.clip(wanted - strip_start, 0, width_cells - 1).reshape(-1))
    leaving = jnp.take(flat_field, cells_out, axis=2)
    returned = lax.all_to_all(leaving, "pts", split_axis=2, concat_axis=2, tiled=True)
    slot_index = jnp.arange(slots_local, dtype=jnp.int32)
    points = slot_index * owners + my_pts
    strip_of = jnp.sum((starts[None, 1:] <= points[:, None]).astype(jnp.int32), axis=1)
    offset = slot_index - jnp.take(own_first, strip_of)
    position = strip_of * capacity + offset
    propagated = jnp.take(returned, position, axis=2)
    band_freq = (my_spec * freq_local + jnp.arange(freq_local)).astype(jnp.float32)
    sigma_freq = 2.0 * math.pi * BASE_FREQ * jnp.power(1.1, band_freq)
    phase_speed = GRAVITY / sigma_freq
    slope_weight = jnp.power(1.1, 0.4 * band_freq)
    slope_part = jnp.sum(propagated * slope_weight[:, None, None], axis=(0, 1))
    slope_total = lax.psum(slope_part, ("spec", "cpl")) / (SLOPE_REF * freq_count * dir_count)
    wind_along = (
        wind_deck[0][None, None, :] * dir_cosine[None, :, None]
        + wind_deck[1][None, None, :] * dir_sine[None, :, None]
    )
    growth = (
        GROWTH_RATE
        * sigma_freq[:, None, None]
        * jnp.maximum(wind_along / phase_speed[:, None, None] - 1.0, 0.0)
    )
    sigma_top = 2.0 * math.pi * BASE_FREQ * 1.1 ** (freq_count - 1)
    damping = (sigma_freq / sigma_top)[:, None, None] * (slope_total * slope_total)[None, None, :]
    updated = propagated * jnp.exp(growth - damping)
    lifted = growth * propagated
    drift_part = updated * jnp.power(1.1, 2.0 * (band_freq - (freq_count - 1)))[:, None, None]
    stress_scale = STRESS_GAIN / freq_count
    stokes_scale = STOKES_GAIN / math.sqrt(freq_count * dir_count)
    coupled_part = jnp.stack(
        [
            stress_scale * jnp.sum(lifted * dir_cosine[None, :, None], axis=(0, 1)),
            stress_scale * jnp.sum(lifted * dir_sine[None, :, None], axis=(0, 1)),
            stokes_scale * jnp.sum(drift_part * dir_cosine[None, :, None], axis=(0, 1)),
            stokes_scale * jnp.sum(drift_part * dir_sine[None, :, None], axis=(0, 1)),
        ]
    )
    coupled_total = lax.psum(coupled_part, ("spec", "cpl"))
    coupled_all = lax.all_gather(coupled_total, "pts", axis=1, tiled=True)
    atm_col = atm_order % owners * slots_local + atm_order // owners
    ocean_col = ocean_order % owners * slots_local + ocean_order // owners
    stress_atm = jnp.take(lax.dynamic_slice_in_dim(coupled_all, my_cpl, 1, 0), atm_col, axis=1)
    stokes_ocn = jnp.take(
        lax.dynamic_slice_in_dim(coupled_all, 2 + my_cpl, 1, 0), ocean_col, axis=1
    )
    return (updated, stress_atm, stokes_ocn)


C_KEEP, C_ROW, C_COL, C_SLOPE, C_EAST, C_NORTH, C_ONE, C_DAMP = range(8)
C_S_EAST, C_S_NORTH, C_T_EAST, C_T_NORTH = range(8, 12)


def split3(value):
    high = value.astype(BF16)
    rest = value - high.astype(F32)
    middle = rest.astype(BF16)
    low = (rest - middle.astype(F32)).astype(BF16)
    return high, middle, low


def times_exact(value, one_hot, dims):
    parts = [
        lax.dot_general(part, one_hot, (dims, ((), ())), preferred_element_type=F32)
        for part in split3(value)
    ]
    return parts[0] + parts[1] + parts[2]


def index_kernel(owners, par_ref, cell_ref, g_ref, idx_ref, *list_refs):
    slots = idx_ref.shape[1]
    blocks = slots // LANES
    half_rows = g_ref.shape[0] // 2
    shift = owners.bit_length() - 1
    pts = par_ref[0]
    number = cell_ref[...].astype(F32)
    sea = number >= 0.0
    first = jnp.min(jnp.where(sea, number, 1e9), axis=1, keepdims=True)
    last = jnp.max(jnp.where(sea, number, -1.0), axis=1, keepdims=True)
    rank = jnp.where(sea, number - first + 1.0, 0.0)
    edge = jnp.full((1, number.shape[1]), -1.0, F32)
    above = jnp.concatenate([edge, number[:-1]], axis=0)
    below = jnp.concatenate([number[1:], edge], axis=0)
    to_above = jnp.where(sea & (above >= 0.0), number - above, 0.0)
    to_below = jnp.where(sea & (below >= 0.0), below - number, 0.0)
    cols = number.shape[1]
    column = lax.broadcasted_iota(I32, number.shape, 1)
    left = jnp.where(column == 0, -1.0, pltpu.roll(number, 1, 1))
    right = jnp.where(column == cols - 1, -1.0, pltpu.roll(number, cols - 1, 1))
    beside = jnp.where(par_ref[4] == 0, left, right)
    beside = jnp.where(sea & (beside >= 0.0), 1.0, 0.0)

    slot = lax.broadcasted_iota(I32, (1, slots), 1)
    point = slot * owners + pts
    pointf = point.astype(F32)
    in_row = (first <= pointf) & (pointf <= last)
    row_hot = jnp.where(in_row, 1.0, 0.0).astype(BF16)
    row_first = jnp.sum(jnp.where(in_row, first, 0.0), axis=0, keepdims=True)

    def of_row(values):
        return jnp.dot(
            jnp.transpose(values).astype(BF16), row_hot, preferred_element_type=F32
        )

    here = of_row(rank) == (pointf - row_first + 1.0)

    def of_point(values):
        return jnp.sum(jnp.where(here, of_row(values), 0.0), axis=0, keepdims=True)

    step_above = of_point(to_above).astype(I32)
    step_below = of_point(to_below).astype(I32)
    has_beside = of_point(beside).astype(I32)

    groups = max(8, owners)
    group = lax.broadcasted_iota(I32, (groups, slots), 0)
    codes, masks = [], []
    for half in range(2):
        up = par_ref[1 + half] < 0
        for sends in range(2):
            minus = up if sends == 0 else jnp.logical_not(up)
            step = jnp.where(minus, step_above, step_below)
            other = jnp.where(minus, point - step_above, point + step_below)
            owner = other & (owners - 1)
            away = (pts - owner) if sends == 0 else (owner - pts)
            away = jnp.where(step > 0, away & (owners - 1), -1)
            codes.append((away, other >> shift))
            masks.append(jnp.where(group == away, 1.0, 0.0))
    mask = jnp.concatenate(masks, axis=0)
    before = jnp.where(
        lax.broadcasted_iota(I32, (LANES, LANES), 0) < lax.broadcasted_iota(I32, (LANES, LANES), 1),
        1.0,
        0.0,
    ).astype(BF16)
    carry = jnp.zeros((mask.shape[0], 1), F32)
    counts = []
    for block in range(blocks):
        part = mask[:, block * LANES : (block + 1) * LANES]
        inside = jnp.dot(part.astype(BF16), before, preferred_element_type=F32)
        counts.append((inside + carry) * part)
        carry = carry + jnp.sum(part, axis=1, keepdims=True)
    counts = jnp.concatenate(counts, axis=1)
    excess = jnp.zeros((1, slots), I32)
    entry = lax.broadcasted_iota(I32, ((owners - 1) * LANES, slots), 0)
    for half in range(2):
        places = [
            jnp.sum(
                counts[(2 * half + sends) * groups : (2 * half + sends + 1) * groups],
                axis=0,
                keepdims=True,
            ).astype(I32)
            for sends in range(2)
        ]
        away, other_slot = codes[2 * half]
        place = places[0]
        excess = jnp.maximum(excess, jnp.where((away > 0) & (place >= LANES), 1, 0))
        same_block = (other_slot >> 7) == (slot >> 7)
        code = jnp.where(away == 0, jnp.where(same_block, 1, 2), away + 2)
        code = jnp.where(away < 0, 0, code)
        lane = jnp.where(away == 0, other_slot & (LANES - 1), jnp.minimum(place, LANES - 1))
        idx_ref[2 * half : 2 * half + 1, :] = jnp.where(away < 0, 0, lane)
        idx_ref[2 * half + 1 : 2 * half + 2, :] = code
        away, _ = codes[2 * half + 1]
        place = places[1]
        key = jnp.where((away > 0) & (place < LANES), (away - 1) * LANES + place, -1)
        one_hot = jnp.where(entry == key, 1.0, 0.0).astype(BF16)
        rows = slice(half * half_rows, (half + 1) * half_rows)
        packed = times_exact(g_ref[rows, :], one_hot, ((1,), (1,)))
        for at, list_ref in enumerate(list_refs):
            list_ref[rows, :] = packed[:, at * LANES : (at + 1) * LANES]
    idx_ref[4:5, :] = has_beside
    idx_ref[5:6, :] = excess
    idx_ref[6:8, :] = jnp.zeros((2, slots), I32)


def lane_take(values, lanes):
    return jnp.take_along_axis(values, lanes, axis=1)


def advance_kernel(owners, par_ref, coef_ref, idx_ref, g_ref, beside_ref, *refs):
    list_refs = refs[: owners - 1]
    out_ref, slope_ref, total_ref = refs[owners - 1 :]
    slots = idx_ref.shape[1]
    blocks = slots // LANES
    tiles = g_ref.shape[0] // 16
    shape = (8, LANES)
    total_ref[...] = jnp.zeros_like(total_ref)
    turn = par_ref[3]
    lane = lax.broadcasted_iota(I32, shape, 1)
    beside_lane = (lane + turn) & (LANES - 1)
    beyond = (lane + turn) != beside_lane

    for half in range(2):
        way = par_ref[1 + half]

        @pl.loop(0, tiles)
        def _(tile):
            rows = pl.ds(pl.multiple_of((half * tiles + tile) * 8, 8), 8)
            coef = coef_ref[rows, :]

            def factor(at):
                return jnp.broadcast_to(coef[:, at : at + 1], shape)

            keep, by_row, by_col = factor(C_KEEP), factor(C_ROW), factor(C_COL)
            by_slope = factor(C_SLOPE)
            lists = [ref[rows, :] for ref in list_refs]
            for block in range(blocks):
                at = slice(block * LANES, (block + 1) * LANES)

                def near(ref, step):
                    which = jnp.clip(block + step, 0, blocks - 1)
                    return ref[rows, pl.ds(pl.multiple_of(which * LANES, LANES), LANES)]

                lanes = jnp.broadcast_to(idx_ref[2 * half : 2 * half + 1, at], shape)
                code = jnp.broadcast_to(idx_ref[2 * half + 1 : 2 * half + 2, at], shape)
                has_beside = jnp.broadcast_to(idx_ref[4:5, at], shape)
                own = g_ref[rows, at]
                row_value = jnp.where(code == 1, lane_take(own, lanes), 0.0)
                row_value = jnp.where(code == 2, lane_take(near(g_ref, way), lanes), row_value)
                for number, values in enumerate(lists):
                    row_value = jnp.where(code == 3 + number, lane_take(values, lanes), row_value)
                col_value = jnp.where(
                    beyond,
                    lane_take(near(beside_ref, turn), beside_lane),
                    lane_take(beside_ref[rows, at], beside_lane),
                )
                col_value = jnp.where(has_beside > 0, col_value, 0.0)
                moved = keep * own + by_row * row_value + by_col * col_value
                out_ref[rows, at] = moved
                total_ref[:, at] += by_slope * moved

    slope_ref[...] = jnp.sum(total_ref[...], axis=0, keepdims=True)


def source_kernel(coef_ref, wind_ref, slope_ref, prop_ref, out_ref, sums_ref, total_ref):
    slots = prop_ref.shape[1]
    blocks = slots // LANES
    shape = (8, LANES)
    total_ref[...] = jnp.zeros_like(total_ref)

    @pl.loop(0, prop_ref.shape[0] // 8)
    def _(tile):
        rows = pl.ds(pl.multiple_of(tile * 8, 8), 8)
        coef = coef_ref[rows, :]

        def factor(at):
            return jnp.broadcast_to(coef[:, at : at + 1], shape)

        east, north, one, damp = factor(C_EAST), factor(C_NORTH), factor(C_ONE), factor(C_DAMP)
        s_east, s_north = factor(C_S_EAST), factor(C_S_NORTH)
        t_east, t_north = factor(C_T_EAST), factor(C_T_NORTH)
        for block in range(blocks):
            at = slice(block * LANES, (block + 1) * LANES)
            wind_east = jnp.broadcast_to(wind_ref[0:1, at], shape)
            wind_north = jnp.broadcast_to(wind_ref[1:2, at], shape)
            slope = jnp.broadcast_to(slope_ref[0:1, at], shape)
            value = prop_ref[rows, at]
            growth = jnp.maximum(east * wind_east + north * wind_north - one, 0.0)
            updated = value * jnp.exp(growth - damp * (slope * slope))
            out_ref[rows, at] = updated
            lifted = growth * value
            total_ref[0, :, at] += s_east * lifted
            total_ref[1, :, at] += s_north * lifted
            total_ref[2, :, at] += t_east * updated
            total_ref[3, :, at] += t_north * updated

    for item in range(4):
        for block in range(blocks):
            at = slice(block * LANES, (block + 1) * LANES)
            sums_ref[item, block : block + 1, :] = jnp.sum(
                total_ref[item, :, at], axis=0, keepdims=True
            )


def pick_kernel(owners, table_ref, atm_ref, ocean_ref, stress_ref, stokes_ref):
    shift = owners.bit_length() - 1
    blocks = table_ref.shape[1] // owners
    for item, (order_ref, out_ref) in enumerate(((atm_ref, stress_ref), (ocean_ref, stokes_ref))):
        point = order_ref[...]
        count = point.shape[1]
        slot = point >> shift
        row = (point & (owners - 1)) * blocks + (slot >> 7)
        lane = slot & (LANES - 1)
        rows = table_ref.shape[1]
        hot = jnp.where(lax.broadcasted_iota(I32, (rows, count), 0) == row, 1.0, 0.0).astype(BF16)
        table = jnp.transpose(table_ref[item])
        found = times_exact(table, hot, ((1,), (0,)))
        pick = lax.broadcasted_iota(I32, (LANES, count), 0) == lane
        out_ref[...] = jnp.sum(jnp.where(pick, found, 0.0), axis=0, keepdims=True)


def coefficients(freq_local, dirs_local, pad_half, my_spec, my_cpl, freq_count, dir_count):
    freq = (my_spec * freq_local + jnp.arange(freq_local)).astype(F32)
    direction = (my_cpl * dirs_local + jnp.arange(dirs_local)).astype(F32)
    angles = 2.0 * math.pi * (direction + 0.5) / dir_count
    cosine, sine = jnp.cos(angles)[:, None], jnp.sin(angles)[:, None]
    speed = COURANT_MAX * jnp.power(1.1, -freq)[None, :]
    by_row, by_col = jnp.abs(speed * cosine), jnp.abs(speed * sine)
    sigma = (2.0 * math.pi * BASE_FREQ * jnp.power(1.1, freq))[None, :]
    sigma_top = 2.0 * math.pi * BASE_FREQ * 1.1 ** (freq_count - 1)
    inverse_speed = sigma / GRAVITY
    rate = GROWTH_RATE * sigma
    drift = jnp.power(1.1, 2.0 * (freq - (freq_count - 1)))[None, :]
    stress_scale = STRESS_GAIN / freq_count
    stokes_scale = STOKES_GAIN / math.sqrt(freq_count * dir_count)
    shape = (dirs_local, freq_local)
    columns = [
        1.0 - by_row - by_col,
        by_row,
        by_col,
        jnp.power(1.1, 0.4 * freq)[None, :] / (SLOPE_REF * freq_count * dir_count),
        rate * inverse_speed * cosine,
        rate * inverse_speed * sine,
        rate,
        sigma / sigma_top,
        stress_scale * cosine,
        stress_scale * sine,
        stokes_scale * drift * cosine,
        stokes_scale * drift * sine,
    ]
    table = jnp.stack([jnp.broadcast_to(column, shape) for column in columns], axis=-1)
    table = table.reshape(2, -1, len(columns))
    table = jnp.pad(table, ((0, 0), (0, pad_half), (0, 16 - len(columns))))
    return table.reshape(-1, 16)


def shape_of(*dims, kind=F32):
    return jax.ShapeDtypeStruct(dims, kind)


def call(kernel, inputs, outputs, scratch=(), flops=0, moved=0):
    return pl.pallas_call(
        kernel,
        in_specs=inputs,
        out_specs=[WHOLE] * len(outputs),
        out_shape=outputs,
        scratch_shapes=list(scratch),
        compiler_params=pltpu.CompilerParams(vmem_limit_bytes=48 * 1024 * 1024),
        cost_estimate=pl.CostEstimate(flops=flops, bytes_accessed=moved, transcendentals=0),
    )


def local(spec_deck, wind_deck, cell_sea, atm_order, ocean_order):
    owners = lax.axis_size("pts")
    spec_groups = lax.axis_size("spec")
    cpl_groups = lax.axis_size("cpl")
    my_pts = lax.axis_index("pts")
    my_spec = lax.axis_index("spec")
    my_cpl = lax.axis_index("cpl")
    freq_local, dirs_local, slots = spec_deck.shape
    freq_count = freq_local * spec_groups
    dir_count = dirs_local * cpl_groups
    blocks = slots // LANES
    half_rows = freq_local * dirs_local // 2
    pad_half = -half_rows % 8
    rows = 2 * (half_rows + pad_half)

    field = jnp.transpose(spec_deck, (1, 0, 2)).reshape(2, half_rows, slots)
    if pad_half:
        field = jnp.pad(field, ((0, 0), (0, pad_half), (0, 0)))
    field = field.reshape(rows, slots)

    flat = owners * cpl_groups
    ring = []
    for owner in range(owners):
        ring.append((owner * 2, (owner + 1) % owners * 2))
        ring.append((owner * 2 + 1, (owner - 1) % owners * 2 + 1))
    assert flat == len(ring)
    beside = lax.ppermute(field, ("pts", "cpl"), ring)

    first_way = 2 * my_cpl - 1
    turn = jnp.where(
        (my_cpl == 0) & (my_pts == 0), -1, jnp.where((my_cpl == 1) & (my_pts == owners - 1), 1, 0)
    )
    par = jnp.stack([my_pts, first_way, -first_way, turn, my_cpl]).astype(I32)
    coef = coefficients(
        freq_local, dirs_local, pad_half, my_spec, my_cpl, freq_count, dir_count
    )

    found = call(
        functools.partial(index_kernel, owners),
        [SCALARS, WHOLE, WHOLE],
        [shape_of(8, slots, kind=I32)] + [shape_of(rows, LANES)] * (owners - 1),
        flops=6 * rows * slots * LANES * owners,
        moved=rows * slots * 4,
    )(par, cell_sea, field)
    idx, lists = found[0], found[1:]
    arrived = [
        lax.ppermute(values, "pts", [(i, (i + 1 + away) % owners) for i in range(owners)])
        for away, values in enumerate(lists)
    ]
    excess = lax.pmax(jnp.max(idx[5]), ("grp", "pts"))

    propagated, slope_part = call(
        functools.partial(advance_kernel, owners),
        [SCALARS] + [WHOLE] * (owners + 3),
        [shape_of(rows, slots), shape_of(1, slots)],
        [pltpu.VMEM((8, slots), F32)],
        flops=rows * slots * 20,
        moved=rows * slots * 12,
    )(par, coef, idx, field, beside, *arrived)

    peers = spec_groups * cpl_groups
    slope = slope_part
    if spec_groups == 2:
        for turned in range(1, peers):
            slope = slope + lax.ppermute(
                slope_part, ("spec", "cpl"), [(i, i ^ turned) for i in range(peers)]
            )
    else:
        slope = lax.psum(slope_part, ("spec", "cpl"))

    updated, sums = call(
        source_kernel,
        [WHOLE] * 4,
        [shape_of(rows, slots), shape_of(4, blocks, LANES)],
        [pltpu.VMEM((4, 8, slots), F32)],
        flops=rows * slots * 40,
        moved=rows * slots * 8,
    )(coef, wind_deck, slope, propagated)

    mine = jnp.take(sums.reshape(2, 2, blocks, LANES), my_cpl, axis=1)
    others = jnp.take(sums.reshape(2, 2, blocks, LANES), 1 - my_cpl, axis=1)
    mine = mine + lax.ppermute(others, "cpl", [(0, 1), (1, 0)])
    if spec_groups == 2:
        mine = mine + lax.ppermute(mine, "spec", [(0, 1), (1, 0)])
    else:
        mine = lax.psum(mine, "spec")
    if owners == 4:
        around = [mine] + [
            lax.ppermute(mine, "pts", [(i, i ^ turned) for i in range(owners)])
            for turned in range(1, owners)
        ]
        table = jnp.stack(around, axis=1)
        looked = lambda order: order ^ my_pts
    else:
        table = lax.all_gather(mine, "pts", axis=1)
        looked = lambda order: order
    table = table.reshape(2, owners * blocks, LANES)
    count = atm_order.shape[0]
    stress_atm, stokes_ocn = call(
        functools.partial(pick_kernel, owners),
        [WHOLE] * 3,
        [shape_of(1, count)] * 2,
        flops=owners * blocks * LANES * count * 12,
        moved=owners * blocks * LANES * 8,
    )(table, looked(atm_order)[None, :], looked(ocean_order)[None, :])

    updated = updated.reshape(2, half_rows + pad_half, slots)[:, :half_rows]
    updated = jnp.transpose(updated.reshape(dirs_local, freq_local, slots), (1, 0, 2))
    return lax.cond(
        excess > 0,
        lambda: general(spec_deck, wind_deck, cell_sea, atm_order, ocean_order),
        lambda: (updated, stress_atm, stokes_ocn),
    )


def solution(mesh):
    return jax.shard_map(
        local,
        mesh=mesh,
        in_specs=(
            P("spec", "cpl", ("grp", "pts")),
            P(None, ("grp", "pts")),
            P("grp", None),
            P(("grp", "pts", "spec")),
            P(("grp", "pts", "spec")),
        ),
        out_specs=(
            P("spec", "cpl", ("grp", "pts")),
            P("cpl", ("grp", "pts", "spec")),
            P("cpl", ("grp", "pts", "spec")),
        ),
        check_vma=False,
    )
```

```python
import functools
import math

import jax
import jax.numpy as jnp
from jax import lax
from jax.experimental import pallas as pl
from jax.experimental.pallas import tpu as pltpu
from jax.sharding import PartitionSpec as P

COURANT_MAX = 0.68
BASE_FREQ = 0.035
GRAVITY = 9.81
GROWTH_RATE = 0.02
SLOPE_REF = 0.09
STRESS_GAIN = 64.0
STOKES_GAIN = 64.0
LANES = 128
F32 = jnp.float32
BF16 = jnp.bfloat16
I32 = jnp.int32
WHOLE = pl.BlockSpec(memory_space=pltpu.VMEM)
SCALARS = pl.BlockSpec(memory_space=pltpu.SMEM)


def passed_along(shard, axis, by):
    devices = lax.axis_size(axis)
    pairs = [(i, i + by) for i in range(devices) if 0 <= i + by < devices]
    return lax.ppermute(shard, axis, pairs)


def upwind(extended, mask_rows, courant_east, courant_north):
    middle = extended[:, :, 1:-1]
    prior_row = extended[:, :, :-2]
    next_row = extended[:, :, 2:]
    side_pad = jnp.pad(middle, ((0, 0), (0, 0), (0, 0), (1, 1)))
    prior_col = side_pad[..., :-2]
    next_col = side_pad[..., 2:]
    advanced = (
        middle
        - jnp.maximum(courant_east, 0.0) * (middle - prior_row)
        - jnp.maximum(-courant_east, 0.0) * (middle - next_row)
        - jnp.maximum(courant_north, 0.0) * (middle - prior_col)
        - jnp.maximum(-courant_north, 0.0) * (middle - next_col)
    )
    return advanced * mask_rows


def general(spec_deck, wind_deck, cell_sea, atm_order, ocean_order):
    owners = lax.axis_size("pts")
    spec_groups = lax.axis_size("spec")
    cpl_groups = lax.axis_size("cpl")
    my_pts = lax.axis_index("pts")
    my_spec = lax.axis_index("spec")
    my_cpl = lax.axis_index("cpl")
    freq_local, dirs_local, slots_local = spec_deck.shape
    grid_rows, grid_cols = cell_sea.shape
    freq_count = freq_local * spec_groups
    dir_count = dirs_local * cpl_groups
    sea_mask = cell_sea >= 0
    row_counts = jnp.sum(sea_mask.astype(jnp.int32), axis=1)
    before_row = jnp.concatenate([jnp.zeros((1,), jnp.int32), jnp.cumsum(row_counts)])
    tile_freq = my_spec * freq_local + jnp.arange(freq_local)
    height = 2 * (grid_rows // owners)
    capacity = (slots_local + grid_cols) // owners + 1
    targets = jnp.arange(owners + 1, dtype=jnp.int32) * slots_local
    row_starts = jnp.sum((before_row[None, :] < targets[:, None]).astype(jnp.int32), axis=1)
    width_cells = height * grid_cols
    bounds = jnp.take(before_row, row_starts)
    starts = bounds[:-1]
    my_row = jnp.take(row_starts, my_pts)
    my_height = jnp.take(row_starts, my_pts + 1) - my_row
    first_slot = -((jnp.arange(owners, dtype=jnp.int32)[None, :] - starts[:, None]) // owners)
    slot_range = jnp.arange(capacity, dtype=jnp.int32)
    own_first = jnp.take(first_slot, my_pts, axis=1)
    picked = jnp.clip(own_first[:, None] + slot_range[None, :], 0, slots_local - 1).reshape(-1)
    outgoing = jnp.take(spec_deck, picked, axis=2)
    arrived = lax.all_to_all(outgoing, "pts", split_axis=2, concat_axis=2, tiled=True)
    freq_here = arrived.shape[0]
    padded_map = jnp.concatenate([cell_sea, jnp.full((height, grid_cols), -1, jnp.int32)], axis=0)
    strip_map = lax.dynamic_slice_in_dim(padded_map, my_row, height, 0)
    row_valid = jnp.arange(height) < my_height
    strip_sea = ((strip_map >= 0) & row_valid[:, None]).reshape(-1)
    strip_map = strip_map.reshape(-1)
    safe_index = jnp.maximum(strip_map, 0)
    source = safe_index % owners
    strip_first = jnp.take(first_slot, my_pts, axis=0)
    where_from = jnp.where(
        strip_sea, source * capacity + safe_index // owners - jnp.take(strip_first, source), 0
    )
    wave_field = jnp.take(arrived, where_from, axis=2) * strip_sea.astype(jnp.float32)
    wave_field = wave_field.reshape(freq_here, dirs_local, height, grid_cols)
    freq_index = tile_freq.astype(jnp.float32)
    dir_index = (my_cpl * dirs_local + jnp.arange(dirs_local)).astype(jnp.float32)
    angles = 2.0 * math.pi * (dir_index + 0.5) / dir_count
    dir_cosine = jnp.cos(angles)
    dir_sine = jnp.sin(angles)
    speeds = COURANT_MAX * jnp.power(1.1, -freq_index)
    courant_east = (speeds[:, None] * dir_cosine[None, :])[:, :, None, None]
    courant_north = (speeds[:, None] * dir_sine[None, :])[:, :, None, None]
    strip_mask = strip_sea.astype(jnp.float32).reshape(height, grid_cols)
    last_row = lax.dynamic_slice_in_dim(wave_field, my_height - 1, 1, 2)
    from_above = passed_along(last_row, "pts", 1)
    from_below = passed_along(wave_field[:, :, :1], "pts", -1)
    extended = jnp.concatenate([from_above, wave_field, jnp.zeros_like(from_below)], axis=2)
    extended = lax.dynamic_update_slice_in_dim(extended, from_below, my_height + 1, 2)
    wave_field = upwind(extended, strip_mask, courant_east, courant_north)
    flat_field = wave_field.reshape(freq_here, dirs_local, width_cells)
    strip_start = jnp.take(starts, my_pts)
    inverse = (
        jnp.zeros((width_cells,), jnp.int32)
        .at[jnp.where(strip_sea, strip_map - strip_start, width_cells)]
        .set(jnp.arange(width_cells, dtype=jnp.int32), mode="drop")
    )
    wanted = (strip_first[:, None] + slot_range[None, :]) * owners + jnp.arange(
        owners, dtype=jnp.int32
    )[:, None]
    cells_out = jnp.take(inverse, jnp.clip(wanted - strip_start, 0, width_cells - 1).reshape(-1))
    leaving = jnp.take(flat_field, cells_out, axis=2)
    returned = lax.all_to_all(leaving, "pts", split_axis=2, concat_axis=2, tiled=True)
    slot_index = jnp.arange(slots_local, dtype=jnp.int32)
    points = slot_index * owners + my_pts
    strip_of = jnp.sum((starts[None, 1:] <= points[:, None]).astype(jnp.int32), axis=1)
    offset = slot_index - jnp.take(own_first, strip_of)
    position = strip_of * capacity + offset
    propagated = jnp.take(returned, position, axis=2)
    band_freq = (my_spec * freq_local + jnp.arange(freq_local)).astype(jnp.float32)
    sigma_freq = 2.0 * math.pi * BASE_FREQ * jnp.power(1.1, band_freq)
    phase_speed = GRAVITY / sigma_freq
    slope_weight = jnp.power(1.1, 0.4 * band_freq)
    slope_part = jnp.sum(propagated * slope_weight[:, None, None], axis=(0, 1))
    slope_total = lax.psum(slope_part, ("spec", "cpl")) / (SLOPE_REF * freq_count * dir_count)
    wind_along = (
        wind_deck[0][None, None, :] * dir_cosine[None, :, None]
        + wind_deck[1][None, None, :] * dir_sine[None, :, None]
    )
    growth = (
        GROWTH_RATE
        * sigma_freq[:, None, None]
        * jnp.maximum(wind_along / phase_speed[:, None, None] - 1.0, 0.0)
    )
    sigma_top = 2.0 * math.pi * BASE_FREQ * 1.1 ** (freq_count - 1)
    damping = (sigma_freq / sigma_top)[:, None, None] * (slope_total * slope_total)[None, None, :]
    updated = propagated * jnp.exp(growth - damping)
    lifted = growth * propagated
    drift_part = updated * jnp.power(1.1, 2.0 * (band_freq - (freq_count - 1)))[:, None, None]
    stress_scale = STRESS_GAIN / freq_count
    stokes_scale = STOKES_GAIN / math.sqrt(freq_count * dir_count)
    coupled_part = jnp.stack(
        [
            stress_scale * jnp.sum(lifted * dir_cosine[None, :, None], axis=(0, 1)),
            stress_scale * jnp.sum(lifted * dir_sine[None, :, None], axis=(0, 1)),
            stokes_scale * jnp.sum(drift_part * dir_cosine[None, :, None], axis=(0, 1)),
            stokes_scale * jnp.sum(drift_part * dir_sine[None, :, None], axis=(0, 1)),
        ]
    )
    coupled_total = lax.psum(coupled_part, ("spec", "cpl"))
    coupled_all = lax.all_gather(coupled_total, "pts", axis=1, tiled=True)
    atm_col = atm_order % owners * slots_local + atm_order // owners
    ocean_col = ocean_order % owners * slots_local + ocean_order // owners
    stress_atm = jnp.take(lax.dynamic_slice_in_dim(coupled_all, my_cpl, 1, 0), atm_col, axis=1)
    stokes_ocn = jnp.take(
        lax.dynamic_slice_in_dim(coupled_all, 2 + my_cpl, 1, 0), ocean_col, axis=1
    )
    return (updated, stress_atm, stokes_ocn)


C_KEEP, C_ROW, C_COL, C_SLOPE, C_EAST, C_NORTH, C_ONE, C_DAMP = range(8)
C_S_EAST, C_S_NORTH, C_T_EAST, C_T_NORTH = range(8, 12)
CHUNK_ENDS = (5, 10, 15)


def split3(value):
    high = value.astype(BF16)
    rest = value - high.astype(F32)
    middle = rest.astype(BF16)
    low = (rest - middle.astype(F32)).astype(BF16)
    return high, middle, low


def times_exact(value, one_hot, dims):
    parts = [
        lax.dot_general(part, one_hot, (dims, ((), ())), preferred_element_type=F32)
        for part in split3(value)
    ]
    return parts[0] + parts[1] + parts[2]


def index_kernel(owners, par_ref, cell_ref, coef_ref, g_ref, idx_ref, count_ref, sum_ref, *list_refs):
    slots = g_ref.shape[1]
    blocks = slots // LANES
    half_rows = g_ref.shape[0] // 2
    shift = owners.bit_length() - 1
    pts = par_ref[0]
    number = cell_ref[...].astype(F32)
    sea = number >= 0.0
    first = jnp.min(jnp.where(sea, number, 1e9), axis=1, keepdims=True)
    last = jnp.max(jnp.where(sea, number, -1.0), axis=1, keepdims=True)
    rank = jnp.where(sea, number - first + 1.0, 0.0)
    edge = jnp.full((1, number.shape[1]), -1.0, F32)
    above = jnp.concatenate([edge, number[:-1]], axis=0)
    below = jnp.concatenate([number[1:], edge], axis=0)
    to_above = jnp.where(sea & (above >= 0.0), number - above, 0.0)
    to_below = jnp.where(sea & (below >= 0.0), below - number, 0.0)
    ids = cell_ref[...] & (owners - 1)
    above_ids = above.astype(I32) & (owners - 1)
    crossing = (to_above > 0.0) & (ids != above_ids)
    pair = jnp.where(crossing, above_ids * owners + ids, -1)

    @pl.loop(0, owners * owners)
    def _(which):
        count_ref[pl.ds(which, 1), :] = jnp.sum(
            jnp.where(pair == which, 1.0, 0.0), axis=0, keepdims=True
        )

    cols = number.shape[1]
    column = lax.broadcasted_iota(I32, number.shape, 1)
    left = jnp.where(column == 0, -1.0, pltpu.roll(number, 1, 1))
    right = jnp.where(column == cols - 1, -1.0, pltpu.roll(number, cols - 1, 1))
    beside = jnp.where(par_ref[4] == 0, left, right)
    beside = jnp.where(sea & (beside >= 0.0), 1.0, 0.0)

    slot = lax.broadcasted_iota(I32, (1, slots), 1)
    point = slot * owners + pts
    pointf = point.astype(F32)
    in_row = (first <= pointf) & (pointf <= last)
    row_hot = jnp.where(in_row, 1.0, 0.0).astype(BF16)
    row_first = jnp.sum(jnp.where(in_row, first, 0.0), axis=0, keepdims=True)

    def of_row(values):
        return jnp.dot(
            jnp.transpose(values).astype(BF16), row_hot, preferred_element_type=F32
        )

    here = of_row(rank) == (pointf - row_first + 1.0)

    def of_point(values):
        return jnp.sum(jnp.where(here, of_row(values), 0.0), axis=0, keepdims=True)

    step_above = of_point(to_above).astype(I32)
    step_below = of_point(to_below).astype(I32)
    has_beside = of_point(beside).astype(I32)

    groups = max(8, owners)
    group = lax.broadcasted_iota(I32, (groups, slots), 0)
    codes, masks = [], []
    for half in range(2):
        up = par_ref[1 + half] < 0
        for sends in range(2):
            minus = up if sends == 0 else jnp.logical_not(up)
            step = jnp.where(minus, step_above, step_below)
            other = jnp.where(minus, point - step_above, point + step_below)
            owner = other & (owners - 1)
            away = (pts - owner) if sends == 0 else (owner - pts)
            away = jnp.where(step > 0, away & (owners - 1), -1)
            codes.append((away, other >> shift))
            masks.append(jnp.where(group == away, 1.0, 0.0))
    mask = jnp.concatenate(masks, axis=0)
    before = jnp.where(
        lax.broadcasted_iota(I32, (LANES, LANES), 0) < lax.broadcasted_iota(I32, (LANES, LANES), 1),
        1.0,
        0.0,
    ).astype(BF16)
    carry = jnp.zeros((mask.shape[0], 1), F32)
    counts = []
    for block in range(blocks):
        part = mask[:, block * LANES : (block + 1) * LANES]
        inside = jnp.dot(part.astype(BF16), before, preferred_element_type=F32)
        counts.append((inside + carry) * part)
        carry = carry + jnp.sum(part, axis=1, keepdims=True)
    counts = jnp.concatenate(counts, axis=1)
    sum_ref[...] = jnp.zeros_like(sum_ref)
    for half in range(2):
        rows = slice(half * half_rows, (half + 1) * half_rows)
        weight = coef_ref[rows, C_SLOPE : C_SLOPE + 1]
        weighted = g_ref[rows, :] * weight
        for at, column_of in ((0, C_KEEP), (1 + half, C_ROW), (3, C_COL)):
            sum_ref[at : at + 1, :] += jnp.sum(
                weighted * coef_ref[rows, column_of : column_of + 1], axis=0, keepdims=True
            )
    entry = lax.broadcasted_iota(I32, ((owners - 1) * LANES, slots), 0)
    for half in range(2):
        places = [
            jnp.sum(
                counts[(2 * half + sends) * groups : (2 * half + sends + 1) * groups],
                axis=0,
                keepdims=True,
            ).astype(I32)
            for sends in range(2)
        ]
        away, other_slot = codes[2 * half]
        place = places[0]
        same_block = (other_slot >> 7) == (slot >> 7)
        code = jnp.where(away == 0, jnp.where(same_block, 1, 2), away + 2)
        code = jnp.where(away < 0, 0, code)
        lane = jnp.where(away == 0, other_slot & (LANES - 1), jnp.minimum(place, LANES - 1))
        lane = jnp.where(away < 0, 0, lane)
        idx_ref[2 * half] = jnp.broadcast_to(lane, (8, slots))
        idx_ref[2 * half + 1] = jnp.broadcast_to(code, (8, slots))
        away, _ = codes[2 * half + 1]
        place = places[1]
        key = jnp.where((away > 0) & (place < LANES), (away - 1) * LANES + place, -1)
        one_hot = jnp.where(entry == key, 1.0, 0.0).astype(BF16)
        rows = slice(half * half_rows, (half + 1) * half_rows)
        packed = times_exact(g_ref[rows, :], one_hot, ((1,), (1,)))
        sums = times_exact(sum_ref[...], one_hot, ((1,), (1,)))
        for at, list_ref in enumerate(list_refs):
            lanes = slice(at * LANES, (at + 1) * LANES)
            list_ref[rows, :] = packed[:, lanes]
            row = 2 * half_rows + half
            list_ref[row : row + 1, :] = sums[1 + half : 2 + half, lanes]
    for list_ref in list_refs:
        list_ref[2 * half_rows + 2 :, :] = jnp.zeros((6, LANES), F32)
    idx_ref[4] = jnp.broadcast_to(has_beside, (8, slots))


def lane_take(values, lanes):
    return jnp.take_along_axis(values, lanes, axis=1)


def row_neighbour(shape, code, lanes, own, near, lists):
    value = jnp.where(code == 1, lane_take(own, lanes), 0.0)
    value = jnp.where(code == 2, lane_take(near, lanes), value)
    for number, values in enumerate(lists):
        value = jnp.where(code == 3 + number, lane_take(values, lanes), value)
    return value


def near_block(ref, rows, block, step):
    which = jnp.clip(block + step, 0, ref.shape[1] // LANES - 1)
    return ref[rows, pl.ds(pl.multiple_of(which * LANES, LANES), LANES)]


def turned_lanes(turn):
    lane = lax.broadcasted_iota(I32, (8, LANES), 1)
    lanes = (lane + turn) & (LANES - 1)
    return lanes, (lane + turn) != lanes


def slope_kernel(par_ref, idx_ref, sum_ref, beside_ref, *refs):
    list_refs, slope_ref = refs[:-1], refs[-1]
    shape = (8, LANES)
    turn = par_ref[3]
    beside_lanes, beyond = turned_lanes(turn)
    every = slice(0, 8)
    lists = [ref[...] for ref in list_refs]
    for block in range(sum_ref.shape[1] // LANES):
        at = slice(block * LANES, (block + 1) * LANES)
        own = sum_ref[:, at]
        slope = own[0:1]
        for half in range(2):
            lanes, code = idx_ref[2 * half, :, at], idx_ref[2 * half + 1, :, at]
            near = near_block(sum_ref, every, block, par_ref[1 + half])
            here = jnp.where(code == 1, lane_take(own, lanes), 0.0)
            here = jnp.where(code == 2, lane_take(near, lanes), here)
            slope = slope + here[1 + half : 2 + half]
            there = jnp.zeros(shape, F32)
            for number, values in enumerate(lists):
                there = jnp.where(code == 3 + number, lane_take(values, lanes), there)
            slope = slope + there[half : half + 1]
        column = jnp.where(
            beyond,
            lane_take(jnp.broadcast_to(near_block(beside_ref, slice(0, 1), block, turn), shape), beside_lanes),
            lane_take(jnp.broadcast_to(beside_ref[:, at], shape), beside_lanes),
        )
        slope_ref[:, at] = slope + jnp.where(idx_ref[4, 0:1, at] > 0, column[0:1], 0.0)


def step_kernel(owners, first_step, half_steps, chained, final, par_ref, idx_ref, wind_ref, slope_ref, coef_ref, g_ref, beside_ref, *refs):
    list_refs, refs = refs[: owners - 1], refs[owners - 1 :]
    if chained:
        _, before_ref, refs = refs[0], refs[1], refs[2:]
    out_ref, sums_refs, total_ref, damp_ref = refs[0], refs[1:-2], refs[-2], refs[-1]
    blocks = g_ref.shape[1] // LANES
    shape = (8, LANES)
    half = jnp.where(pl.program_id(0) + first_step >= half_steps, 1, 0)
    way, turn = par_ref[1 + half], par_ref[3]
    beside_lanes, beyond = turned_lanes(turn)

    @pl.when(pl.program_id(0) == 0)
    def _():
        total_ref[...] = jnp.zeros_like(total_ref)
        slope = slope_ref[...]
        damp_ref[...] = jnp.broadcast_to(slope * slope, damp_ref.shape)

    for tile in range(g_ref.shape[0] // 8):
        rows = slice(tile * 8, tile * 8 + 8)
        coef = coef_ref[rows, :]

        def factor(at):
            return jnp.broadcast_to(coef[:, at : at + 1], shape)

        keep, by_row, by_col = factor(C_KEEP), factor(C_ROW), factor(C_COL)
        east, north, one, damp = factor(C_EAST), factor(C_NORTH), factor(C_ONE), factor(C_DAMP)
        s_east, s_north = factor(C_S_EAST), factor(C_S_NORTH)
        t_east, t_north = factor(C_T_EAST), factor(C_T_NORTH)
        lists = [ref[rows, :] for ref in list_refs]
        for block in range(blocks):
            at = slice(block * LANES, (block + 1) * LANES)
            lanes, code = idx_ref[2 * half, :, at], idx_ref[2 * half + 1, :, at]
            has_beside = idx_ref[4, :, at]
            own = g_ref[rows, at]
            near = near_block(g_ref, rows, block, way)
            row_value = row_neighbour(shape, code, lanes, own, near, lists)
            col_value = jnp.where(
                beyond,
                lane_take(near_block(beside_ref, rows, block, turn), beside_lanes),
                lane_take(beside_ref[rows, at], beside_lanes),
            )
            col_value = jnp.where(has_beside > 0, col_value, 0.0)
            value = keep * own + by_row * row_value + by_col * col_value
            wind_east = jnp.broadcast_to(wind_ref[0:1, at], shape)
            wind_north = jnp.broadcast_to(wind_ref[1:2, at], shape)
            growth = jnp.maximum(east * wind_east + north * wind_north - one, 0.0)
            updated = value * jnp.exp(growth - damp * damp_ref[:, at])
            out_ref[rows, at] = updated
            lifted = growth * value
            total_ref[0, :, at] += s_east * lifted
            total_ref[1, :, at] += s_north * lifted
            total_ref[2, :, at] += t_east * updated
            total_ref[3, :, at] += t_north * updated

    @pl.when(pl.program_id(0) == pl.num_programs(0) - 1)
    def _():
        cpl = par_ref[4]
        for item in range(2):
            for block in range(blocks):
                at = slice(block * LANES, (block + 1) * LANES)
                pair = []
                for part in range(2):
                    value = jnp.sum(total_ref[2 * item + part, :, at], axis=0, keepdims=True)
                    if chained:
                        value = value + before_ref[2 * item + part, block : block + 1, :]
                    pair.append(value)
                where = slice(block, block + 1)
                if final:
                    sums_refs[0][item, where, :] = jnp.where(cpl == 0, pair[0], pair[1])
                    sums_refs[1][item, where, :] = jnp.where(cpl == 0, pair[1], pair[0])
                else:
                    sums_refs[0][2 * item, where, :] = pair[0]
                    sums_refs[0][2 * item + 1, where, :] = pair[1]


def pick_kernel(owners, atm_ref, ocean_ref, *refs):
    table_refs, (stress_ref, stokes_ref) = refs[:owners], refs[owners:]
    shift = owners.bit_length() - 1
    blocks = table_refs[0].shape[1]
    for item, (order_ref, out_ref) in enumerate(((atm_ref, stress_ref), (ocean_ref, stokes_ref))):
        point = order_ref[...]
        count = point.shape[1]
        slot = point >> shift
        row = (point & (owners - 1)) * blocks + (slot >> 7)
        lane = slot & (LANES - 1)
        rows = owners * blocks
        hot = jnp.where(lax.broadcasted_iota(I32, (rows, count), 0) == row, 1.0, 0.0).astype(BF16)
        table = jnp.concatenate([ref[item] for ref in table_refs], axis=0)
        table = jnp.transpose(table)
        found = times_exact(table, hot, ((1,), (0,)))
        pick = lax.broadcasted_iota(I32, (LANES, count), 0) == lane
        out_ref[...] = jnp.sum(jnp.where(pick, found, 0.0), axis=0, keepdims=True)


def coefficients(freq_local, dirs_local, pad_half, my_spec, my_cpl, freq_count, dir_count):
    freq = (my_spec * freq_local + jnp.arange(freq_local)).astype(F32)
    direction = (my_cpl * dirs_local + jnp.arange(dirs_local)).astype(F32)
    angles = 2.0 * math.pi * (direction + 0.5) / dir_count
    cosine, sine = jnp.cos(angles)[:, None], jnp.sin(angles)[:, None]
    speed = COURANT_MAX * jnp.power(1.1, -freq)[None, :]
    by_row, by_col = jnp.abs(speed * cosine), jnp.abs(speed * sine)
    sigma = (2.0 * math.pi * BASE_FREQ * jnp.power(1.1, freq))[None, :]
    sigma_top = 2.0 * math.pi * BASE_FREQ * 1.1 ** (freq_count - 1)
    inverse_speed = sigma / GRAVITY
    rate = GROWTH_RATE * sigma
    drift = jnp.power(1.1, 2.0 * (freq - (freq_count - 1)))[None, :]
    stress_scale = STRESS_GAIN / freq_count
    stokes_scale = STOKES_GAIN / math.sqrt(freq_count * dir_count)
    shape = (dirs_local, freq_local)
    columns = [
        1.0 - by_row - by_col,
        by_row,
        by_col,
        jnp.power(1.1, 0.4 * freq)[None, :] / (SLOPE_REF * freq_count * dir_count),
        rate * inverse_speed * cosine,
        rate * inverse_speed * sine,
        rate,
        sigma / sigma_top,
        stress_scale * cosine,
        stress_scale * sine,
        stokes_scale * drift * cosine,
        stokes_scale * drift * sine,
    ]
    table = jnp.stack([jnp.broadcast_to(column, shape) for column in columns], axis=-1)
    table = table.reshape(2, -1, len(columns))
    table = jnp.pad(table, ((0, 0), (0, pad_half), (0, 16 - len(columns))))
    return table.reshape(-1, 16)


def shape_of(*dims, kind=F32):
    return jax.ShapeDtypeStruct(dims, kind)


def call(kernel, inputs, outputs, scratch=(), flops=0, moved=0):
    return pl.pallas_call(
        kernel,
        in_specs=inputs,
        out_specs=[WHOLE] * len(outputs),
        out_shape=outputs,
        scratch_shapes=list(scratch),
        compiler_params=pltpu.CompilerParams(vmem_limit_bytes=48 * 1024 * 1024),
        cost_estimate=pl.CostEstimate(flops=flops, bytes_accessed=moved, transcendentals=0),
    )


def chunks_of(steps):
    ends = sorted({max(1, steps * part // 18) for part in CHUNK_ENDS} | {steps})
    return list(zip([0] + ends[:-1], ends))


def local(spec_deck, wind_deck, cell_sea, atm_order, ocean_order):
    owners = lax.axis_size("pts")
    spec_groups = lax.axis_size("spec")
    cpl_groups = lax.axis_size("cpl")
    groups = lax.axis_size("grp")
    my_pts = lax.axis_index("pts")
    my_spec = lax.axis_index("spec")
    my_cpl = lax.axis_index("cpl")
    assert cpl_groups == 2 and owners & (owners - 1) == 0
    freq_local, dirs_local, slots = spec_deck.shape
    freq_count = freq_local * spec_groups
    dir_count = dirs_local * cpl_groups
    blocks = slots // LANES
    half_rows = freq_local * dirs_local // 2
    pad_half = -half_rows % 8
    rows = 2 * (half_rows + pad_half)
    step_rows = 16 if (half_rows + pad_half) % 16 == 0 else 8
    steps = rows // step_rows

    field = jnp.transpose(spec_deck, (1, 0, 2)).reshape(2, half_rows, slots)
    if pad_half:
        field = jnp.pad(field, ((0, 0), (0, pad_half), (0, 0)))
    field = field.reshape(rows, slots)

    ring = []
    for owner in range(owners):
        ring.append((owner * 2, (owner + 1) % owners * 2))
        ring.append((owner * 2 + 1, (owner - 1) % owners * 2 + 1))

    def around(values):
        return lax.ppermute(values, ("pts", "cpl"), ring)

    def chunk(values, at):
        return values[at[0] * step_rows : at[1] * step_rows]

    chunks = chunks_of(steps)
    beside = [around(chunk(field, chunks[0]))]

    first_way = 2 * my_cpl - 1
    turn = jnp.where(
        (my_cpl == 0) & (my_pts == 0), -1, jnp.where((my_cpl == 1) & (my_pts == owners - 1), 1, 0)
    )
    par = jnp.stack([my_pts, first_way, -first_way, turn, my_cpl]).astype(I32)
    coef = coefficients(
        freq_local, dirs_local, pad_half, my_spec, my_cpl, freq_count, dir_count
    )

    found = call(
        functools.partial(index_kernel, owners),
        [SCALARS, WHOLE, WHOLE, WHOLE],
        [
            shape_of(5, 8, slots, kind=I32),
            shape_of(owners * owners, cell_sea.shape[1]),
            shape_of(8, slots),
        ]
        + [shape_of(rows + 8, LANES)] * (owners - 1),
        flops=6 * rows * slots * LANES * owners,
        moved=rows * slots * 4,
    )(par, cell_sea, coef, field)
    (idx, counts, row_sums), lists = found[:3], found[3:]
    arrived = [
        lax.ppermute(values, "pts", [(i, (i + 1 + away) % owners) for i in range(owners)])
        for away, values in enumerate(lists)
    ]
    beside_sums = around(row_sums[3:4])
    later, *_ = lax.optimization_barrier((field, *lists))
    beside += [around(chunk(later, at)) for at in chunks[1:]]

    longest = jnp.max(jnp.sum(counts, axis=1)).reshape(1, 1)
    if groups == 2:
        longest = jnp.maximum(longest, lax.ppermute(longest, "grp", [(0, 1), (1, 0)]))
    else:
        longest = lax.pmax(longest, "grp")

    tail_block = pl.BlockSpec((8, LANES), lambda i: (rows // 8, 0))
    whole = lambda *dims: pl.BlockSpec(dims, lambda i: (0,) * len(dims))
    slope_part = pl.pallas_call(
        slope_kernel,
        grid=(1,),
        in_specs=[SCALARS, whole(5, 8, slots), whole(8, slots), whole(1, slots)]
        + [tail_block] * (owners - 1),
        out_specs=whole(1, slots),
        out_shape=shape_of(1, slots),
    )(par, idx, row_sums, beside_sums, *arrived)

    peers = spec_groups * cpl_groups
    slope = slope_part
    if spec_groups == 2:
        for turned in range(1, peers):
            slope = slope + lax.ppermute(
                slope_part, ("spec", "cpl"), [(i, i ^ turned) for i in range(peers)]
            )
    else:
        slope = lax.psum(slope_part, ("spec", "cpl"))

    updated = sums = None
    for at, near in zip(chunks, beside):
        start, stop = at
        chained, final = start > 0, stop == steps
        in_rows = lambda width: pl.BlockSpec(
            (step_rows, width), functools.partial(lambda first, i: (first + i, 0), start)
        )
        inputs = [par, idx, wind_deck, slope, coef, field, near, *arrived]
        specs = [SCALARS, whole(5, 8, slots), whole(2, slots), whole(1, slots), in_rows(16)]
        specs += [in_rows(slots), pl.BlockSpec((step_rows, slots), lambda i: (i, 0))]
        specs += [in_rows(LANES)] * (owners - 1)
        aliases = {}
        if chained:
            aliases = {len(inputs): 0}
            inputs += [updated, sums]
            specs += [pl.BlockSpec(memory_space=pl.ANY), whole(4, blocks, LANES)]
        sum_shapes = [(2, blocks, LANES)] * 2 if final else [(4, blocks, LANES)]
        updated, *sums = pl.pallas_call(
            functools.partial(step_kernel, owners, start, steps // 2, chained, final),
            grid=(stop - start,),
            in_specs=specs,
            out_specs=[in_rows(slots)] + [whole(*dims) for dims in sum_shapes],
            out_shape=[shape_of(rows, slots)] + [shape_of(*dims) for dims in sum_shapes],
            scratch_shapes=[pltpu.VMEM((4, 8, slots), F32), pltpu.VMEM((8, slots), F32)],
            input_output_aliases=aliases,
            compiler_params=pltpu.CompilerParams(vmem_limit_bytes=24 * 1024 * 1024),
            cost_estimate=pl.CostEstimate(
                flops=(stop - start) * step_rows * slots * 50,
                bytes_accessed=(stop - start) * step_rows * slots * 12,
                transcendentals=(stop - start) * step_rows * slots,
            ),
        )(*inputs)
        if not final:
            sums = sums[0]

    mine, others = sums
    mine = mine + lax.ppermute(others, "cpl", [(0, 1), (1, 0)])
    if spec_groups == 2:
        mine = mine + lax.ppermute(mine, "spec", [(0, 1), (1, 0)])
    else:
        mine = lax.psum(mine, "spec")
    if owners == 4:
        tables = [mine] + [
            lax.ppermute(mine, "pts", [(i, i ^ turned) for i in range(owners)])
            for turned in range(1, owners)
        ]
        looked = lambda order: (order ^ my_pts)[None, :]
    else:
        gathered = lax.all_gather(mine, "pts", axis=0)
        tables = [gathered[owner] for owner in range(owners)]
        looked = lambda order: order[None, :]
    count = atm_order.shape[0]
    stress_atm, stokes_ocn = call(
        functools.partial(pick_kernel, owners),
        [WHOLE] * (2 + owners),
        [shape_of(1, count)] * 2,
        flops=owners * blocks * LANES * count * 12,
        moved=owners * blocks * LANES * 8,
    )(looked(atm_order), looked(ocean_order), *tables)

    def by_direction(values):
        return jnp.transpose(values, (1, 0, 2)).reshape(dirs_local * freq_local, slots)

    def general_way():
        spectra, stress, stokes = general(spec_deck, wind_deck, cell_sea, atm_order, ocean_order)
        return by_direction(spectra), stress, stokes

    if pad_half:
        updated = updated.reshape(2, half_rows + pad_half, slots)[:, :half_rows]
        updated = updated.reshape(2 * half_rows, slots)
    updated, stress_atm, stokes_ocn = lax.cond(
        longest[0, 0] > LANES, general_way, lambda: (updated, stress_atm, stokes_ocn)
    )
    updated = jnp.transpose(updated.reshape(dirs_local, freq_local, slots), (1, 0, 2))
    return updated, stress_atm, stokes_ocn


def solution(mesh):
    return jax.shard_map(
        local,
        mesh=mesh,
        in_specs=(
            P("spec", "cpl", ("grp", "pts")),
            P(None, ("grp", "pts")),
            P("grp", None),
            P(("grp", "pts", "spec")),
            P(("grp", "pts", "spec")),
        ),
        out_specs=(
            P("spec", "cpl", ("grp", "pts")),
            P("cpl", ("grp", "pts", "spec")),
            P("cpl", ("grp", "pts", "spec")),
        ),
        check_vma=False,
    )
```

```python
import functools
import math

import jax
import jax.numpy as jnp
from jax import lax
from jax.experimental import pallas as pl
from jax.experimental.pallas import tpu as pltpu
from jax.sharding import PartitionSpec as P

COURANT_MAX = 0.68
BASE_FREQ = 0.035
GRAVITY = 9.81
GROWTH_RATE = 0.02
SLOPE_REF = 0.09
STRESS_GAIN = 64.0
STOKES_GAIN = 64.0
LANES = 128
F32 = jnp.float32
BF16 = jnp.bfloat16
I32 = jnp.int32
WHOLE = pl.BlockSpec(memory_space=pltpu.VMEM)
SCALARS = pl.BlockSpec(memory_space=pltpu.SMEM)


def passed_along(shard, axis, by):
    devices = lax.axis_size(axis)
    pairs = [(i, i + by) for i in range(devices) if 0 <= i + by < devices]
    return lax.ppermute(shard, axis, pairs)


def upwind(extended, mask_rows, courant_east, courant_north):
    middle = extended[:, :, 1:-1]
    prior_row = extended[:, :, :-2]
    next_row = extended[:, :, 2:]
    side_pad = jnp.pad(middle, ((0, 0), (0, 0), (0, 0), (1, 1)))
    prior_col = side_pad[..., :-2]
    next_col = side_pad[..., 2:]
    advanced = (
        middle
        - jnp.maximum(courant_east, 0.0) * (middle - prior_row)
        - jnp.maximum(-courant_east, 0.0) * (middle - next_row)
        - jnp.maximum(courant_north, 0.0) * (middle - prior_col)
        - jnp.maximum(-courant_north, 0.0) * (middle - next_col)
    )
    return advanced * mask_rows


def general(spec_deck, wind_deck, cell_sea, atm_order, ocean_order):
    owners = lax.axis_size("pts")
    spec_groups = lax.axis_size("spec")
    cpl_groups = lax.axis_size("cpl")
    my_pts = lax.axis_index("pts")
    my_spec = lax.axis_index("spec")
    my_cpl = lax.axis_index("cpl")
    freq_local, dirs_local, slots_local = spec_deck.shape
    grid_rows, grid_cols = cell_sea.shape
    freq_count = freq_local * spec_groups
    dir_count = dirs_local * cpl_groups
    sea_mask = cell_sea >= 0
    row_counts = jnp.sum(sea_mask.astype(jnp.int32), axis=1)
    before_row = jnp.concatenate([jnp.zeros((1,), jnp.int32), jnp.cumsum(row_counts)])
    tile_freq = my_spec * freq_local + jnp.arange(freq_local)
    height = 2 * (grid_rows // owners)
    capacity = (slots_local + grid_cols) // owners + 1
    targets = jnp.arange(owners + 1, dtype=jnp.int32) * slots_local
    row_starts = jnp.sum((before_row[None, :] < targets[:, None]).astype(jnp.int32), axis=1)
    width_cells = height * grid_cols
    bounds = jnp.take(before_row, row_starts)
    starts = bounds[:-1]
    my_row = jnp.take(row_starts, my_pts)
    my_height = jnp.take(row_starts, my_pts + 1) - my_row
    first_slot = -((jnp.arange(owners, dtype=jnp.int32)[None, :] - starts[:, None]) // owners)
    slot_range = jnp.arange(capacity, dtype=jnp.int32)
    own_first = jnp.take(first_slot, my_pts, axis=1)
    picked = jnp.clip(own_first[:, None] + slot_range[None, :], 0, slots_local - 1).reshape(-1)
    outgoing = jnp.take(spec_deck, picked, axis=2)
    arrived = lax.all_to_all(outgoing, "pts", split_axis=2, concat_axis=2, tiled=True)
    freq_here = arrived.shape[0]
    padded_map = jnp.concatenate([cell_sea, jnp.full((height, grid_cols), -1, jnp.int32)], axis=0)
    strip_map = lax.dynamic_slice_in_dim(padded_map, my_row, height, 0)
    row_valid = jnp.arange(height) < my_height
    strip_sea = ((strip_map >= 0) & row_valid[:, None]).reshape(-1)
    strip_map = strip_map.reshape(-1)
    safe_index = jnp.maximum(strip_map, 0)
    source = safe_index % owners
    strip_first = jnp.take(first_slot, my_pts, axis=0)
    where_from = jnp.where(
        strip_sea, source * capacity + safe_index // owners - jnp.take(strip_first, source), 0
    )
    wave_field = jnp.take(arrived, where_from, axis=2) * strip_sea.astype(jnp.float32)
    wave_field = wave_field.reshape(freq_here, dirs_local, height, grid_cols)
    freq_index = tile_freq.astype(jnp.float32)
    dir_index = (my_cpl * dirs_local + jnp.arange(dirs_local)).astype(jnp.float32)
    angles = 2.0 * math.pi * (dir_index + 0.5) / dir_count
    dir_cosine = jnp.cos(angles)
    dir_sine = jnp.sin(angles)
    speeds = COURANT_MAX * jnp.power(1.1, -freq_index)
    courant_east = (speeds[:, None] * dir_cosine[None, :])[:, :, None, None]
    courant_north = (speeds[:, None] * dir_sine[None, :])[:, :, None, None]
    strip_mask = strip_sea.astype(jnp.float32).reshape(height, grid_cols)
    last_row = lax.dynamic_slice_in_dim(wave_field, my_height - 1, 1, 2)
    from_above = passed_along(last_row, "pts", 1)
    from_below = passed_along(wave_field[:, :, :1], "pts", -1)
    extended = jnp.concatenate([from_above, wave_field, jnp.zeros_like(from_below)], axis=2)
    extended = lax.dynamic_update_slice_in_dim(extended, from_below, my_height + 1, 2)
    wave_field = upwind(extended, strip_mask, courant_east, courant_north)
    flat_field = wave_field.reshape(freq_here, dirs_local, width_cells)
    strip_start = jnp.take(starts, my_pts)
    inverse = (
        jnp.zeros((width_cells,), jnp.int32)
        .at[jnp.where(strip_sea, strip_map - strip_start, width_cells)]
        .set(jnp.arange(width_cells, dtype=jnp.int32), mode="drop")
    )
    wanted = (strip_first[:, None] + slot_range[None, :]) * owners + jnp.arange(
        owners, dtype=jnp.int32
    )[:, None]
    cells_out = jnp.take(inverse, jnp.clip(wanted - strip_start, 0, width_cells - 1).reshape(-1))
    leaving = jnp.take(flat_field, cells_out, axis=2)
    returned = lax.all_to_all(leaving, "pts", split_axis=2, concat_axis=2, tiled=True)
    slot_index = jnp.arange(slots_local, dtype=jnp.int32)
    points = slot_index * owners + my_pts
    strip_of = jnp.sum((starts[None, 1:] <= points[:, None]).astype(jnp.int32), axis=1)
    offset = slot_index - jnp.take(own_first, strip_of)
    position = strip_of * capacity + offset
    propagated = jnp.take(returned, position, axis=2)
    band_freq = (my_spec * freq_local + jnp.arange(freq_local)).astype(jnp.float32)
    sigma_freq = 2.0 * math.pi * BASE_FREQ * jnp.power(1.1, band_freq)
    phase_speed = GRAVITY / sigma_freq
    slope_weight = jnp.power(1.1, 0.4 * band_freq)
    slope_part = jnp.sum(propagated * slope_weight[:, None, None], axis=(0, 1))
    slope_total = lax.psum(slope_part, ("spec", "cpl")) / (SLOPE_REF * freq_count * dir_count)
    wind_along = (
        wind_deck[0][None, None, :] * dir_cosine[None, :, None]
        + wind_deck[1][None, None, :] * dir_sine[None, :, None]
    )
    growth = (
        GROWTH_RATE
        * sigma_freq[:, None, None]
        * jnp.maximum(wind_along / phase_speed[:, None, None] - 1.0, 0.0)
    )
    sigma_top = 2.0 * math.pi * BASE_FREQ * 1.1 ** (freq_count - 1)
    damping = (sigma_freq / sigma_top)[:, None, None] * (slope_total * slope_total)[None, None, :]
    updated = propagated * jnp.exp(growth - damping)
    lifted = growth * propagated
    drift_part = updated * jnp.power(1.1, 2.0 * (band_freq - (freq_count - 1)))[:, None, None]
    stress_scale = STRESS_GAIN / freq_count
    stokes_scale = STOKES_GAIN / math.sqrt(freq_count * dir_count)
    coupled_part = jnp.stack(
        [
            stress_scale * jnp.sum(lifted * dir_cosine[None, :, None], axis=(0, 1)),
            stress_scale * jnp.sum(lifted * dir_sine[None, :, None], axis=(0, 1)),
            stokes_scale * jnp.sum(drift_part * dir_cosine[None, :, None], axis=(0, 1)),
            stokes_scale * jnp.sum(drift_part * dir_sine[None, :, None], axis=(0, 1)),
        ]
    )
    coupled_total = lax.psum(coupled_part, ("spec", "cpl"))
    coupled_all = lax.all_gather(coupled_total, "pts", axis=1, tiled=True)
    atm_col = atm_order % owners * slots_local + atm_order // owners
    ocean_col = ocean_order % owners * slots_local + ocean_order // owners
    stress_atm = jnp.take(lax.dynamic_slice_in_dim(coupled_all, my_cpl, 1, 0), atm_col, axis=1)
    stokes_ocn = jnp.take(
        lax.dynamic_slice_in_dim(coupled_all, 2 + my_cpl, 1, 0), ocean_col, axis=1
    )
    return (updated, stress_atm, stokes_ocn)


C_KEEP, C_ROW, C_COL, C_SLOPE, C_EAST, C_NORTH, C_ONE, C_DAMP = range(8)
C_S_EAST, C_S_NORTH, C_T_EAST, C_T_NORTH = range(8, 12)
CHUNK_ENDS = (4, 8, 13, 16)
VMEM_BYTES = 40 * 1024 * 1024


def split3(value):
    high = value.astype(BF16)
    rest = value - high.astype(F32)
    middle = rest.astype(BF16)
    low = (rest - middle.astype(F32)).astype(BF16)
    return high, middle, low


def times_exact(value, one_hot, dims):
    parts = [
        lax.dot_general(part, one_hot, (dims, ((), ())), preferred_element_type=F32)
        for part in split3(value)
    ]
    return parts[0] + parts[1] + parts[2]


def index_kernel(owners, par_ref, cell_ref, coef_ref, g_ref, idx_ref, count_ref, sum_ref, *list_refs):
    slots = g_ref.shape[1]
    blocks = slots // LANES
    half_rows = g_ref.shape[0] // 2
    shift = owners.bit_length() - 1
    pts = par_ref[0]
    number = cell_ref[...].astype(F32)
    sea = number >= 0.0
    first = jnp.min(jnp.where(sea, number, 1e9), axis=1, keepdims=True)
    last = jnp.max(jnp.where(sea, number, -1.0), axis=1, keepdims=True)
    rank = jnp.where(sea, number - first + 1.0, 0.0)
    edge = jnp.full((1, number.shape[1]), -1.0, F32)
    above = jnp.concatenate([edge, number[:-1]], axis=0)
    below = jnp.concatenate([number[1:], edge], axis=0)
    to_above = jnp.where(sea & (above >= 0.0), number - above, 0.0)
    to_below = jnp.where(sea & (below >= 0.0), below - number, 0.0)
    ids = cell_ref[...] & (owners - 1)
    above_ids = above.astype(I32) & (owners - 1)
    crossing = (to_above > 0.0) & (ids != above_ids)
    pair = jnp.where(crossing, above_ids * owners + ids, -1)

    @pl.loop(0, owners * owners)
    def _(which):
        count_ref[pl.ds(which, 1), :] = jnp.sum(
            jnp.where(pair == which, 1.0, 0.0), axis=0, keepdims=True
        )

    cols = number.shape[1]
    column = lax.broadcasted_iota(I32, number.shape, 1)
    left = jnp.where(column == 0, -1.0, pltpu.roll(number, 1, 1))
    right = jnp.where(column == cols - 1, -1.0, pltpu.roll(number, cols - 1, 1))
    beside = jnp.where(par_ref[4] == 0, left, right)
    beside = jnp.where(sea & (beside >= 0.0), 1.0, 0.0)

    slot = lax.broadcasted_iota(I32, (1, slots), 1)
    point = slot * owners + pts
    pointf = point.astype(F32)
    in_row = (first <= pointf) & (pointf <= last)
    row_hot = jnp.where(in_row, 1.0, 0.0).astype(BF16)
    row_first = jnp.sum(jnp.where(in_row, first, 0.0), axis=0, keepdims=True)

    def of_row(values):
        return jnp.dot(
            jnp.transpose(values).astype(BF16), row_hot, preferred_element_type=F32
        )

    here = of_row(rank) == (pointf - row_first + 1.0)

    def of_point(values):
        return jnp.sum(jnp.where(here, of_row(values), 0.0), axis=0, keepdims=True)

    step_above = of_point(to_above).astype(I32)
    step_below = of_point(to_below).astype(I32)
    has_beside = of_point(beside).astype(I32)

    groups = max(8, owners)
    group = lax.broadcasted_iota(I32, (groups, slots), 0)
    codes, masks = [], []
    for half in range(2):
        up = par_ref[1 + half] < 0
        for sends in range(2):
            minus = up if sends == 0 else jnp.logical_not(up)
            step = jnp.where(minus, step_above, step_below)
            other = jnp.where(minus, point - step_above, point + step_below)
            owner = other & (owners - 1)
            away = (pts - owner) if sends == 0 else (owner - pts)
            away = jnp.where(step > 0, away & (owners - 1), -1)
            codes.append((away, other >> shift))
            masks.append(jnp.where(group == away, 1.0, 0.0))
    mask = jnp.concatenate(masks, axis=0)
    before = jnp.where(
        lax.broadcasted_iota(I32, (LANES, LANES), 0) < lax.broadcasted_iota(I32, (LANES, LANES), 1),
        1.0,
        0.0,
    ).astype(BF16)
    carry = jnp.zeros((mask.shape[0], 1), F32)
    counts = []
    for block in range(blocks):
        part = mask[:, block * LANES : (block + 1) * LANES]
        inside = jnp.dot(part.astype(BF16), before, preferred_element_type=F32)
        counts.append((inside + carry) * part)
        carry = carry + jnp.sum(part, axis=1, keepdims=True)
    counts = jnp.concatenate(counts, axis=1)
    sum_ref[...] = jnp.zeros_like(sum_ref)
    for half in range(2):
        rows = slice(half * half_rows, (half + 1) * half_rows)
        weight = coef_ref[rows, C_SLOPE : C_SLOPE + 1]
        weighted = g_ref[rows, :] * weight
        for at, column_of in ((0, C_KEEP), (1 + half, C_ROW), (3, C_COL)):
            sum_ref[at : at + 1, :] += jnp.sum(
                weighted * coef_ref[rows, column_of : column_of + 1], axis=0, keepdims=True
            )
    entry = lax.broadcasted_iota(I32, ((owners - 1) * LANES, slots), 0)
    for half in range(2):
        places = [
            jnp.sum(
                counts[(2 * half + sends) * groups : (2 * half + sends + 1) * groups],
                axis=0,
                keepdims=True,
            ).astype(I32)
            for sends in range(2)
        ]
        away, other_slot = codes[2 * half]
        place = places[0]
        same_block = (other_slot >> 7) == (slot >> 7)
        code = jnp.where(away == 0, jnp.where(same_block, 1, 2), away + 2)
        code = jnp.where(away < 0, 0, code)
        lane = jnp.where(away == 0, other_slot & (LANES - 1), jnp.minimum(place, LANES - 1))
        lane = jnp.where(away < 0, 0, lane)
        idx_ref[2 * half] = jnp.broadcast_to(lane, (8, slots))
        idx_ref[2 * half + 1] = jnp.broadcast_to(code, (8, slots))
        away, _ = codes[2 * half + 1]
        place = places[1]
        key = jnp.where((away > 0) & (place < LANES), (away - 1) * LANES + place, -1)
        one_hot = jnp.where(entry == key, 1.0, 0.0).astype(BF16)
        rows = slice(half * half_rows, (half + 1) * half_rows)
        packed = times_exact(g_ref[rows, :], one_hot, ((1,), (1,)))
        sums = times_exact(sum_ref[...], one_hot, ((1,), (1,)))
        for at, list_ref in enumerate(list_refs):
            lanes = slice(at * LANES, (at + 1) * LANES)
            list_ref[rows, :] = packed[:, lanes]
            row = 2 * half_rows + half
            list_ref[row : row + 1, :] = sums[1 + half : 2 + half, lanes]
    for list_ref in list_refs:
        list_ref[2 * half_rows + 2 :, :] = jnp.zeros((6, LANES), F32)
    idx_ref[4] = jnp.broadcast_to(has_beside, (8, slots))


def lane_take(values, lanes):
    return jnp.take_along_axis(values, lanes, axis=1)


def row_neighbour(shape, code, lanes, own, near, lists):
    value = jnp.where(code == 1, lane_take(own, lanes), 0.0)
    value = jnp.where(code == 2, lane_take(near, lanes), value)
    for number, values in enumerate(lists):
        value = jnp.where(code == 3 + number, lane_take(values, lanes), value)
    return value


def near_block(ref, rows, block, step):
    which = jnp.clip(block + step, 0, ref.shape[1] // LANES - 1)
    return ref[rows, pl.ds(pl.multiple_of(which * LANES, LANES), LANES)]


def turned_lanes(turn):
    lane = lax.broadcasted_iota(I32, (8, LANES), 1)
    lanes = (lane + turn) & (LANES - 1)
    return lanes, (lane + turn) != lanes


def slope_kernel(par_ref, idx_ref, sum_ref, beside_ref, *refs):
    list_refs, slope_ref = refs[:-1], refs[-1]
    shape = (8, LANES)
    turn = par_ref[3]
    beside_lanes, beyond = turned_lanes(turn)
    every = slice(0, 8)
    lists = [ref[-8:, :] for ref in list_refs]
    for block in range(sum_ref.shape[1] // LANES):
        at = slice(block * LANES, (block + 1) * LANES)
        own = sum_ref[:, at]
        slope = own[0:1]
        for half in range(2):
            lanes, code = idx_ref[2 * half, :, at], idx_ref[2 * half + 1, :, at]
            near = near_block(sum_ref, every, block, par_ref[1 + half])
            here = jnp.where(code == 1, lane_take(own, lanes), 0.0)
            here = jnp.where(code == 2, lane_take(near, lanes), here)
            slope = slope + here[1 + half : 2 + half]
            there = jnp.zeros(shape, F32)
            for number, values in enumerate(lists):
                there = jnp.where(code == 3 + number, lane_take(values, lanes), there)
            slope = slope + there[half : half + 1]
        column = jnp.where(
            beyond,
            lane_take(jnp.broadcast_to(near_block(beside_ref, slice(0, 1), block, turn), shape), beside_lanes),
            lane_take(jnp.broadcast_to(beside_ref[:, at], shape), beside_lanes),
        )
        slope_ref[:, at] = slope + jnp.where(idx_ref[4, 0:1, at] > 0, column[0:1], 0.0)


def step_kernel(owners, first_step, half_steps, chained, final, par_ref, idx_ref, wind_ref, slope_ref, coef_ref, g_ref, beside_ref, *refs):
    list_refs, refs = refs[: owners - 1], refs[owners - 1 :]
    if chained:
        _, before_ref, refs = refs[0], refs[1], refs[2:]
    out_ref, sums_refs, total_ref, damp_ref = refs[0], refs[1:-2], refs[-2], refs[-1]
    blocks = g_ref.shape[1] // LANES
    shape = (8, LANES)
    half = jnp.where(pl.program_id(0) + first_step >= half_steps, 1, 0)
    way, turn = par_ref[1 + half], par_ref[3]
    beside_lanes, beyond = turned_lanes(turn)

    @pl.when(pl.program_id(0) == 0)
    def _():
        total_ref[...] = jnp.zeros_like(total_ref)
        slope = slope_ref[...]
        damp_ref[...] = jnp.broadcast_to(slope * slope, damp_ref.shape)

    for tile in range(out_ref.shape[0] // 8):
        here = slice(tile * 8, tile * 8 + 8)
        first = pl.program_id(0) * out_ref.shape[0] + tile * 8
        near_rows = pl.ds(pl.multiple_of(first, 8), 8)
        rows = pl.ds(pl.multiple_of(first + first_step * out_ref.shape[0], 8), 8)
        coef = coef_ref[rows, :]

        def factor(at):
            return jnp.broadcast_to(coef[:, at : at + 1], shape)

        keep, by_row, by_col = factor(C_KEEP), factor(C_ROW), factor(C_COL)
        east, north, one, damp = factor(C_EAST), factor(C_NORTH), factor(C_ONE), factor(C_DAMP)
        s_east, s_north = factor(C_S_EAST), factor(C_S_NORTH)
        t_east, t_north = factor(C_T_EAST), factor(C_T_NORTH)
        lists = [ref[rows, :] for ref in list_refs]
        for block in range(blocks):
            at = slice(block * LANES, (block + 1) * LANES)
            lanes, code = idx_ref[2 * half, :, at], idx_ref[2 * half + 1, :, at]
            has_beside = idx_ref[4, :, at]
            own = g_ref[rows, at]
            near = near_block(g_ref, rows, block, way)
            row_value = row_neighbour(shape, code, lanes, own, near, lists)
            col_value = jnp.where(
                beyond,
                lane_take(near_block(beside_ref, near_rows, block, turn), beside_lanes),
                lane_take(beside_ref[near_rows, at], beside_lanes),
            )
            col_value = jnp.where(has_beside > 0, col_value, 0.0)
            value = keep * own + by_row * row_value + by_col * col_value
            wind_east = jnp.broadcast_to(wind_ref[0:1, at], shape)
            wind_north = jnp.broadcast_to(wind_ref[1:2, at], shape)
            growth = jnp.maximum(east * wind_east + north * wind_north - one, 0.0)
            updated = value * jnp.exp(growth - damp * damp_ref[:, at])
            out_ref[here, at] = updated
            lifted = growth * value
            total_ref[0, :, at] += s_east * lifted
            total_ref[1, :, at] += s_north * lifted
            total_ref[2, :, at] += t_east * updated
            total_ref[3, :, at] += t_north * updated

    @pl.when(pl.program_id(0) == pl.num_programs(0) - 1)
    def _():
        cpl = par_ref[4]
        for item in range(2):
            for block in range(blocks):
                at = slice(block * LANES, (block + 1) * LANES)
                pair = []
                for part in range(2):
                    value = jnp.sum(total_ref[2 * item + part, :, at], axis=0, keepdims=True)
                    if chained:
                        value = value + before_ref[2 * item + part, block : block + 1, :]
                    pair.append(value)
                where = slice(block, block + 1)
                if final:
                    sums_refs[0][item, where, :] = jnp.where(cpl == 0, pair[0], pair[1])
                    sums_refs[1][item, where, :] = jnp.where(cpl == 0, pair[1], pair[0])
                else:
                    sums_refs[0][2 * item, where, :] = pair[0]
                    sums_refs[0][2 * item + 1, where, :] = pair[1]


def pick_kernel(owners, atm_ref, ocean_ref, *refs):
    table_refs, (stress_ref, stokes_ref) = refs[:owners], refs[owners:]
    shift = owners.bit_length() - 1
    blocks = table_refs[0].shape[1]
    for item, (order_ref, out_ref) in enumerate(((atm_ref, stress_ref), (ocean_ref, stokes_ref))):
        point = order_ref[...]
        count = point.shape[1]
        slot = point >> shift
        row = (point & (owners - 1)) * blocks + (slot >> 7)
        lane = slot & (LANES - 1)
        rows = owners * blocks
        hot = jnp.where(lax.broadcasted_iota(I32, (rows, count), 0) == row, 1.0, 0.0).astype(BF16)
        table = jnp.concatenate([ref[item] for ref in table_refs], axis=0)
        table = jnp.transpose(table)
        found = times_exact(table, hot, ((1,), (0,)))
        pick = lax.broadcasted_iota(I32, (LANES, count), 0) == lane
        out_ref[...] = jnp.sum(jnp.where(pick, found, 0.0), axis=0, keepdims=True)


def coefficients(freq_local, dirs_local, pad_half, my_spec, my_cpl, freq_count, dir_count):
    freq = (my_spec * freq_local + jnp.arange(freq_local)).astype(F32)
    direction = (my_cpl * dirs_local + jnp.arange(dirs_local)).astype(F32)
    angles = 2.0 * math.pi * (direction + 0.5) / dir_count
    cosine, sine = jnp.cos(angles)[:, None], jnp.sin(angles)[:, None]
    speed = COURANT_MAX * jnp.power(1.1, -freq)[None, :]
    by_row, by_col = jnp.abs(speed * cosine), jnp.abs(speed * sine)
    sigma = (2.0 * math.pi * BASE_FREQ * jnp.power(1.1, freq))[None, :]
    sigma_top = 2.0 * math.pi * BASE_FREQ * 1.1 ** (freq_count - 1)
    inverse_speed = sigma / GRAVITY
    rate = GROWTH_RATE * sigma
    drift = jnp.power(1.1, 2.0 * (freq - (freq_count - 1)))[None, :]
    stress_scale = STRESS_GAIN / freq_count
    stokes_scale = STOKES_GAIN / math.sqrt(freq_count * dir_count)
    shape = (dirs_local, freq_local)
    columns = [
        1.0 - by_row - by_col,
        by_row,
        by_col,
        jnp.power(1.1, 0.4 * freq)[None, :] / (SLOPE_REF * freq_count * dir_count),
        rate * inverse_speed * cosine,
        rate * inverse_speed * sine,
        rate,
        sigma / sigma_top,
        stress_scale * cosine,
        stress_scale * sine,
        stokes_scale * drift * cosine,
        stokes_scale * drift * sine,
    ]
    table = jnp.stack([jnp.broadcast_to(column, shape) for column in columns], axis=-1)
    table = table.reshape(2, -1, len(columns))
    table = jnp.pad(table, ((0, 0), (0, pad_half), (0, 16 - len(columns))))
    return table.reshape(-1, 16)


def shape_of(*dims, kind=F32):
    return jax.ShapeDtypeStruct(dims, kind)


def call(kernel, inputs, outputs, scratch=(), flops=0, moved=0):
    return pl.pallas_call(
        kernel,
        in_specs=inputs,
        out_specs=[WHOLE] * len(outputs),
        out_shape=outputs,
        scratch_shapes=list(scratch),
        compiler_params=pltpu.CompilerParams(vmem_limit_bytes=VMEM_BYTES),
        cost_estimate=pl.CostEstimate(flops=flops, bytes_accessed=moved, transcendentals=0),
    )


def chunks_of(steps):
    ends = sorted({max(1, steps * part // 18) for part in CHUNK_ENDS} | {steps})
    return list(zip([0] + ends[:-1], ends))


def local(spec_deck, wind_deck, cell_sea, atm_order, ocean_order):
    owners = lax.axis_size("pts")
    spec_groups = lax.axis_size("spec")
    cpl_groups = lax.axis_size("cpl")
    groups = lax.axis_size("grp")
    my_pts = lax.axis_index("pts")
    my_spec = lax.axis_index("spec")
    my_cpl = lax.axis_index("cpl")
    assert cpl_groups == 2 and owners & (owners - 1) == 0
    freq_local, dirs_local, slots = spec_deck.shape
    freq_count = freq_local * spec_groups
    dir_count = dirs_local * cpl_groups
    blocks = slots // LANES
    half_rows = freq_local * dirs_local // 2
    pad_half = -half_rows % 8
    rows = 2 * (half_rows + pad_half)
    step_rows = 16 if (half_rows + pad_half) % 16 == 0 else 8
    steps = rows // step_rows

    field = jnp.transpose(spec_deck, (1, 0, 2)).reshape(2, half_rows, slots)
    if pad_half:
        field = jnp.pad(field, ((0, 0), (0, pad_half), (0, 0)))
    field = field.reshape(rows, slots)

    ring = []
    for owner in range(owners):
        ring.append((owner * 2, (owner + 1) % owners * 2))
        ring.append((owner * 2 + 1, (owner - 1) % owners * 2 + 1))

    def around(values):
        return lax.ppermute(values, ("pts", "cpl"), ring)

    def chunk(values, at):
        return values[at[0] * step_rows : at[1] * step_rows]

    chunks = chunks_of(steps)
    beside = [around(chunk(field, chunks[0]))]

    first_way = 2 * my_cpl - 1
    turn = jnp.where(
        (my_cpl == 0) & (my_pts == 0), -1, jnp.where((my_cpl == 1) & (my_pts == owners - 1), 1, 0)
    )
    par = jnp.stack([my_pts, first_way, -first_way, turn, my_cpl]).astype(I32)
    coef = coefficients(
        freq_local, dirs_local, pad_half, my_spec, my_cpl, freq_count, dir_count
    )

    found = call(
        functools.partial(index_kernel, owners),
        [SCALARS, WHOLE, WHOLE, WHOLE],
        [
            shape_of(5, 8, slots, kind=I32),
            shape_of(owners * owners, cell_sea.shape[1]),
            shape_of(8, slots),
        ]
        + [shape_of(rows + 8, LANES)] * (owners - 1),
        flops=6 * rows * slots * LANES * owners,
        moved=rows * slots * 4,
    )(par, cell_sea, coef, field)
    (idx, counts, row_sums), *lists = lax.optimization_barrier((found[:3], *found[3:], beside[0]))
    beside = [lists.pop()]
    arrived = [
        lax.ppermute(values, "pts", [(i, (i + 1 + away) % owners) for i in range(owners)])
        for away, values in enumerate(lists)
    ]
    beside_sums = around(row_sums[3:4])
    second = chunk(field, chunks[1])
    second, *_ = lax.optimization_barrier((second, *lists))
    beside.append(around(second))
    later = [chunk(field, at) for at in chunks[2:]]
    later, arrived, beside_sums = lax.optimization_barrier((later, arrived, beside_sums))
    beside += [around(values) for values in later]

    longest = jnp.max(jnp.sum(counts, axis=1)).reshape(1, 1)
    if groups == 2:
        longest = jnp.maximum(longest, lax.ppermute(longest, "grp", [(0, 1), (1, 0)]))
    else:
        longest = lax.pmax(longest, "grp")

    slope_part = pl.pallas_call(
        slope_kernel,
        in_specs=[SCALARS, WHOLE, WHOLE, WHOLE] + [WHOLE] * (owners - 1),
        out_specs=WHOLE,
        out_shape=shape_of(1, slots),
    )(par, idx, row_sums, beside_sums, *arrived)

    peers = spec_groups * cpl_groups
    slope = slope_part
    if spec_groups == 2:
        for turned in range(1, peers):
            slope = slope + lax.ppermute(
                slope_part, ("spec", "cpl"), [(i, i ^ turned) for i in range(peers)]
            )
    else:
        slope = lax.psum(slope_part, ("spec", "cpl"))

    slope, longest = lax.optimization_barrier((slope, longest))
    updated = sums = None
    for at, near in zip(chunks, beside):
        start, stop = at
        chained, final = start > 0, stop == steps
        in_rows = lambda width: pl.BlockSpec(
            (step_rows, width), functools.partial(lambda first, i: (first + i, 0), start)
        )
        inputs = [par, idx, wind_deck, slope, coef, field, near, *arrived]
        specs = [SCALARS] + [WHOLE] * (owners + 5)
        aliases = {}
        if chained:
            aliases = {len(inputs): 0}
            inputs += [updated, sums]
            specs += [pl.BlockSpec(memory_space=pl.ANY), WHOLE]
        sum_shapes = [(2, blocks, LANES)] * 2 if final else [(4, blocks, LANES)]
        updated, *sums = pl.pallas_call(
            functools.partial(step_kernel, owners, start, steps // 2, chained, final),
            grid=(stop - start,),
            in_specs=specs,
            out_specs=[in_rows(slots)] + [WHOLE] * len(sum_shapes),
            out_shape=[pltpu.HBM((rows, slots), F32)] + [shape_of(*dims) for dims in sum_shapes],
            scratch_shapes=[pltpu.VMEM((4, 8, slots), F32), pltpu.VMEM((8, slots), F32)],
            input_output_aliases=aliases,
            compiler_params=pltpu.CompilerParams(vmem_limit_bytes=VMEM_BYTES),
            cost_estimate=pl.CostEstimate(
                flops=(stop - start) * step_rows * slots * 50,
                bytes_accessed=(stop - start) * step_rows * slots * 12,
                transcendentals=(stop - start) * step_rows * slots,
            ),
        )(*inputs)
        if not final:
            sums = sums[0]

    mine, others = sums
    mine = mine + lax.ppermute(others, "cpl", [(0, 1), (1, 0)])
    if spec_groups == 2:
        mine = mine + lax.ppermute(mine, "spec", [(0, 1), (1, 0)])
    else:
        mine = lax.psum(mine, "spec")
    if owners == 4:
        tables = [mine] + [
            lax.ppermute(mine, "pts", [(i, i ^ turned) for i in range(owners)])
            for turned in range(1, owners)
        ]
        looked = lambda order: (order ^ my_pts)[None, :]
    else:
        gathered = lax.all_gather(mine, "pts", axis=0)
        tables = [gathered[owner] for owner in range(owners)]
        looked = lambda order: order[None, :]
    count = atm_order.shape[0]
    stress_atm, stokes_ocn = call(
        functools.partial(pick_kernel, owners),
        [WHOLE] * (2 + owners),
        [shape_of(1, count)] * 2,
        flops=owners * blocks * LANES * count * 12,
        moved=owners * blocks * LANES * 8,
    )(looked(atm_order), looked(ocean_order), *tables)

    def by_direction(values):
        return jnp.transpose(values, (1, 0, 2)).reshape(dirs_local * freq_local, slots)

    def general_way():
        spectra, stress, stokes = general(spec_deck, wind_deck, cell_sea, atm_order, ocean_order)
        return by_direction(spectra), stress, stokes

    if pad_half:
        updated = updated.reshape(2, half_rows + pad_half, slots)[:, :half_rows]
        updated = updated.reshape(2 * half_rows, slots)
    updated, stress_atm, stokes_ocn = lax.cond(
        longest[0, 0] > LANES, general_way, lambda: (updated, stress_atm, stokes_ocn)
    )
    updated = jnp.transpose(updated.reshape(dirs_local, freq_local, slots), (1, 0, 2))
    return updated, stress_atm, stokes_ocn


def solution(mesh):
    return jax.shard_map(
        local,
        mesh=mesh,
        in_specs=(
            P("spec", "cpl", ("grp", "pts")),
            P(None, ("grp", "pts")),
            P("grp", None),
            P(("grp", "pts", "spec")),
            P(("grp", "pts", "spec")),
        ),
        out_specs=(
            P("spec", "cpl", ("grp", "pts")),
            P("cpl", ("grp", "pts", "spec")),
            P("cpl", ("grp", "pts", "spec")),
        ),
        check_vma=False,
    )
```

```python
import functools
import math

import jax
import jax.numpy as jnp
from jax import lax
from jax.experimental import pallas as pl
from jax.experimental.pallas import tpu as pltpu
from jax.sharding import PartitionSpec as P

COURANT_MAX = 0.68
BASE_FREQ = 0.035
GRAVITY = 9.81
GROWTH_RATE = 0.02
SLOPE_REF = 0.09
STRESS_GAIN = 64.0
STOKES_GAIN = 64.0
LANES = 128
F32 = jnp.float32
BF16 = jnp.bfloat16
I32 = jnp.int32
WHOLE = pl.BlockSpec(memory_space=pltpu.VMEM)
SHORT = pl.CostEstimate(flops=1000, bytes_accessed=1000, transcendentals=0)
SCALARS = pl.BlockSpec(memory_space=pltpu.SMEM)


def passed_along(shard, axis, by):
    devices = lax.axis_size(axis)
    pairs = [(i, i + by) for i in range(devices) if 0 <= i + by < devices]
    return lax.ppermute(shard, axis, pairs)


def upwind(extended, mask_rows, courant_east, courant_north):
    middle = extended[:, :, 1:-1]
    prior_row = extended[:, :, :-2]
    next_row = extended[:, :, 2:]
    side_pad = jnp.pad(middle, ((0, 0), (0, 0), (0, 0), (1, 1)))
    prior_col = side_pad[..., :-2]
    next_col = side_pad[..., 2:]
    advanced = (
        middle
        - jnp.maximum(courant_east, 0.0) * (middle - prior_row)
        - jnp.maximum(-courant_east, 0.0) * (middle - next_row)
        - jnp.maximum(courant_north, 0.0) * (middle - prior_col)
        - jnp.maximum(-courant_north, 0.0) * (middle - next_col)
    )
    return advanced * mask_rows


def general(spec_deck, wind_deck, cell_sea, atm_order, ocean_order):
    owners = lax.axis_size("pts")
    spec_groups = lax.axis_size("spec")
    cpl_groups = lax.axis_size("cpl")
    my_pts = lax.axis_index("pts")
    my_spec = lax.axis_index("spec")
    my_cpl = lax.axis_index("cpl")
    freq_local, dirs_local, slots_local = spec_deck.shape
    grid_rows, grid_cols = cell_sea.shape
    freq_count = freq_local * spec_groups
    dir_count = dirs_local * cpl_groups
    sea_mask = cell_sea >= 0
    row_counts = jnp.sum(sea_mask.astype(jnp.int32), axis=1)
    before_row = jnp.concatenate([jnp.zeros((1,), jnp.int32), jnp.cumsum(row_counts)])
    tile_freq = my_spec * freq_local + jnp.arange(freq_local)
    height = 2 * (grid_rows // owners)
    capacity = (slots_local + grid_cols) // owners + 1
    targets = jnp.arange(owners + 1, dtype=jnp.int32) * slots_local
    row_starts = jnp.sum((before_row[None, :] < targets[:, None]).astype(jnp.int32), axis=1)
    width_cells = height * grid_cols
    bounds = jnp.take(before_row, row_starts)
    starts = bounds[:-1]
    my_row = jnp.take(row_starts, my_pts)
    my_height = jnp.take(row_starts, my_pts + 1) - my_row
    first_slot = -((jnp.arange(owners, dtype=jnp.int32)[None, :] - starts[:, None]) // owners)
    slot_range = jnp.arange(capacity, dtype=jnp.int32)
    own_first = jnp.take(first_slot, my_pts, axis=1)
    picked = jnp.clip(own_first[:, None] + slot_range[None, :], 0, slots_local - 1).reshape(-1)
    outgoing = jnp.take(spec_deck, picked, axis=2)
    arrived = lax.all_to_all(outgoing, "pts", split_axis=2, concat_axis=2, tiled=True)
    freq_here = arrived.shape[0]
    padded_map = jnp.concatenate([cell_sea, jnp.full((height, grid_cols), -1, jnp.int32)], axis=0)
    strip_map = lax.dynamic_slice_in_dim(padded_map, my_row, height, 0)
    row_valid = jnp.arange(height) < my_height
    strip_sea = ((strip_map >= 0) & row_valid[:, None]).reshape(-1)
    strip_map = strip_map.reshape(-1)
    safe_index = jnp.maximum(strip_map, 0)
    source = safe_index % owners
    strip_first = jnp.take(first_slot, my_pts, axis=0)
    where_from = jnp.where(
        strip_sea, source * capacity + safe_index // owners - jnp.take(strip_first, source), 0
    )
    wave_field = jnp.take(arrived, where_from, axis=2) * strip_sea.astype(jnp.float32)
    wave_field = wave_field.reshape(freq_here, dirs_local, height, grid_cols)
    freq_index = tile_freq.astype(jnp.float32)
    dir_index = (my_cpl * dirs_local + jnp.arange(dirs_local)).astype(jnp.float32)
    angles = 2.0 * math.pi * (dir_index + 0.5) / dir_count
    dir_cosine = jnp.cos(angles)
    dir_sine = jnp.sin(angles)
    speeds = COURANT_MAX * jnp.power(1.1, -freq_index)
    courant_east = (speeds[:, None] * dir_cosine[None, :])[:, :, None, None]
    courant_north = (speeds[:, None] * dir_sine[None, :])[:, :, None, None]
    strip_mask = strip_sea.astype(jnp.float32).reshape(height, grid_cols)
    last_row = lax.dynamic_slice_in_dim(wave_field, my_height - 1, 1, 2)
    from_above = passed_along(last_row, "pts", 1)
    from_below = passed_along(wave_field[:, :, :1], "pts", -1)
    extended = jnp.concatenate([from_above, wave_field, jnp.zeros_like(from_below)], axis=2)
    extended = lax.dynamic_update_slice_in_dim(extended, from_below, my_height + 1, 2)
    wave_field = upwind(extended, strip_mask, courant_east, courant_north)
    flat_field = wave_field.reshape(freq_here, dirs_local, width_cells)
    strip_start = jnp.take(starts, my_pts)
    inverse = (
        jnp.zeros((width_cells,), jnp.int32)
        .at[jnp.where(strip_sea, strip_map - strip_start, width_cells)]
        .set(jnp.arange(width_cells, dtype=jnp.int32), mode="drop")
    )
    wanted = (strip_first[:, None] + slot_range[None, :]) * owners + jnp.arange(
        owners, dtype=jnp.int32
    )[:, None]
    cells_out = jnp.take(inverse, jnp.clip(wanted - strip_start, 0, width_cells - 1).reshape(-1))
    leaving = jnp.take(flat_field, cells_out, axis=2)
    returned = lax.all_to_all(leaving, "pts", split_axis=2, concat_axis=2, tiled=True)
    slot_index = jnp.arange(slots_local, dtype=jnp.int32)
    points = slot_index * owners + my_pts
    strip_of = jnp.sum((starts[None, 1:] <= points[:, None]).astype(jnp.int32), axis=1)
    offset = slot_index - jnp.take(own_first, strip_of)
    position = strip_of * capacity + offset
    propagated = jnp.take(returned, position, axis=2)
    band_freq = (my_spec * freq_local + jnp.arange(freq_local)).astype(jnp.float32)
    sigma_freq = 2.0 * math.pi * BASE_FREQ * jnp.power(1.1, band_freq)
    phase_speed = GRAVITY / sigma_freq
    slope_weight = jnp.power(1.1, 0.4 * band_freq)
    slope_part = jnp.sum(propagated * slope_weight[:, None, None], axis=(0, 1))
    slope_total = lax.psum(slope_part, ("spec", "cpl")) / (SLOPE_REF * freq_count * dir_count)
    wind_along = (
        wind_deck[0][None, None, :] * dir_cosine[None, :, None]
        + wind_deck[1][None, None, :] * dir_sine[None, :, None]
    )
    growth = (
        GROWTH_RATE
        * sigma_freq[:, None, None]
        * jnp.maximum(wind_along / phase_speed[:, None, None] - 1.0, 0.0)
    )
    sigma_top = 2.0 * math.pi * BASE_FREQ * 1.1 ** (freq_count - 1)
    damping = (sigma_freq / sigma_top)[:, None, None] * (slope_total * slope_total)[None, None, :]
    updated = propagated * jnp.exp(growth - damping)
    lifted = growth * propagated
    drift_part = updated * jnp.power(1.1, 2.0 * (band_freq - (freq_count - 1)))[:, None, None]
    stress_scale = STRESS_GAIN / freq_count
    stokes_scale = STOKES_GAIN / math.sqrt(freq_count * dir_count)
    coupled_part = jnp.stack(
        [
            stress_scale * jnp.sum(lifted * dir_cosine[None, :, None], axis=(0, 1)),
            stress_scale * jnp.sum(lifted * dir_sine[None, :, None], axis=(0, 1)),
            stokes_scale * jnp.sum(drift_part * dir_cosine[None, :, None], axis=(0, 1)),
            stokes_scale * jnp.sum(drift_part * dir_sine[None, :, None], axis=(0, 1)),
        ]
    )
    coupled_total = lax.psum(coupled_part, ("spec", "cpl"))
    coupled_all = lax.all_gather(coupled_total, "pts", axis=1, tiled=True)
    atm_col = atm_order % owners * slots_local + atm_order // owners
    ocean_col = ocean_order % owners * slots_local + ocean_order // owners
    stress_atm = jnp.take(lax.dynamic_slice_in_dim(coupled_all, my_cpl, 1, 0), atm_col, axis=1)
    stokes_ocn = jnp.take(
        lax.dynamic_slice_in_dim(coupled_all, 2 + my_cpl, 1, 0), ocean_col, axis=1
    )
    return (updated, stress_atm, stokes_ocn)


C_KEEP, C_ROW, C_COL, C_SLOPE, C_EAST, C_NORTH, C_ONE, C_DAMP = range(8)
C_S_EAST, C_S_NORTH, C_T_EAST, C_T_NORTH = range(8, 12)
CHUNK_ENDS = (3, 6, 7, 12, 16)
VMEM_BYTES = 24 * 1024 * 1024


def times_hot(value, one_hot, dims, parts=3):
    count = value.shape[0]
    pieces = []
    for _ in range(parts):
        pieces.append(value.astype(BF16).astype(F32))
        value = value - pieces[-1]
    stacked = jnp.concatenate(pieces, axis=0).astype(BF16)
    found = lax.dot_general(stacked, one_hot, (dims, ((), ())), preferred_element_type=F32)
    return sum(found[part * count : (part + 1) * count] for part in range(parts))


def index_kernel(owners, starts, par_ref, cell_ref, coef_ref, g_ref, idx_ref, count_ref, sum_ref, *refs):
    list_refs, chunk_refs = refs[: owners - 2], refs[owners - 2 :]
    slots = g_ref.shape[1]
    blocks = slots // LANES
    half_rows = g_ref.shape[0] // 2
    shift = owners.bit_length() - 1
    pts = par_ref[0]
    number = cell_ref[...].astype(F32)
    sea = number >= 0.0
    first = jnp.min(jnp.where(sea, number, 1e9), axis=1, keepdims=True)
    last = jnp.max(jnp.where(sea, number, -1.0), axis=1, keepdims=True)
    rank = jnp.where(sea, number - first + 1.0, 0.0)
    edge = jnp.full((1, number.shape[1]), -1.0, F32)
    above = jnp.concatenate([edge, number[:-1]], axis=0)
    below = jnp.concatenate([number[1:], edge], axis=0)
    to_above = jnp.where(sea & (above >= 0.0), number - above, 0.0)
    to_below = jnp.where(sea & (below >= 0.0), below - number, 0.0)
    ids = cell_ref[...] & (owners - 1)
    above_ids = above.astype(I32) & (owners - 1)
    crossing = (to_above > 0.0) & (ids != above_ids)
    pair = jnp.where(crossing, above_ids * owners + ids, -1)

    @pl.loop(0, owners * owners)
    def _(which):
        count_ref[pl.ds(which, 1), :] = jnp.sum(
            jnp.where(pair == which, 1.0, 0.0), axis=0, keepdims=True
        )

    cols = number.shape[1]
    column = lax.broadcasted_iota(I32, number.shape, 1)
    left = jnp.where(column == 0, -1.0, pltpu.roll(number, 1, 1))
    right = jnp.where(column == cols - 1, -1.0, pltpu.roll(number, cols - 1, 1))
    beside = jnp.where(par_ref[4] == 0, left, right)
    beside = jnp.where(sea & (beside >= 0.0), 1.0, 0.0)

    slot = lax.broadcasted_iota(I32, (1, slots), 1)
    point = slot * owners + pts
    pointf = point.astype(F32)
    in_row = (first <= pointf) & (pointf <= last)
    row_hot = jnp.where(in_row, 1.0, 0.0).astype(BF16)
    row_first = jnp.sum(jnp.where(in_row, first, 0.0), axis=0, keepdims=True)

    def of_row(values):
        return jnp.dot(
            jnp.transpose(values).astype(BF16), row_hot, preferred_element_type=F32
        )

    here = of_row(rank) == (pointf - row_first + 1.0)

    def of_point(values):
        return jnp.sum(jnp.where(here, of_row(values), 0.0), axis=0, keepdims=True)

    step_above = of_point(to_above).astype(I32)
    step_below = of_point(to_below).astype(I32)
    has_beside = of_point(beside).astype(I32)

    groups = max(8, owners)
    group = lax.broadcasted_iota(I32, (groups, slots), 0)
    codes, masks = [], []
    for half in range(2):
        up = par_ref[1 + half] < 0
        for sends in range(2):
            minus = up if sends == 0 else jnp.logical_not(up)
            step = jnp.where(minus, step_above, step_below)
            other = jnp.where(minus, point - step_above, point + step_below)
            owner = other & (owners - 1)
            away = ((pts - owner) if sends == 0 else (owner - pts)) * par_ref[5]
            away = jnp.where(step > 0, away & (owners - 1), -1)
            codes.append((away, other >> shift))
            masks.append(jnp.where(group == away, 1.0, 0.0))
    mask = jnp.concatenate(masks, axis=0)
    before = jnp.where(
        lax.broadcasted_iota(I32, (LANES, LANES), 0) < lax.broadcasted_iota(I32, (LANES, LANES), 1),
        1.0,
        0.0,
    ).astype(BF16)
    carry = jnp.zeros((mask.shape[0], 1), F32)
    counts = []
    for block in range(blocks):
        part = mask[:, block * LANES : (block + 1) * LANES]
        inside = jnp.dot(part.astype(BF16), before, preferred_element_type=F32)
        counts.append((inside + carry) * part)
        carry = carry + jnp.sum(part, axis=1, keepdims=True)
    counts = jnp.concatenate(counts, axis=1)
    sum_ref[...] = jnp.zeros_like(sum_ref)
    for half in range(2):
        rows = slice(half * half_rows, (half + 1) * half_rows)
        weight = coef_ref[rows, C_SLOPE : C_SLOPE + 1]
        weighted = g_ref[rows, :] * weight
        for at, column_of in ((0, C_KEEP), (1 + half, C_ROW), (3, C_COL)):
            sum_ref[at : at + 1, :] += jnp.sum(
                weighted * coef_ref[rows, column_of : column_of + 1], axis=0, keepdims=True
            )
    lanes_all = (owners - 2) * 2 * LANES
    entry = lax.broadcasted_iota(I32, (lanes_all, slots), 0)
    packed, sums = [], []
    for half in range(2):
        receive, send = [
            jnp.sum(
                counts[(2 * half + sends) * groups : (2 * half + sends + 1) * groups],
                axis=0,
                keepdims=True,
            ).astype(I32)
            for sends in range(2)
        ]
        away, other_slot = codes[2 * half]
        spilled = receive >= LANES
        place = jnp.where(spilled, jnp.maximum(2 * LANES - 1 - receive, 0), receive)
        other_block = jnp.where((other_slot >> 7) == (slot >> 7), 0, 1)
        code = jnp.where(away <= 1, 1 + 2 * away + other_block, 1 + 2 * away + jnp.where(spilled, 1, 0))
        lane = jnp.where(away <= 1, other_slot & (LANES - 1), place)
        idx_ref[2 * half] = jnp.broadcast_to(jnp.where(away < 0, 0, lane), (8, slots))
        idx_ref[2 * half + 1] = jnp.broadcast_to(jnp.where(away < 0, 0, code), (8, slots))
        away, _ = codes[2 * half + 1]
        place = jnp.where(send >= LANES, 3 * LANES - 1 - send, send)
        place = jnp.where(send >= 2 * LANES, -1, place)
        key = jnp.where((away > 1) & (place >= 0), (away - 2) * 2 * LANES + place, -1)
        one_hot = jnp.where(entry == key, 1.0, 0.0).astype(BF16)
        rows = slice(half * half_rows, (half + 1) * half_rows)
        packed.append(times_hot(g_ref[rows, :], one_hot, ((1,), (1,)), 2))
        sums.append(times_hot(sum_ref[...], one_hot, ((1,), (1,))))
    for at, list_ref in enumerate(list_refs):
        inner = slice(2 * at * LANES, (2 * at + 1) * LANES)
        outer = slice((2 * at + 1) * LANES, (2 * at + 2) * LANES)
        for half in range(2):
            rows = slice(half * half_rows, (half + 1) * half_rows)
            list_ref[rows, :] = packed[half][:, inner] + packed[1 - half][:, outer]
            row, other = 1 + half, 2 - half
            list_ref[2 * half_rows + half : 2 * half_rows + half + 1, :] = (
                sums[half][row : row + 1, inner] + sums[1 - half][other : other + 1, outer]
            )
    chunk_refs[0][-8:, :] = sum_ref[...]
    for start, chunk_ref in zip(starts, chunk_refs):
        count = chunk_ref.shape[0] - (8 if start == starts[0] else 0)
        chunk_ref[:count, :] = g_ref[start : start + count, :]
    for list_ref in list_refs:
        list_ref[2 * half_rows + 2 :, :] = jnp.zeros((6, LANES), F32)
    idx_ref[4] = jnp.broadcast_to(has_beside, (8, slots))


def lane_take(values, lanes):
    return jnp.take_along_axis(values, lanes, axis=1)


def row_neighbour(code, lanes, sources):
    value = jnp.zeros(code.shape, F32)
    for number, source in enumerate(sources):
        value = jnp.where(code == 1 + number, lane_take(source, lanes), value)
    return value


def near_block(ref, rows, block, step):
    which = jnp.clip(block + step, 0, ref.shape[1] // LANES - 1)
    return ref[rows, pl.ds(pl.multiple_of(which * LANES, LANES), LANES)]


def turned_lanes(turn):
    lane = lax.broadcasted_iota(I32, (8, LANES), 1)
    lanes = (lane + turn) & (LANES - 1)
    return lanes, (lane + turn) != lanes


def slope_kernel(par_ref, idx_ref, sum_ref, beside_ref, *refs):
    list_refs, slope_ref = refs[:-1], refs[-1]
    shape = (8, LANES)
    turn = par_ref[3]
    beside_lanes, beyond = turned_lanes(turn)
    every, last = slice(0, 8), slice(beside_ref.shape[0] - 8, beside_ref.shape[0])
    lists = [ref[-8:, :] for ref in list_refs]
    for block in range(sum_ref.shape[1] // LANES):
        at = slice(block * LANES, (block + 1) * LANES)
        own, beside = sum_ref[:, at], beside_ref[last, at]
        slope = own[0:1]
        for half in range(2):
            lanes, code = idx_ref[2 * half, :, at], idx_ref[2 * half + 1, :, at]
            way = par_ref[1 + half]
            sources = [own, near_block(sum_ref, every, block, way)]
            sources += [beside, near_block(beside_ref, last, block, way)]
            value = row_neighbour(code, lanes, sources)
            slope = slope + value[1 + half : 2 + half]
            code = code - 4
            for values in lists:
                for row in (half, 1 - half):
                    value = jnp.where(code == 1, lane_take(values, lanes), 0.0)
                    slope = slope + value[row : row + 1]
                    code = code - 1
        column = jnp.where(
            beyond,
            lane_take(near_block(beside_ref, last, block, turn), beside_lanes),
            lane_take(beside, beside_lanes),
        )
        slope_ref[:, at] = slope + jnp.where(idx_ref[4, 0:1, at] > 0, column[3:4], 0.0)


def step_kernel(owners, first_step, half_steps, chained, final, par_ref, idx_ref, wind_ref, slope_ref, coef_ref, g_ref, beside_ref, *refs):
    list_refs, refs = refs[: owners - 2], refs[owners - 2 :]
    if chained:
        _, before_ref, refs = refs[0], refs[1], refs[2:]
    out_ref, sums_refs, total_ref, damp_ref = refs[0], refs[1:-2], refs[-2], refs[-1]
    blocks = g_ref.shape[1] // LANES
    shape = (8, LANES)
    half = jnp.where(pl.program_id(0) + first_step >= half_steps, 1, 0)
    way, turn = par_ref[1 + half], par_ref[3]
    beside_lanes, beyond = turned_lanes(turn)

    @pl.when(pl.program_id(0) == 0)
    def _():
        total_ref[...] = jnp.zeros_like(total_ref)
        slope = slope_ref[...]
        damp_ref[...] = jnp.broadcast_to(slope * slope, damp_ref.shape)

    for tile in range(out_ref.shape[0] // 8):
        here = slice(tile * 8, tile * 8 + 8)
        first = pl.program_id(0) * out_ref.shape[0] + tile * 8
        near_rows = pl.ds(pl.multiple_of(first, 8), 8)
        rows = pl.ds(pl.multiple_of(first + first_step * out_ref.shape[0], 8), 8)
        half_rows = half_steps * out_ref.shape[0]
        other_rows = pl.ds(
            pl.multiple_of(first + first_step * out_ref.shape[0] + (1 - 2 * half) * half_rows, 8), 8
        )
        coef = coef_ref[rows, :]

        def factor(at):
            return jnp.broadcast_to(coef[:, at : at + 1], shape)

        keep, by_row, by_col = factor(C_KEEP), factor(C_ROW), factor(C_COL)
        east, north, one, damp = factor(C_EAST), factor(C_NORTH), factor(C_ONE), factor(C_DAMP)
        s_east, s_north = factor(C_S_EAST), factor(C_S_NORTH)
        t_east, t_north = factor(C_T_EAST), factor(C_T_NORTH)
        lists = [ref[which, :] for ref in list_refs for which in (rows, other_rows)]
        for block in range(blocks):
            at = slice(block * LANES, (block + 1) * LANES)
            lanes, code = idx_ref[2 * half, :, at], idx_ref[2 * half + 1, :, at]
            has_beside = idx_ref[4, :, at]
            own, beside = g_ref[here, at], beside_ref[near_rows, at]
            sources = [own, near_block(g_ref, here, block, way)]
            sources += [beside, near_block(beside_ref, near_rows, block, way)]
            row_value = row_neighbour(code, lanes, sources + lists)
            col_value = jnp.where(
                beyond,
                lane_take(near_block(beside_ref, near_rows, block, turn), beside_lanes),
                lane_take(beside, beside_lanes),
            )
            col_value = jnp.where(has_beside > 0, col_value, 0.0)
            value = keep * own + by_row * row_value + by_col * col_value
            wind_east = jnp.broadcast_to(wind_ref[0:1, at], shape)
            wind_north = jnp.broadcast_to(wind_ref[1:2, at], shape)
            growth = jnp.maximum(east * wind_east + north * wind_north - one, 0.0)
            updated = value * jnp.exp(growth - damp * damp_ref[:, at])
            out_ref[here, at] = updated
            lifted = growth * value
            total_ref[0, :, at] += s_east * lifted
            total_ref[1, :, at] += s_north * lifted
            total_ref[2, :, at] += t_east * updated
            total_ref[3, :, at] += t_north * updated

    @pl.when(pl.program_id(0) == pl.num_programs(0) - 1)
    def _():
        cpl = par_ref[4]
        for item in range(2):
            for block in range(blocks):
                at = slice(block * LANES, (block + 1) * LANES)
                pair = []
                for part in range(2):
                    value = jnp.sum(total_ref[2 * item + part, :, at], axis=0, keepdims=True)
                    if chained:
                        value = value + before_ref[2 * item + part, block : block + 1, :]
                    pair.append(value)
                where = slice(block, block + 1)
                if final:
                    sums_refs[0][item, where, :] = jnp.where(cpl == 0, pair[0], pair[1])
                    sums_refs[1][item, where, :] = jnp.where(cpl == 0, pair[1], pair[0])
                else:
                    sums_refs[0][2 * item, where, :] = pair[0]
                    sums_refs[0][2 * item + 1, where, :] = pair[1]


def pick_kernel(owners, atm_ref, ocean_ref, *refs):
    table_refs, (stress_ref, stokes_ref) = refs[:owners], refs[owners:]
    shift = owners.bit_length() - 1
    blocks = table_refs[0].shape[1]
    for item, (order_ref, out_ref) in enumerate(((atm_ref, stress_ref), (ocean_ref, stokes_ref))):
        point = order_ref[...]
        count = point.shape[1]
        slot = point >> shift
        row = (point & (owners - 1)) * blocks + (slot >> 7)
        lane = slot & (LANES - 1)
        rows = owners * blocks
        hot = jnp.where(lax.broadcasted_iota(I32, (rows, count), 0) == row, 1.0, 0.0).astype(BF16)
        table = jnp.concatenate([ref[item] for ref in table_refs], axis=0)
        table = jnp.transpose(table)
        found = times_hot(table, hot, ((1,), (0,)))
        pick = lax.broadcasted_iota(I32, (LANES, count), 0) == lane
        out_ref[...] = jnp.sum(jnp.where(pick, found, 0.0), axis=0, keepdims=True)


def coefficients(freq_local, dirs_local, pad_half, my_spec, my_cpl, freq_count, dir_count):
    freq = (my_spec * freq_local + jnp.arange(freq_local)).astype(F32)
    direction = (my_cpl * dirs_local + jnp.arange(dirs_local)).astype(F32)
    angles = 2.0 * math.pi * (direction + 0.5) / dir_count
    cosine, sine = jnp.cos(angles)[:, None], jnp.sin(angles)[:, None]
    speed = COURANT_MAX * jnp.power(1.1, -freq)[None, :]
    by_row, by_col = jnp.abs(speed * cosine), jnp.abs(speed * sine)
    sigma = (2.0 * math.pi * BASE_FREQ * jnp.power(1.1, freq))[None, :]
    sigma_top = 2.0 * math.pi * BASE_FREQ * 1.1 ** (freq_count - 1)
    inverse_speed = sigma / GRAVITY
    rate = GROWTH_RATE * sigma
    drift = jnp.power(1.1, 2.0 * (freq - (freq_count - 1)))[None, :]
    stress_scale = STRESS_GAIN / freq_count
    stokes_scale = STOKES_GAIN / math.sqrt(freq_count * dir_count)
    shape = (dirs_local, freq_local)
    columns = [
        1.0 - by_row - by_col,
        by_row,
        by_col,
        jnp.power(1.1, 0.4 * freq)[None, :] / (SLOPE_REF * freq_count * dir_count),
        rate * inverse_speed * cosine,
        rate * inverse_speed * sine,
        rate,
        sigma / sigma_top,
        stress_scale * cosine,
        stress_scale * sine,
        stokes_scale * drift * cosine,
        stokes_scale * drift * sine,
    ]
    table = jnp.stack([jnp.broadcast_to(column, shape) for column in columns], axis=-1)
    table = table.reshape(2, -1, len(columns))
    table = jnp.pad(table, ((0, 0), (0, pad_half), (0, 16 - len(columns))))
    return table.reshape(-1, 16)


def shape_of(*dims, kind=F32):
    return jax.ShapeDtypeStruct(dims, kind)


def call(kernel, inputs, outputs):
    return pl.pallas_call(
        kernel,
        in_specs=inputs,
        out_specs=[WHOLE] * len(outputs),
        out_shape=outputs,
        compiler_params=pltpu.CompilerParams(vmem_limit_bytes=VMEM_BYTES),
        cost_estimate=SHORT,
    )


def chunks_of(steps):
    ends = sorted({max(1, steps * part // 18) for part in CHUNK_ENDS} | {steps})
    return list(zip([0] + ends[:-1], ends))


def local(spec_deck, wind_deck, cell_sea, atm_order, ocean_order):
    owners = lax.axis_size("pts")
    spec_groups = lax.axis_size("spec")
    cpl_groups = lax.axis_size("cpl")
    groups = lax.axis_size("grp")
    my_pts = lax.axis_index("pts")
    my_spec = lax.axis_index("spec")
    my_cpl = lax.axis_index("cpl")
    assert cpl_groups == 2 and owners & (owners - 1) == 0
    freq_local, dirs_local, slots = spec_deck.shape
    freq_count = freq_local * spec_groups
    dir_count = dirs_local * cpl_groups
    blocks = slots // LANES
    half_rows = freq_local * dirs_local // 2
    pad_half = -half_rows % 8
    rows = 2 * (half_rows + pad_half)
    step_rows = 16 if (half_rows + pad_half) % 16 == 0 else 8
    steps = rows // step_rows

    field = jnp.transpose(spec_deck, (1, 0, 2)).reshape(2, half_rows, slots)
    if pad_half:
        field = jnp.pad(field, ((0, 0), (0, pad_half), (0, 0)))
    field = field.reshape(rows, slots)

    def around(values, distance=1):
        pairs = []
        for owner in range(owners):
            pairs.append((owner * 2, (owner + distance) % owners * 2))
            pairs.append((owner * 2 + 1, (owner - distance) % owners * 2 + 1))
        return lax.ppermute(values, ("pts", "cpl"), pairs)

    def chunk(values, at):
        return values[at[0] * step_rows : at[1] * step_rows]

    chunks = chunks_of(steps)
    beside = [around(chunk(field, at)) for at in chunks[:2]]

    first_way = 2 * my_cpl - 1
    turn = jnp.where(
        (my_cpl == 0) & (my_pts == 0), -1, jnp.where((my_cpl == 1) & (my_pts == owners - 1), 1, 0)
    )
    par = jnp.stack([my_pts, first_way, -first_way, turn, my_cpl, -first_way]).astype(I32)
    coef = coefficients(
        freq_local, dirs_local, pad_half, my_spec, my_cpl, freq_count, dir_count
    )

    found = call(
        functools.partial(index_kernel, owners, [start * step_rows for start, _ in chunks[2:]]),
        [SCALARS, WHOLE, WHOLE, WHOLE],
        [
            shape_of(5, 8, slots, kind=I32),
            shape_of(owners * owners, cell_sea.shape[1]),
            shape_of(8, slots),
        ]
        + [shape_of(rows + 8, LANES)] * (owners - 2)
        + [
            shape_of((stop - start) * step_rows + (8 if at == 0 else 0), slots)
            for at, (start, stop) in enumerate(chunks[2:])
        ],
    )(par, cell_sea, coef, field)
    found, beside[0] = lax.optimization_barrier((found, beside[0]))
    (idx, counts, row_sums), lists = found[:3], found[3 : owners + 1]
    leaving = found[owners + 1 :]
    arrived = [around(values, 2 + at) for at, values in enumerate(lists)]
    beside.append(around(leaving[0]))
    later, arrived, beside = lax.optimization_barrier((leaving[1:], arrived, beside))
    beside += [around(values) for values in later]

    pairs = jnp.sum(counts, axis=1).reshape(owners, owners)
    longest = jnp.max(pairs + pairs.T).reshape(1, 1)
    if groups == 2:
        longest = jnp.maximum(longest, lax.ppermute(longest, "grp", [(0, 1), (1, 0)]))
    else:
        longest = lax.pmax(longest, "grp")

    (slope_part,) = call(
        slope_kernel, [SCALARS] + [WHOLE] * (owners + 1), [shape_of(1, slots)]
    )(par, idx, row_sums, beside[2], *arrived)

    slope = slope_part + lax.ppermute(slope_part, "cpl", [(0, 1), (1, 0)])
    if spec_groups == 2:
        slope = slope + lax.ppermute(slope, "spec", [(0, 1), (1, 0)])
    else:
        slope = lax.psum(slope, "spec")

    slope, longest = lax.optimization_barrier((slope, longest))
    updated = sums = None
    for at, near in zip(chunks, beside):
        start, stop = at
        chained, final = start > 0, stop == steps
        in_rows = lambda width: pl.BlockSpec(
            (step_rows, width), functools.partial(lambda first, i: (first + i, 0), start)
        )
        inputs = [par, idx, wind_deck, slope, coef, field, near, *arrived]
        specs = [SCALARS] + [WHOLE] * 4 + [in_rows(slots)] + [WHOLE] * (owners - 1)
        aliases = {}
        if chained:
            aliases = {len(inputs): 0}
            inputs += [updated, sums]
            specs += [pl.BlockSpec(memory_space=pl.ANY), WHOLE]
        sum_shapes = [(2, blocks, LANES)] * 2 if final else [(4, blocks, LANES)]
        updated, *sums = pl.pallas_call(
            functools.partial(step_kernel, owners, start, steps // 2, chained, final),
            grid=(stop - start,),
            in_specs=specs,
            out_specs=[in_rows(slots)] + [WHOLE] * len(sum_shapes),
            out_shape=[pltpu.HBM((rows, slots), F32)] + [shape_of(*dims) for dims in sum_shapes],
            scratch_shapes=[pltpu.VMEM((4, 8, slots), F32), pltpu.VMEM((8, slots), F32)],
            input_output_aliases=aliases,
            compiler_params=pltpu.CompilerParams(vmem_limit_bytes=VMEM_BYTES),
            cost_estimate=SHORT,
        )(*inputs)
        if not final:
            sums = sums[0]

    mine, others = sums
    mine = mine + lax.ppermute(others, "cpl", [(0, 1), (1, 0)])
    if spec_groups == 2:
        mine = mine + lax.ppermute(mine, "spec", [(0, 1), (1, 0)])
    else:
        mine = lax.psum(mine, "spec")
    if owners == 4:
        tables = [mine] + [
            lax.ppermute(mine, "pts", [(i, i ^ turned) for i in range(owners)])
            for turned in range(1, owners)
        ]
        looked = lambda order: (order ^ my_pts)[None, :]
    else:
        gathered = lax.all_gather(mine, "pts", axis=0)
        tables = [gathered[owner] for owner in range(owners)]
        looked = lambda order: order[None, :]
    count = atm_order.shape[0]
    stress_atm, stokes_ocn = call(
        functools.partial(pick_kernel, owners),
        [WHOLE] * (2 + owners),
        [shape_of(1, count)] * 2,
    )(looked(atm_order), looked(ocean_order), *tables)

    def by_direction(values):
        return jnp.transpose(values, (1, 0, 2)).reshape(dirs_local * freq_local, slots)

    def general_way():
        spectra, stress, stokes = general(spec_deck, wind_deck, cell_sea, atm_order, ocean_order)
        return by_direction(spectra), stress, stokes

    if pad_half:
        updated = updated.reshape(2, half_rows + pad_half, slots)[:, :half_rows]
        updated = updated.reshape(2 * half_rows, slots)
    updated, stress_atm, stokes_ocn = lax.cond(
        longest[0, 0] > 2 * LANES, general_way, lambda: (updated, stress_atm, stokes_ocn)
    )
    updated = jnp.transpose(updated.reshape(dirs_local, freq_local, slots), (1, 0, 2))
    return updated, stress_atm, stokes_ocn


def solution(mesh):
    return jax.shard_map(
        local,
        mesh=mesh,
        in_specs=(
            P("spec", "cpl", ("grp", "pts")),
            P(None, ("grp", "pts")),
            P("grp", None),
            P(("grp", "pts", "spec")),
            P(("grp", "pts", "spec")),
        ),
        out_specs=(
            P("spec", "cpl", ("grp", "pts")),
            P("cpl", ("grp", "pts", "spec")),
            P("cpl", ("grp", "pts", "spec")),
        ),
        check_vma=False,
    )
```

```python
import functools
import math

import jax
import jax.numpy as jnp
from jax import lax
from jax.experimental import pallas as pl
from jax.experimental.pallas import tpu as pltpu
from jax.sharding import PartitionSpec as P

COURANT_MAX = 0.68
BASE_FREQ = 0.035
GRAVITY = 9.81
GROWTH_RATE = 0.02
SLOPE_REF = 0.09
STRESS_GAIN = 64.0
STOKES_GAIN = 64.0
LANES = 128
F32 = jnp.float32
BF16 = jnp.bfloat16
I32 = jnp.int32
WHOLE = pl.BlockSpec(memory_space=pltpu.VMEM)
SHORT = pl.CostEstimate(flops=1000, bytes_accessed=1000, transcendentals=0)
SCALARS = pl.BlockSpec(memory_space=pltpu.SMEM)


def passed_along(shard, axis, by):
    devices = lax.axis_size(axis)
    pairs = [(i, i + by) for i in range(devices) if 0 <= i + by < devices]
    return lax.ppermute(shard, axis, pairs)


def upwind(extended, mask_rows, courant_east, courant_north):
    middle = extended[:, :, 1:-1]
    prior_row = extended[:, :, :-2]
    next_row = extended[:, :, 2:]
    side_pad = jnp.pad(middle, ((0, 0), (0, 0), (0, 0), (1, 1)))
    prior_col = side_pad[..., :-2]
    next_col = side_pad[..., 2:]
    advanced = (
        middle
        - jnp.maximum(courant_east, 0.0) * (middle - prior_row)
        - jnp.maximum(-courant_east, 0.0) * (middle - next_row)
        - jnp.maximum(courant_north, 0.0) * (middle - prior_col)
        - jnp.maximum(-courant_north, 0.0) * (middle - next_col)
    )
    return advanced * mask_rows


def general(spec_deck, wind_deck, cell_sea, atm_order, ocean_order):
    owners = lax.axis_size("pts")
    spec_groups = lax.axis_size("spec")
    cpl_groups = lax.axis_size("cpl")
    my_pts = lax.axis_index("pts")
    my_spec = lax.axis_index("spec")
    my_cpl = lax.axis_index("cpl")
    freq_local, dirs_local, slots_local = spec_deck.shape
    grid_rows, grid_cols = cell_sea.shape
    freq_count = freq_local * spec_groups
    dir_count = dirs_local * cpl_groups
    sea_mask = cell_sea >= 0
    row_counts = jnp.sum(sea_mask.astype(jnp.int32), axis=1)
    before_row = jnp.concatenate([jnp.zeros((1,), jnp.int32), jnp.cumsum(row_counts)])
    tile_freq = my_spec * freq_local + jnp.arange(freq_local)
    height = 2 * (grid_rows // owners)
    capacity = (slots_local + grid_cols) // owners + 1
    targets = jnp.arange(owners + 1, dtype=jnp.int32) * slots_local
    row_starts = jnp.sum((before_row[None, :] < targets[:, None]).astype(jnp.int32), axis=1)
    width_cells = height * grid_cols
    bounds = jnp.take(before_row, row_starts)
    starts = bounds[:-1]
    my_row = jnp.take(row_starts, my_pts)
    my_height = jnp.take(row_starts, my_pts + 1) - my_row
    first_slot = -((jnp.arange(owners, dtype=jnp.int32)[None, :] - starts[:, None]) // owners)
    slot_range = jnp.arange(capacity, dtype=jnp.int32)
    own_first = jnp.take(first_slot, my_pts, axis=1)
    picked = jnp.clip(own_first[:, None] + slot_range[None, :], 0, slots_local - 1).reshape(-1)
    outgoing = jnp.take(spec_deck, picked, axis=2)
    arrived = lax.all_to_all(outgoing, "pts", split_axis=2, concat_axis=2, tiled=True)
    freq_here = arrived.shape[0]
    padded_map = jnp.concatenate([cell_sea, jnp.full((height, grid_cols), -1, jnp.int32)], axis=0)
    strip_map = lax.dynamic_slice_in_dim(padded_map, my_row, height, 0)
    row_valid = jnp.arange(height) < my_height
    strip_sea = ((strip_map >= 0) & row_valid[:, None]).reshape(-1)
    strip_map = strip_map.reshape(-1)
    safe_index = jnp.maximum(strip_map, 0)
    source = safe_index % owners
    strip_first = jnp.take(first_slot, my_pts, axis=0)
    where_from = jnp.where(
        strip_sea, source * capacity + safe_index // owners - jnp.take(strip_first, source), 0
    )
    wave_field = jnp.take(arrived, where_from, axis=2) * strip_sea.astype(jnp.float32)
    wave_field = wave_field.reshape(freq_here, dirs_local, height, grid_cols)
    freq_index = tile_freq.astype(jnp.float32)
    dir_index = (my_cpl * dirs_local + jnp.arange(dirs_local)).astype(jnp.float32)
    angles = 2.0 * math.pi * (dir_index + 0.5) / dir_count
    dir_cosine = jnp.cos(angles)
    dir_sine = jnp.sin(angles)
    speeds = COURANT_MAX * jnp.power(1.1, -freq_index)
    courant_east = (speeds[:, None] * dir_cosine[None, :])[:, :, None, None]
    courant_north = (speeds[:, None] * dir_sine[None, :])[:, :, None, None]
    strip_mask = strip_sea.astype(jnp.float32).reshape(height, grid_cols)
    last_row = lax.dynamic_slice_in_dim(wave_field, my_height - 1, 1, 2)
    from_above = passed_along(last_row, "pts", 1)
    from_below = passed_along(wave_field[:, :, :1], "pts", -1)
    extended = jnp.concatenate([from_above, wave_field, jnp.zeros_like(from_below)], axis=2)
    extended = lax.dynamic_update_slice_in_dim(extended, from_below, my_height + 1, 2)
    wave_field = upwind(extended, strip_mask, courant_east, courant_north)
    flat_field = wave_field.reshape(freq_here, dirs_local, width_cells)
    strip_start = jnp.take(starts, my_pts)
    inverse = (
        jnp.zeros((width_cells,), jnp.int32)
        .at[jnp.where(strip_sea, strip_map - strip_start, width_cells)]
        .set(jnp.arange(width_cells, dtype=jnp.int32), mode="drop")
    )
    wanted = (strip_first[:, None] + slot_range[None, :]) * owners + jnp.arange(
        owners, dtype=jnp.int32
    )[:, None]
    cells_out = jnp.take(inverse, jnp.clip(wanted - strip_start, 0, width_cells - 1).reshape(-1))
    leaving = jnp.take(flat_field, cells_out, axis=2)
    returned = lax.all_to_all(leaving, "pts", split_axis=2, concat_axis=2, tiled=True)
    slot_index = jnp.arange(slots_local, dtype=jnp.int32)
    points = slot_index * owners + my_pts
    strip_of = jnp.sum((starts[None, 1:] <= points[:, None]).astype(jnp.int32), axis=1)
    offset = slot_index - jnp.take(own_first, strip_of)
    position = strip_of * capacity + offset
    propagated = jnp.take(returned, position, axis=2)
    band_freq = (my_spec * freq_local + jnp.arange(freq_local)).astype(jnp.float32)
    sigma_freq = 2.0 * math.pi * BASE_FREQ * jnp.power(1.1, band_freq)
    phase_speed = GRAVITY / sigma_freq
    slope_weight = jnp.power(1.1, 0.4 * band_freq)
    slope_part = jnp.sum(propagated * slope_weight[:, None, None], axis=(0, 1))
    slope_total = lax.psum(slope_part, ("spec", "cpl")) / (SLOPE_REF * freq_count * dir_count)
    wind_along = (
        wind_deck[0][None, None, :] * dir_cosine[None, :, None]
        + wind_deck[1][None, None, :] * dir_sine[None, :, None]
    )
    growth = (
        GROWTH_RATE
        * sigma_freq[:, None, None]
        * jnp.maximum(wind_along / phase_speed[:, None, None] - 1.0, 0.0)
    )
    sigma_top = 2.0 * math.pi * BASE_FREQ * 1.1 ** (freq_count - 1)
    damping = (sigma_freq / sigma_top)[:, None, None] * (slope_total * slope_total)[None, None, :]
    updated = propagated * jnp.exp(growth - damping)
    lifted = growth * propagated
    drift_part = updated * jnp.power(1.1, 2.0 * (band_freq - (freq_count - 1)))[:, None, None]
    stress_scale = STRESS_GAIN / freq_count
    stokes_scale = STOKES_GAIN / math.sqrt(freq_count * dir_count)
    coupled_part = jnp.stack(
        [
            stress_scale * jnp.sum(lifted * dir_cosine[None, :, None], axis=(0, 1)),
            stress_scale * jnp.sum(lifted * dir_sine[None, :, None], axis=(0, 1)),
            stokes_scale * jnp.sum(drift_part * dir_cosine[None, :, None], axis=(0, 1)),
            stokes_scale * jnp.sum(drift_part * dir_sine[None, :, None], axis=(0, 1)),
        ]
    )
    coupled_total = lax.psum(coupled_part, ("spec", "cpl"))
    coupled_all = lax.all_gather(coupled_total, "pts", axis=1, tiled=True)
    atm_col = atm_order % owners * slots_local + atm_order // owners
    ocean_col = ocean_order % owners * slots_local + ocean_order // owners
    stress_atm = jnp.take(lax.dynamic_slice_in_dim(coupled_all, my_cpl, 1, 0), atm_col, axis=1)
    stokes_ocn = jnp.take(
        lax.dynamic_slice_in_dim(coupled_all, 2 + my_cpl, 1, 0), ocean_col, axis=1
    )
    return (updated, stress_atm, stokes_ocn)


C_KEEP, C_ROW, C_COL, C_SLOPE, C_EAST, C_NORTH, C_ONE, C_DAMP = range(8)
C_S_EAST, C_S_NORTH, C_T_EAST, C_T_NORTH = range(8, 12)
CHUNK_ENDS = (3, 6, 7, 12, 16)
FOURTH_EARLY = True
VMEM_BYTES = 24 * 1024 * 1024


def times_hot(value, one_hot, dims, parts=3):
    count = value.shape[0]
    pieces = []
    for _ in range(parts):
        pieces.append(value.astype(BF16).astype(F32))
        value = value - pieces[-1]
    stacked = jnp.concatenate(pieces, axis=0).astype(BF16)
    found = lax.dot_general(stacked, one_hot, (dims, ((), ())), preferred_element_type=F32)
    return sum(found[part * count : (part + 1) * count] for part in range(parts))


def index_kernel(owners, starts, par_ref, cell_ref, coef_ref, g_ref, idx_ref, count_ref, sum_ref, *refs):
    list_refs, chunk_refs = refs[: owners - 2], refs[owners - 2 :]
    slots = g_ref.shape[1]
    blocks = slots // LANES
    half_rows = g_ref.shape[0] // 2
    shift = owners.bit_length() - 1
    pts = par_ref[0]
    number = cell_ref[...].astype(F32)
    sea = number >= 0.0
    first = jnp.min(jnp.where(sea, number, 1e9), axis=1, keepdims=True)
    last = jnp.max(jnp.where(sea, number, -1.0), axis=1, keepdims=True)
    rank = jnp.where(sea, number - first + 1.0, 0.0)
    edge = jnp.full((1, number.shape[1]), -1.0, F32)
    above = jnp.concatenate([edge, number[:-1]], axis=0)
    below = jnp.concatenate([number[1:], edge], axis=0)
    to_above = jnp.where(sea & (above >= 0.0), number - above, 0.0)
    to_below = jnp.where(sea & (below >= 0.0), below - number, 0.0)
    ids = cell_ref[...] & (owners - 1)
    above_ids = above.astype(I32) & (owners - 1)
    crossing = (to_above > 0.0) & (ids != above_ids)
    pair = jnp.where(crossing, above_ids * owners + ids, -1)

    @pl.loop(0, owners * owners)
    def _(which):
        count_ref[pl.ds(which, 1), :] = jnp.sum(
            jnp.where(pair == which, 1.0, 0.0), axis=0, keepdims=True
        )

    cols = number.shape[1]
    column = lax.broadcasted_iota(I32, number.shape, 1)
    left = jnp.where(column == 0, -1.0, pltpu.roll(number, 1, 1))
    right = jnp.where(column == cols - 1, -1.0, pltpu.roll(number, cols - 1, 1))
    beside = jnp.where(par_ref[4] == 0, left, right)
    beside = jnp.where(sea & (beside >= 0.0), 1.0, 0.0)

    slot = lax.broadcasted_iota(I32, (1, slots), 1)
    point = slot * owners + pts
    pointf = point.astype(F32)
    in_row = (first <= pointf) & (pointf <= last)
    row_hot = jnp.where(in_row, 1.0, 0.0).astype(BF16)
    row_first = jnp.sum(jnp.where(in_row, first, 0.0), axis=0, keepdims=True)

    def of_row(values):
        return jnp.dot(
            jnp.transpose(values).astype(BF16), row_hot, preferred_element_type=F32
        )

    here = of_row(rank) == (pointf - row_first + 1.0)

    def of_point(values):
        return jnp.sum(jnp.where(here, of_row(values), 0.0), axis=0, keepdims=True)

    step_above = of_point(to_above).astype(I32)
    step_below = of_point(to_below).astype(I32)
    has_beside = of_point(beside).astype(I32)

    groups = max(8, owners)
    group = lax.broadcasted_iota(I32, (groups, slots), 0)
    codes, masks = [], []
    for half in range(2):
        up = par_ref[1 + half] < 0
        for sends in range(2):
            minus = up if sends == 0 else jnp.logical_not(up)
            step = jnp.where(minus, step_above, step_below)
            other = jnp.where(minus, point - step_above, point + step_below)
            owner = other & (owners - 1)
            away = ((pts - owner) if sends == 0 else (owner - pts)) * par_ref[5]
            away = jnp.where(step > 0, away & (owners - 1), -1)
            codes.append((away, other >> shift))
            masks.append(jnp.where(group == away, 1.0, 0.0))
    mask = jnp.concatenate(masks, axis=0)
    before = jnp.where(
        lax.broadcasted_iota(I32, (LANES, LANES), 0) < lax.broadcasted_iota(I32, (LANES, LANES), 1),
        1.0,
        0.0,
    ).astype(BF16)
    carry = jnp.zeros((mask.shape[0], 1), F32)
    counts = []
    for block in range(blocks):
        part = mask[:, block * LANES : (block + 1) * LANES]
        inside = jnp.dot(part.astype(BF16), before, preferred_element_type=F32)
        counts.append((inside + carry) * part)
        carry = carry + jnp.sum(part, axis=1, keepdims=True)
    counts = jnp.concatenate(counts, axis=1)
    sum_ref[...] = jnp.zeros_like(sum_ref)
    for half in range(2):
        rows = slice(half * half_rows, (half + 1) * half_rows)
        weight = coef_ref[rows, C_SLOPE : C_SLOPE + 1]
        weighted = g_ref[rows, :] * weight
        for at, column_of in ((0, C_KEEP), (1 + half, C_ROW), (3, C_COL)):
            sum_ref[at : at + 1, :] += jnp.sum(
                weighted * coef_ref[rows, column_of : column_of + 1], axis=0, keepdims=True
            )
    entry = lax.broadcasted_iota(I32, (2 * LANES, slots), 0)
    keys = []
    for half in range(2):
        receive, send = [
            jnp.sum(
                counts[(2 * half + sends) * groups : (2 * half + sends + 1) * groups],
                axis=0,
                keepdims=True,
            ).astype(I32)
            for sends in range(2)
        ]
        away, other_slot = codes[2 * half]
        spilled = receive >= LANES
        place = jnp.where(spilled, jnp.maximum(2 * LANES - 1 - receive, 0), receive)
        other_block = jnp.where((other_slot >> 7) == (slot >> 7), 0, 1)
        code = jnp.where(away <= 1, 1 + 2 * away + other_block, 1 + 2 * away + jnp.where(spilled, 1, 0))
        lane = jnp.where(away <= 1, other_slot & (LANES - 1), place)
        idx_ref[2 * half] = jnp.broadcast_to(jnp.where(away < 0, 0, lane), (8, slots))
        idx_ref[2 * half + 1] = jnp.broadcast_to(jnp.where(away < 0, 0, code), (8, slots))
        away, _ = codes[2 * half + 1]
        place = jnp.where(send >= LANES, 3 * LANES - 1 - send, send)
        place = jnp.where(send >= 2 * LANES, -1, place)
        key = jnp.where((away > 1) & (place >= 0), (away - 2) * 2 * LANES + place, -1)
        keys.append(key)
    for at, list_ref in enumerate(list_refs):
        for half in range(2):
            one_hot = jnp.where(entry == keys[half] - at * 2 * LANES, 1.0, 0.0).astype(BF16)
            rows = slice(half * half_rows, (half + 1) * half_rows)
            packed = times_hot(g_ref[rows, :], one_hot, ((1,), (1,)), 2)
            sums = times_hot(sum_ref[...], one_hot, ((1,), (1,)))[1 + half : 2 + half]
            other = slice((1 - half) * half_rows, (2 - half) * half_rows)
            own_row = slice(2 * half_rows + half, 2 * half_rows + half + 1)
            other_row = slice(2 * half_rows + 1 - half, 2 * half_rows + 2 - half)
            if half == 0:
                list_ref[rows, :] = packed[:, :LANES]
                list_ref[other, :] = packed[:, LANES:]
                list_ref[own_row, :] = sums[:, :LANES]
                list_ref[other_row, :] = sums[:, LANES:]
            else:
                list_ref[rows, :] += packed[:, :LANES]
                list_ref[other, :] += packed[:, LANES:]
                list_ref[own_row, :] += sums[:, :LANES]
                list_ref[other_row, :] += sums[:, LANES:]
    chunk_refs[0][-8:, :] = sum_ref[...]
    for start, chunk_ref in zip(starts, chunk_refs):
        count = chunk_ref.shape[0] - (8 if start == starts[0] else 0)
        chunk_ref[:count, :] = g_ref[start : start + count, :]
    for list_ref in list_refs:
        list_ref[2 * half_rows + 2 :, :] = jnp.zeros((6, LANES), F32)
    idx_ref[4] = jnp.broadcast_to(has_beside, (8, slots))


def lane_take(values, lanes):
    return jnp.take_along_axis(values, lanes, axis=1)


def row_neighbour(code, lanes, sources, places=range(4)):
    value = jnp.zeros(code.shape, F32)
    for place, source in zip(places, sources):
        value = jnp.where(code == 1 + place, lane_take(source, lanes), value)
    return value


def near_block(ref, rows, block, step):
    which = jnp.clip(block + step, 0, ref.shape[1] // LANES - 1)
    return ref[rows, pl.ds(pl.multiple_of(which * LANES, LANES), LANES)]


def turned_lanes(turn):
    lane = lax.broadcasted_iota(I32, (8, LANES), 1)
    lanes = (lane + turn) & (LANES - 1)
    return lanes, (lane + turn) != lanes


def slope_kernel(par_ref, idx_ref, sum_ref, beside_ref, *refs):
    list_refs, slope_ref = refs[:-1], refs[-1]
    shape = (8, LANES)
    turn = par_ref[3]
    beside_lanes, beyond = turned_lanes(turn)
    every, last = slice(0, 8), slice(beside_ref.shape[0] - 8, beside_ref.shape[0])
    lists = [ref[-8:, :] for ref in list_refs]
    for block in range(sum_ref.shape[1] // LANES):
        at = slice(block * LANES, (block + 1) * LANES)
        own, beside = sum_ref[:, at], beside_ref[last, at]
        slope = own[0:1]
        for half in range(2):
            lanes, code = idx_ref[2 * half, :, at], idx_ref[2 * half + 1, :, at]
            way = par_ref[1 + half]
            sources = [own, near_block(sum_ref, every, block, way)]
            sources += [beside, near_block(beside_ref, last, block, way)]
            value = row_neighbour(code, lanes, sources)
            slope = slope + value[1 + half : 2 + half]
            code = code - 4
            for values in lists:
                for row in (half, 1 - half):
                    value = jnp.where(code == 1, lane_take(values, lanes), 0.0)
                    slope = slope + value[row : row + 1]
                    code = code - 1
        column = jnp.where(
            beyond,
            lane_take(near_block(beside_ref, last, block, turn), beside_lanes),
            lane_take(beside, beside_lanes),
        )
        slope_ref[:, at] = slope + jnp.where(idx_ref[4, 0:1, at] > 0, column[3:4], 0.0)


def step_kernel(owners, parts, half_steps, chained, final, par_ref, spill_ref, idx_ref, wind_ref, slope_ref, coef_ref, g_ref, *refs):
    beside_refs, refs = refs[: len(parts)], refs[len(parts) :]
    list_refs, refs = refs[: owners - 2], refs[owners - 2 :]
    if chained:
        _, before_ref, refs = refs[0], refs[1], refs[2:]
    out_ref, sums_refs, total_ref, damp_ref = refs[0], refs[1:-2], refs[-2], refs[-1]
    blocks = g_ref.shape[1] // LANES
    shape = (8, LANES)
    step = pl.program_id(0)
    step_rows = out_ref.shape[0]
    first_step = parts[0][0]
    half = jnp.where(step + first_step >= half_steps, 1, 0)
    way, turn = par_ref[1 + half], par_ref[3]
    lane = lax.broadcasted_iota(I32, shape, 1)
    turned = (lane + turn) & (LANES - 1)
    edge = lane == jnp.where(turn < 0, LANES - 1, jnp.where(turn > 0, 0, -1))

    @pl.when(step == 0)
    def _():
        total_ref[...] = jnp.zeros_like(total_ref)
        slope = slope_ref[...]
        damp_ref[...] = jnp.broadcast_to(slope * slope, damp_ref.shape)

    def tiles(beside_ref, spills):
        for tile in range(step_rows // 8):
            here = slice(tile * 8, tile * 8 + 8)

            def at_row(first):
                return pl.ds(pl.multiple_of(first, 8), 8)

            first = (step + first_step) * step_rows + tile * 8
            rows = at_row(first)
            other_rows = at_row(first + (1 - 2 * half) * half_steps * step_rows)
            coef = coef_ref[rows, :]

            def factor(at):
                return jnp.broadcast_to(coef[:, at : at + 1], shape)

            keep, by_row, by_col = factor(C_KEEP), factor(C_ROW), factor(C_COL)
            east, north, one, damp = factor(C_EAST), factor(C_NORTH), factor(C_ONE), factor(C_DAMP)
            s_east, s_north = factor(C_S_EAST), factor(C_S_NORTH)
            t_east, t_north = factor(C_T_EAST), factor(C_T_NORTH)
            sides = (rows, other_rows) if spills else (rows,)
            lists = [ref[which, :] for ref in list_refs for which in sides]
            places = list(range(4))
            places += [4 + 2 * at + side for at in range(owners - 2) for side in range(len(sides))]
            for block in range(blocks):
                at = slice(block * LANES, (block + 1) * LANES)
                lanes, code = idx_ref[2 * half, :, at], idx_ref[2 * half + 1, :, at]
                has_beside = idx_ref[4, :, at]
                own, beside = g_ref[here, at], beside_ref[here, at]
                sources = [own, near_block(g_ref, here, block, way)]
                sources += [beside, near_block(beside_ref, here, block, way)]
                row_value = row_neighbour(code, lanes, sources + lists, places)
                turning = near_block(beside_ref, here, block, turn)
                col_value = lane_take(jnp.where(edge, turning, beside), turned)
                col_value = jnp.where(has_beside > 0, col_value, 0.0)
                value = keep * own + by_row * row_value + by_col * col_value
                wind_east = jnp.broadcast_to(wind_ref[0:1, at], shape)
                wind_north = jnp.broadcast_to(wind_ref[1:2, at], shape)
                growth = jnp.maximum(east * wind_east + north * wind_north - one, 0.0)
                updated = value * jnp.exp(growth - damp * damp_ref[:, at])
                out_ref[here, at] = updated
                lifted = growth * value
                total_ref[0, :, at] += s_east * lifted
                total_ref[1, :, at] += s_north * lifted
                total_ref[2, :, at] += t_east * updated
                total_ref[3, :, at] += t_north * updated

    for (start, stop), beside_ref in zip(parts, beside_refs):
        for spills in (False, True):
            inside = (step >= start - first_step) & (step < stop - first_step)

            @pl.when(inside & ((spill_ref[0] > 0) == spills))
            def _():
                tiles(beside_ref, spills)

    @pl.when(step == pl.num_programs(0) - 1)
    def _():
        cpl = par_ref[4]
        for item in range(2):
            for block in range(blocks):
                at = slice(block * LANES, (block + 1) * LANES)
                pair = []
                for part in range(2):
                    value = jnp.sum(total_ref[2 * item + part, :, at], axis=0, keepdims=True)
                    if chained:
                        value = value + before_ref[2 * item + part, block : block + 1, :]
                    pair.append(value)
                where = slice(block, block + 1)
                if final:
                    sums_refs[0][item, where, :] = jnp.where(cpl == 0, pair[0], pair[1])
                    sums_refs[1][item, where, :] = jnp.where(cpl == 0, pair[1], pair[0])
                else:
                    sums_refs[0][2 * item, where, :] = pair[0]
                    sums_refs[0][2 * item + 1, where, :] = pair[1]


def pick_kernel(owners, atm_ref, ocean_ref, *refs):
    table_refs, (stress_ref, stokes_ref) = refs[:owners], refs[owners:]
    shift = owners.bit_length() - 1
    blocks = table_refs[0].shape[1]
    for item, (order_ref, out_ref) in enumerate(((atm_ref, stress_ref), (ocean_ref, stokes_ref))):
        point = order_ref[...]
        count = point.shape[1]
        slot = point >> shift
        row = (point & (owners - 1)) * blocks + (slot >> 7)
        lane = slot & (LANES - 1)
        rows = owners * blocks
        hot = jnp.where(lax.broadcasted_iota(I32, (rows, count), 0) == row, 1.0, 0.0).astype(BF16)
        table = jnp.concatenate([ref[item] for ref in table_refs], axis=0)
        table = jnp.transpose(table)
        found = times_hot(table, hot, ((1,), (0,)))
        pick = lax.broadcasted_iota(I32, (LANES, count), 0) == lane
        out_ref[...] = jnp.sum(jnp.where(pick, found, 0.0), axis=0, keepdims=True)


def coefficients(freq_local, dirs_local, pad_half, my_spec, my_cpl, freq_count, dir_count):
    freq = (my_spec * freq_local + jnp.arange(freq_local)).astype(F32)
    direction = (my_cpl * dirs_local + jnp.arange(dirs_local)).astype(F32)
    angles = 2.0 * math.pi * (direction + 0.5) / dir_count
    cosine, sine = jnp.cos(angles)[:, None], jnp.sin(angles)[:, None]
    speed = COURANT_MAX * jnp.power(1.1, -freq)[None, :]
    by_row, by_col = jnp.abs(speed * cosine), jnp.abs(speed * sine)
    sigma = (2.0 * math.pi * BASE_FREQ * jnp.power(1.1, freq))[None, :]
    sigma_top = 2.0 * math.pi * BASE_FREQ * 1.1 ** (freq_count - 1)
    inverse_speed = sigma / GRAVITY
    rate = GROWTH_RATE * sigma
    drift = jnp.power(1.1, 2.0 * (freq - (freq_count - 1)))[None, :]
    stress_scale = STRESS_GAIN / freq_count
    stokes_scale = STOKES_GAIN / math.sqrt(freq_count * dir_count)
    shape = (dirs_local, freq_local)
    columns = [
        1.0 - by_row - by_col,
        by_row,
        by_col,
        jnp.power(1.1, 0.4 * freq)[None, :] / (SLOPE_REF * freq_count * dir_count),
        rate * inverse_speed * cosine,
        rate * inverse_speed * sine,
        rate,
        sigma / sigma_top,
        stress_scale * cosine,
        stress_scale * sine,
        stokes_scale * drift * cosine,
        stokes_scale * drift * sine,
    ]
    table = jnp.stack([jnp.broadcast_to(column, shape) for column in columns], axis=-1)
    table = table.reshape(2, -1, len(columns))
    table = jnp.pad(table, ((0, 0), (0, pad_half), (0, 16 - len(columns))))
    return table.reshape(-1, 16)


def shape_of(*dims, kind=F32):
    return jax.ShapeDtypeStruct(dims, kind)


def call(kernel, inputs, outputs):
    return pl.pallas_call(
        kernel,
        in_specs=inputs,
        out_specs=[WHOLE] * len(outputs),
        out_shape=outputs,
        compiler_params=pltpu.CompilerParams(vmem_limit_bytes=VMEM_BYTES),
        cost_estimate=SHORT,
    )


def chunks_of(steps):
    ends = sorted({max(1, steps * part // 18) for part in CHUNK_ENDS} | {steps})
    return list(zip([0] + ends[:-1], ends))


def local(spec_deck, wind_deck, cell_sea, atm_order, ocean_order):
    owners = lax.axis_size("pts")
    spec_groups = lax.axis_size("spec")
    cpl_groups = lax.axis_size("cpl")
    groups = lax.axis_size("grp")
    my_pts = lax.axis_index("pts")
    my_spec = lax.axis_index("spec")
    my_cpl = lax.axis_index("cpl")
    assert cpl_groups == 2 and owners & (owners - 1) == 0
    freq_local, dirs_local, slots = spec_deck.shape
    freq_count = freq_local * spec_groups
    dir_count = dirs_local * cpl_groups
    blocks = slots // LANES
    half_rows = freq_local * dirs_local // 2
    pad_half = -half_rows % 8
    rows = 2 * (half_rows + pad_half)
    step_rows = 16 if (half_rows + pad_half) % 16 == 0 else 8
    steps = rows // step_rows

    field = jnp.transpose(spec_deck, (1, 0, 2)).reshape(2, half_rows, slots)
    if pad_half:
        field = jnp.pad(field, ((0, 0), (0, pad_half), (0, 0)))
    field = field.reshape(rows, slots)

    def around(values, distance=1):
        pairs = []
        for owner in range(owners):
            pairs.append((owner * 2, (owner + distance) % owners * 2))
            pairs.append((owner * 2 + 1, (owner - distance) % owners * 2 + 1))
        return lax.ppermute(values, ("pts", "cpl"), pairs)

    def chunk(values, at):
        return values[at[0] * step_rows : at[1] * step_rows]

    chunks = chunks_of(steps)
    first = chunk(field, chunks[0])
    rest, first = lax.optimization_barrier((field, first))
    beside = [around(first), around(chunk(rest, chunks[1]))]

    first_way = 2 * my_cpl - 1
    turn = jnp.where(
        (my_cpl == 0) & (my_pts == 0), -1, jnp.where((my_cpl == 1) & (my_pts == owners - 1), 1, 0)
    )
    par = jnp.stack([my_pts, first_way, -first_way, turn, my_cpl, -first_way]).astype(I32)
    coef = coefficients(
        freq_local, dirs_local, pad_half, my_spec, my_cpl, freq_count, dir_count
    )

    found = call(
        functools.partial(index_kernel, owners, [start * step_rows for start, _ in chunks[2:]]),
        [SCALARS, WHOLE, WHOLE, WHOLE],
        [
            shape_of(5, 8, slots, kind=I32),
            shape_of(owners * owners, cell_sea.shape[1]),
            shape_of(8, slots),
        ]
        + [shape_of(rows + 8, LANES)] * (owners - 2)
        + [
            shape_of((stop - start) * step_rows + (8 if at == 0 else 0), slots)
            for at, (start, stop) in enumerate(chunks[2:])
        ],
    )(par, cell_sea, coef, field)
    found, beside[0] = lax.optimization_barrier((found, beside[0]))
    (idx, counts, row_sums), lists = found[:3], found[3 : owners + 1]
    leaving = found[owners + 1 :]
    arrived = [around(values, 2 + at) for at, values in enumerate(lists)]
    pairs = jnp.sum(counts, axis=1).reshape(owners, owners)
    spills = jnp.where(jnp.max(pairs) > LANES, 1, 0).astype(I32).reshape(1)
    longest = jnp.max(pairs + pairs.T).reshape(1, 1)
    if groups == 2:
        longest = jnp.maximum(longest, lax.ppermute(longest, "grp", [(0, 1), (1, 0)]))
    else:
        longest = lax.pmax(longest, "grp")
    beside.append(around(leaving[0]))
    later = list(leaving[1:])
    if FOURTH_EARLY:
        later[0], beside[1] = lax.optimization_barrier((later[0], beside[1]))
        beside.append(around(later.pop(0)))
    later, arrived, beside[2], longest, spills = lax.optimization_barrier(
        (later, arrived, beside[2], longest, spills)
    )
    beside += [around(values) for values in later]

    (slope_part,) = call(
        slope_kernel, [SCALARS] + [WHOLE] * (owners + 1), [shape_of(1, slots)]
    )(par, idx, row_sums, beside[2], *arrived)

    slope = slope_part + lax.ppermute(slope_part, "cpl", [(0, 1), (1, 0)])
    if spec_groups == 2:
        slope = slope + lax.ppermute(slope, "spec", [(0, 1), (1, 0)])
    else:
        slope = lax.psum(slope, "spec")

    updated = sums = None
    for parts in [chunks[:3]] + [[at] for at in chunks[3:]]:
        start, stop = parts[0][0], parts[-1][1]
        chained, final = start > 0, stop == steps
        in_rows = pl.BlockSpec(
            (step_rows, slots), functools.partial(lambda first, i: (first + i, 0), start)
        )
        near, beside = beside[: len(parts)], beside[len(parts) :]
        inputs = [par, spills, idx, wind_deck, slope, coef, field, *near, *arrived]
        specs = [SCALARS] * 2 + [WHOLE] * 4 + [in_rows]
        for first, end in parts:
            within = lambda skipped, most, i: (jnp.clip(i - skipped, 0, most), 0)
            within = functools.partial(within, first - start, end - first - 1)
            specs.append(pl.BlockSpec((step_rows, slots), within))
        specs += [WHOLE] * len(arrived)
        aliases = {}
        if chained:
            aliases = {len(inputs): 0}
            inputs += [updated, sums]
            specs += [pl.BlockSpec(memory_space=pl.ANY), WHOLE]
        sum_shapes = [(2, blocks, LANES)] * 2 if final else [(4, blocks, LANES)]
        updated, *sums = pl.pallas_call(
            functools.partial(step_kernel, owners, parts, steps // 2, chained, final),
            grid=(stop - start,),
            in_specs=specs,
            out_specs=[in_rows] + [WHOLE] * len(sum_shapes),
            out_shape=[pltpu.HBM((rows, slots), F32)] + [shape_of(*dims) for dims in sum_shapes],
            scratch_shapes=[pltpu.VMEM((4, 8, slots), F32), pltpu.VMEM((8, slots), F32)],
            input_output_aliases=aliases,
            compiler_params=pltpu.CompilerParams(vmem_limit_bytes=VMEM_BYTES),
            cost_estimate=SHORT,
        )(*inputs)
        if not final:
            sums = sums[0]

    mine, others = sums
    mine = mine + lax.ppermute(others, "cpl", [(0, 1), (1, 0)])
    if spec_groups == 2:
        mine = mine + lax.ppermute(mine, "spec", [(0, 1), (1, 0)])
    else:
        mine = lax.psum(mine, "spec")
    if owners == 4:
        tables = [mine] + [
            lax.ppermute(mine, "pts", [(i, i ^ turned) for i in range(owners)])
            for turned in range(1, owners)
        ]
        looked = lambda order: (order ^ my_pts)[None, :]
    else:
        gathered = lax.all_gather(mine, "pts", axis=0)
        tables = [gathered[owner] for owner in range(owners)]
        looked = lambda order: order[None, :]
    count = atm_order.shape[0]
    stress_atm, stokes_ocn = call(
        functools.partial(pick_kernel, owners),
        [WHOLE] * (2 + owners),
        [shape_of(1, count)] * 2,
    )(looked(atm_order), looked(ocean_order), *tables)

    def by_direction(values):
        return jnp.transpose(values, (1, 0, 2)).reshape(dirs_local * freq_local, slots)

    def general_way():
        spectra, stress, stokes = general(spec_deck, wind_deck, cell_sea, atm_order, ocean_order)
        return by_direction(spectra), stress, stokes

    if pad_half:
        updated = updated.reshape(2, half_rows + pad_half, slots)[:, :half_rows]
        updated = updated.reshape(2 * half_rows, slots)
    updated, stress_atm, stokes_ocn = lax.cond(
        longest[0, 0] > 2 * LANES, general_way, lambda: (updated, stress_atm, stokes_ocn)
    )
    updated = jnp.transpose(updated.reshape(dirs_local, freq_local, slots), (1, 0, 2))
    return updated, stress_atm, stokes_ocn


def solution(mesh):
    return jax.shard_map(
        local,
        mesh=mesh,
        in_specs=(
            P("spec", "cpl", ("grp", "pts")),
            P(None, ("grp", "pts")),
            P("grp", None),
            P(("grp", "pts", "spec")),
            P(("grp", "pts", "spec")),
        ),
        out_specs=(
            P("spec", "cpl", ("grp", "pts")),
            P("cpl", ("grp", "pts", "spec")),
            P("cpl", ("grp", "pts", "spec")),
        ),
        check_vma=False,
    )
```

```python
import functools
import math

import jax
import jax.numpy as jnp
from jax import lax
from jax.experimental import pallas as pl
from jax.experimental.pallas import tpu as pltpu
from jax.sharding import PartitionSpec as P

COURANT_MAX = 0.68
BASE_FREQ = 0.035
GRAVITY = 9.81
GROWTH_RATE = 0.02
SLOPE_REF = 0.09
STRESS_GAIN = 64.0
STOKES_GAIN = 64.0
LANES = 128
F32 = jnp.float32
BF16 = jnp.bfloat16
I32 = jnp.int32
WHOLE = pl.BlockSpec(memory_space=pltpu.VMEM)
SHORT = pl.CostEstimate(flops=1000, bytes_accessed=1000, transcendentals=0)
SCALARS = pl.BlockSpec(memory_space=pltpu.SMEM)


def passed_along(shard, axis, by):
    devices = lax.axis_size(axis)
    pairs = [(i, i + by) for i in range(devices) if 0 <= i + by < devices]
    return lax.ppermute(shard, axis, pairs)


def upwind(extended, mask_rows, courant_east, courant_north):
    middle = extended[:, :, 1:-1]
    prior_row = extended[:, :, :-2]
    next_row = extended[:, :, 2:]
    side_pad = jnp.pad(middle, ((0, 0), (0, 0), (0, 0), (1, 1)))
    prior_col = side_pad[..., :-2]
    next_col = side_pad[..., 2:]
    advanced = (
        middle
        - jnp.maximum(courant_east, 0.0) * (middle - prior_row)
        - jnp.maximum(-courant_east, 0.0) * (middle - next_row)
        - jnp.maximum(courant_north, 0.0) * (middle - prior_col)
        - jnp.maximum(-courant_north, 0.0) * (middle - next_col)
    )
    return advanced * mask_rows


def general(spec_deck, wind_deck, cell_sea, atm_order, ocean_order):
    owners = lax.axis_size("pts")
    spec_groups = lax.axis_size("spec")
    cpl_groups = lax.axis_size("cpl")
    my_pts = lax.axis_index("pts")
    my_spec = lax.axis_index("spec")
    my_cpl = lax.axis_index("cpl")
    freq_local, dirs_local, slots_local = spec_deck.shape
    grid_rows, grid_cols = cell_sea.shape
    freq_count = freq_local * spec_groups
    dir_count = dirs_local * cpl_groups
    sea_mask = cell_sea >= 0
    row_counts = jnp.sum(sea_mask.astype(jnp.int32), axis=1)
    before_row = jnp.concatenate([jnp.zeros((1,), jnp.int32), jnp.cumsum(row_counts)])
    tile_freq = my_spec * freq_local + jnp.arange(freq_local)
    height = 2 * (grid_rows // owners)
    capacity = (slots_local + grid_cols) // owners + 1
    targets = jnp.arange(owners + 1, dtype=jnp.int32) * slots_local
    row_starts = jnp.sum((before_row[None, :] < targets[:, None]).astype(jnp.int32), axis=1)
    width_cells = height * grid_cols
    bounds = jnp.take(before_row, row_starts)
    starts = bounds[:-1]
    my_row = jnp.take(row_starts, my_pts)
    my_height = jnp.take(row_starts, my_pts + 1) - my_row
    first_slot = -((jnp.arange(owners, dtype=jnp.int32)[None, :] - starts[:, None]) // owners)
    slot_range = jnp.arange(capacity, dtype=jnp.int32)
    own_first = jnp.take(first_slot, my_pts, axis=1)
    picked = jnp.clip(own_first[:, None] + slot_range[None, :], 0, slots_local - 1).reshape(-1)
    outgoing = jnp.take(spec_deck, picked, axis=2)
    arrived = lax.all_to_all(outgoing, "pts", split_axis=2, concat_axis=2, tiled=True)
    freq_here = arrived.shape[0]
    padded_map = jnp.concatenate([cell_sea, jnp.full((height, grid_cols), -1, jnp.int32)], axis=0)
    strip_map = lax.dynamic_slice_in_dim(padded_map, my_row, height, 0)
    row_valid = jnp.arange(height) < my_height
    strip_sea = ((strip_map >= 0) & row_valid[:, None]).reshape(-1)
    strip_map = strip_map.reshape(-1)
    safe_index = jnp.maximum(strip_map, 0)
    source = safe_index % owners
    strip_first = jnp.take(first_slot, my_pts, axis=0)
    where_from = jnp.where(
        strip_sea, source * capacity + safe_index // owners - jnp.take(strip_first, source), 0
    )
    wave_field = jnp.take(arrived, where_from, axis=2) * strip_sea.astype(jnp.float32)
    wave_field = wave_field.reshape(freq_here, dirs_local, height, grid_cols)
    freq_index = tile_freq.astype(jnp.float32)
    dir_index = (my_cpl * dirs_local + jnp.arange(dirs_local)).astype(jnp.float32)
    angles = 2.0 * math.pi * (dir_index + 0.5) / dir_count
    dir_cosine = jnp.cos(angles)
    dir_sine = jnp.sin(angles)
    speeds = COURANT_MAX * jnp.power(1.1, -freq_index)
    courant_east = (speeds[:, None] * dir_cosine[None, :])[:, :, None, None]
    courant_north = (speeds[:, None] * dir_sine[None, :])[:, :, None, None]
    strip_mask = strip_sea.astype(jnp.float32).reshape(height, grid_cols)
    last_row = lax.dynamic_slice_in_dim(wave_field, my_height - 1, 1, 2)
    from_above = passed_along(last_row, "pts", 1)
    from_below = passed_along(wave_field[:, :, :1], "pts", -1)
    extended = jnp.concatenate([from_above, wave_field, jnp.zeros_like(from_below)], axis=2)
    extended = lax.dynamic_update_slice_in_dim(extended, from_below, my_height + 1, 2)
    wave_field = upwind(extended, strip_mask, courant_east, courant_north)
    flat_field = wave_field.reshape(freq_here, dirs_local, width_cells)
    strip_start = jnp.take(starts, my_pts)
    inverse = (
        jnp.zeros((width_cells,), jnp.int32)
        .at[jnp.where(strip_sea, strip_map - strip_start, width_cells)]
        .set(jnp.arange(width_cells, dtype=jnp.int32), mode="drop")
    )
    wanted = (strip_first[:, None] + slot_range[None, :]) * owners + jnp.arange(
        owners, dtype=jnp.int32
    )[:, None]
    cells_out = jnp.take(inverse, jnp.clip(wanted - strip_start, 0, width_cells - 1).reshape(-1))
    leaving = jnp.take(flat_field, cells_out, axis=2)
    returned = lax.all_to_all(leaving, "pts", split_axis=2, concat_axis=2, tiled=True)
    slot_index = jnp.arange(slots_local, dtype=jnp.int32)
    points = slot_index * owners + my_pts
    strip_of = jnp.sum((starts[None, 1:] <= points[:, None]).astype(jnp.int32), axis=1)
    offset = slot_index - jnp.take(own_first, strip_of)
    position = strip_of * capacity + offset
    propagated = jnp.take(returned, position, axis=2)
    band_freq = (my_spec * freq_local + jnp.arange(freq_local)).astype(jnp.float32)
    sigma_freq = 2.0 * math.pi * BASE_FREQ * jnp.power(1.1, band_freq)
    phase_speed = GRAVITY / sigma_freq
    slope_weight = jnp.power(1.1, 0.4 * band_freq)
    slope_part = jnp.sum(propagated * slope_weight[:, None, None], axis=(0, 1))
    slope_total = lax.psum(slope_part, ("spec", "cpl")) / (SLOPE_REF * freq_count * dir_count)
    wind_along = (
        wind_deck[0][None, None, :] * dir_cosine[None, :, None]
        + wind_deck[1][None, None, :] * dir_sine[None, :, None]
    )
    growth = (
        GROWTH_RATE
        * sigma_freq[:, None, None]
        * jnp.maximum(wind_along / phase_speed[:, None, None] - 1.0, 0.0)
    )
    sigma_top = 2.0 * math.pi * BASE_FREQ * 1.1 ** (freq_count - 1)
    damping = (sigma_freq / sigma_top)[:, None, None] * (slope_total * slope_total)[None, None, :]
    updated = propagated * jnp.exp(growth - damping)
    lifted = growth * propagated
    drift_part = updated * jnp.power(1.1, 2.0 * (band_freq - (freq_count - 1)))[:, None, None]
    stress_scale = STRESS_GAIN / freq_count
    stokes_scale = STOKES_GAIN / math.sqrt(freq_count * dir_count)
    coupled_part = jnp.stack(
        [
            stress_scale * jnp.sum(lifted * dir_cosine[None, :, None], axis=(0, 1)),
            stress_scale * jnp.sum(lifted * dir_sine[None, :, None], axis=(0, 1)),
            stokes_scale * jnp.sum(drift_part * dir_cosine[None, :, None], axis=(0, 1)),
            stokes_scale * jnp.sum(drift_part * dir_sine[None, :, None], axis=(0, 1)),
        ]
    )
    coupled_total = lax.psum(coupled_part, ("spec", "cpl"))
    coupled_all = lax.all_gather(coupled_total, "pts", axis=1, tiled=True)
    atm_col = atm_order % owners * slots_local + atm_order // owners
    ocean_col = ocean_order % owners * slots_local + ocean_order // owners
    stress_atm = jnp.take(lax.dynamic_slice_in_dim(coupled_all, my_cpl, 1, 0), atm_col, axis=1)
    stokes_ocn = jnp.take(
        lax.dynamic_slice_in_dim(coupled_all, 2 + my_cpl, 1, 0), ocean_col, axis=1
    )
    return (updated, stress_atm, stokes_ocn)


C_KEEP, C_ROW, C_COL, C_SLOPE, C_EAST, C_NORTH, C_ONE, C_DAMP = range(8)
C_S_EAST, C_S_NORTH, C_T_EAST, C_T_NORTH = range(8, 12)
CHUNK_ENDS = (3, 6, 7, 12, 16)
VMEM_BYTES = 24 * 1024 * 1024


def times_hot(value, one_hot, dims, parts=3):
    count = value.shape[0]
    pieces = []
    for _ in range(parts):
        pieces.append(value.astype(BF16).astype(F32))
        value = value - pieces[-1]
    stacked = jnp.concatenate(pieces, axis=0).astype(BF16)
    found = lax.dot_general(stacked, one_hot, (dims, ((), ())), preferred_element_type=F32)
    return sum(found[part * count : (part + 1) * count] for part in range(parts))


def index_kernel(owners, starts, par_ref, cell_ref, coef_ref, g_ref, idx_ref, count_ref, sum_ref, *refs):
    list_refs, chunk_refs = refs[: owners - 2], refs[owners - 2 :]
    slots = g_ref.shape[1]
    blocks = slots // LANES
    half_rows = g_ref.shape[0] // 2
    shift = owners.bit_length() - 1
    pts = par_ref[0]
    number = cell_ref[...].astype(F32)
    sea = number >= 0.0
    first = jnp.min(jnp.where(sea, number, 1e9), axis=1, keepdims=True)
    last = jnp.max(jnp.where(sea, number, -1.0), axis=1, keepdims=True)
    rank = jnp.where(sea, number - first + 1.0, 0.0)
    edge = jnp.full((1, number.shape[1]), -1.0, F32)
    above = jnp.concatenate([edge, number[:-1]], axis=0)
    below = jnp.concatenate([number[1:], edge], axis=0)
    to_above = jnp.where(sea & (above >= 0.0), number - above, 0.0)
    to_below = jnp.where(sea & (below >= 0.0), below - number, 0.0)
    ids = cell_ref[...] & (owners - 1)
    above_ids = above.astype(I32) & (owners - 1)
    crossing = (to_above > 0.0) & (ids != above_ids)
    pair = jnp.where(crossing, above_ids * owners + ids, -1)

    @pl.loop(0, owners * owners)
    def _(which):
        count_ref[pl.ds(which, 1), :] = jnp.sum(
            jnp.where(pair == which, 1.0, 0.0), axis=0, keepdims=True
        )

    cols = number.shape[1]
    column = lax.broadcasted_iota(I32, number.shape, 1)
    left = jnp.where(column == 0, -1.0, pltpu.roll(number, 1, 1))
    right = jnp.where(column == cols - 1, -1.0, pltpu.roll(number, cols - 1, 1))
    beside = jnp.where(par_ref[4] == 0, left, right)
    beside = jnp.where(sea & (beside >= 0.0), 1.0, 0.0)

    slot = lax.broadcasted_iota(I32, (1, slots), 1)
    point = slot * owners + pts
    pointf = point.astype(F32)
    in_row = (first <= pointf) & (pointf <= last)
    row_hot = jnp.where(in_row, 1.0, 0.0).astype(BF16)
    row_first = jnp.sum(jnp.where(in_row, first, 0.0), axis=0, keepdims=True)

    def of_row(values):
        return jnp.dot(
            jnp.transpose(values).astype(BF16), row_hot, preferred_element_type=F32
        )

    here = of_row(rank) == (pointf - row_first + 1.0)

    def of_point(values):
        return jnp.sum(jnp.where(here, of_row(values), 0.0), axis=0, keepdims=True)

    step_above = of_point(to_above).astype(I32)
    step_below = of_point(to_below).astype(I32)
    has_beside = of_point(beside).astype(I32)

    groups = max(8, owners)
    group = lax.broadcasted_iota(I32, (groups, slots), 0)
    codes, masks = [], []
    for half in range(2):
        up = par_ref[1 + half] < 0
        for sends in range(2):
            minus = up if sends == 0 else jnp.logical_not(up)
            step = jnp.where(minus, step_above, step_below)
            other = jnp.where(minus, point - step_above, point + step_below)
            owner = other & (owners - 1)
            away = ((pts - owner) if sends == 0 else (owner - pts)) * par_ref[5]
            away = jnp.where(step > 0, away & (owners - 1), -1)
            codes.append((away, other >> shift))
            masks.append(jnp.where(group == away, 1.0, 0.0))
    mask = jnp.concatenate(masks, axis=0)
    before = jnp.where(
        lax.broadcasted_iota(I32, (LANES, LANES), 0) < lax.broadcasted_iota(I32, (LANES, LANES), 1),
        1.0,
        0.0,
    ).astype(BF16)
    carry = jnp.zeros((mask.shape[0], 1), F32)
    counts = []
    for block in range(blocks):
        part = mask[:, block * LANES : (block + 1) * LANES]
        inside = jnp.dot(part.astype(BF16), before, preferred_element_type=F32)
        counts.append((inside + carry) * part)
        carry = carry + jnp.sum(part, axis=1, keepdims=True)
    counts = jnp.concatenate(counts, axis=1)
    sum_ref[...] = jnp.zeros_like(sum_ref)
    for half in range(2):
        rows = slice(half * half_rows, (half + 1) * half_rows)
        weight = coef_ref[rows, C_SLOPE : C_SLOPE + 1]
        weighted = g_ref[rows, :] * weight
        for at, column_of in ((0, C_KEEP), (1 + half, C_ROW), (3, C_COL)):
            sum_ref[at : at + 1, :] += jnp.sum(
                weighted * coef_ref[rows, column_of : column_of + 1], axis=0, keepdims=True
            )
    entry = lax.broadcasted_iota(I32, (2 * LANES, slots), 0)
    keys = []
    for half in range(2):
        receive, send = [
            jnp.sum(
                counts[(2 * half + sends) * groups : (2 * half + sends + 1) * groups],
                axis=0,
                keepdims=True,
            ).astype(I32)
            for sends in range(2)
        ]
        away, other_slot = codes[2 * half]
        spilled = receive >= LANES
        place = jnp.where(spilled, jnp.maximum(2 * LANES - 1 - receive, 0), receive)
        other_block = jnp.where((other_slot >> 7) == (slot >> 7), 0, 1)
        code = jnp.where(away <= 1, 1 + 2 * away + other_block, 1 + 2 * away + jnp.where(spilled, 1, 0))
        lane = jnp.where(away <= 1, other_slot & (LANES - 1), place)
        idx_ref[2 * half] = jnp.broadcast_to(jnp.where(away < 0, 0, lane), (8, slots))
        idx_ref[2 * half + 1] = jnp.broadcast_to(jnp.where(away < 0, 0, code), (8, slots))
        away, _ = codes[2 * half + 1]
        place = jnp.where(send >= LANES, 3 * LANES - 1 - send, send)
        place = jnp.where(send >= 2 * LANES, -1, place)
        key = jnp.where((away > 1) & (place >= 0), (away - 2) * 2 * LANES + place, -1)
        keys.append(key)
    for at, list_ref in enumerate(list_refs):
        for half in range(2):
            one_hot = jnp.where(entry == keys[half] - at * 2 * LANES, 1.0, 0.0).astype(BF16)
            rows = slice(half * half_rows, (half + 1) * half_rows)
            packed = times_hot(g_ref[rows, :], one_hot, ((1,), (1,)), 2)
            sums = times_hot(sum_ref[...], one_hot, ((1,), (1,)))[1 + half : 2 + half]
            other = slice((1 - half) * half_rows, (2 - half) * half_rows)
            own_row = slice(2 * half_rows + half, 2 * half_rows + half + 1)
            other_row = slice(2 * half_rows + 1 - half, 2 * half_rows + 2 - half)
            if half == 0:
                list_ref[rows, :] = packed[:, :LANES]
                list_ref[other, :] = packed[:, LANES:]
                list_ref[own_row, :] = sums[:, :LANES]
                list_ref[other_row, :] = sums[:, LANES:]
            else:
                list_ref[rows, :] += packed[:, :LANES]
                list_ref[other, :] += packed[:, LANES:]
                list_ref[own_row, :] += sums[:, :LANES]
                list_ref[other_row, :] += sums[:, LANES:]
    chunk_refs[0][-8:, :] = sum_ref[...]
    for start, chunk_ref in zip(starts, chunk_refs):
        count = chunk_ref.shape[0] - (8 if start == starts[0] else 0)
        chunk_ref[:count, :] = g_ref[start : start + count, :]
    for list_ref in list_refs:
        list_ref[2 * half_rows + 2 :, :] = jnp.zeros((6, LANES), F32)
    idx_ref[4] = jnp.broadcast_to(has_beside, (8, slots))


def copy_kernel(in_ref, out_ref):
    out_ref[...] = in_ref[...]


def lane_take(values, lanes):
    return jnp.take_along_axis(values, lanes, axis=1)


def row_neighbour(code, lanes, sources, places=range(4)):
    value = jnp.zeros(code.shape, F32)
    for place, source in zip(places, sources):
        value = jnp.where(code == 1 + place, lane_take(source, lanes), value)
    return value


def near_block(ref, rows, block, step):
    which = jnp.clip(block + step, 0, ref.shape[1] // LANES - 1)
    return ref[rows, pl.ds(pl.multiple_of(which * LANES, LANES), LANES)]


def turned_lanes(turn):
    lane = lax.broadcasted_iota(I32, (8, LANES), 1)
    lanes = (lane + turn) & (LANES - 1)
    return lanes, (lane + turn) != lanes


def slope_kernel(par_ref, idx_ref, sum_ref, beside_ref, *refs):
    list_refs, slope_ref = refs[:-1], refs[-1]
    shape = (8, LANES)
    turn = par_ref[3]
    beside_lanes, beyond = turned_lanes(turn)
    every, last = slice(0, 8), slice(beside_ref.shape[0] - 8, beside_ref.shape[0])
    lists = [ref[-8:, :] for ref in list_refs]
    for block in range(sum_ref.shape[1] // LANES):
        at = slice(block * LANES, (block + 1) * LANES)
        own, beside = sum_ref[:, at], beside_ref[last, at]
        slope = own[0:1]
        for half in range(2):
            lanes, code = idx_ref[2 * half, :, at], idx_ref[2 * half + 1, :, at]
            way = par_ref[1 + half]
            sources = [own, near_block(sum_ref, every, block, way)]
            sources += [beside, near_block(beside_ref, last, block, way)]
            value = row_neighbour(code, lanes, sources)
            slope = slope + value[1 + half : 2 + half]
            code = code - 4
            for values in lists:
                for row in (half, 1 - half):
                    value = jnp.where(code == 1, lane_take(values, lanes), 0.0)
                    slope = slope + value[row : row + 1]
                    code = code - 1
        column = jnp.where(
            beyond,
            lane_take(near_block(beside_ref, last, block, turn), beside_lanes),
            lane_take(beside, beside_lanes),
        )
        slope_ref[:, at] = slope + jnp.where(idx_ref[4, 0:1, at] > 0, column[3:4], 0.0)


def step_kernel(owners, parts, half_rows, chained, final, par_ref, spill_ref, idx_ref, wind_ref, slope_ref, coef_ref, g_ref, *refs):
    beside_refs, refs = refs[: len(parts)], refs[len(parts) :]
    list_refs, refs = refs[: owners - 2], refs[owners - 2 :]
    if chained:
        _, before_ref, refs = refs[0], refs[1], refs[2:]
    out_ref, sums_refs, total_ref, damp_ref = refs[0], refs[1:-2], refs[-2], refs[-1]
    blocks = g_ref.shape[1] // LANES
    shape = (8, LANES)
    step = pl.program_id(0)
    step_rows = out_ref.shape[0]
    first_step = parts[0][0]
    turn = par_ref[3]
    lane = lax.broadcasted_iota(I32, shape, 1)
    turned = (lane + turn) & (LANES - 1)
    edge = lane == jnp.where(turn < 0, LANES - 1, jnp.where(turn > 0, 0, -1))

    @pl.when(step == 0)
    def _():
        total_ref[...] = jnp.zeros_like(total_ref)
        slope = slope_ref[...]
        damp_ref[...] = jnp.broadcast_to(slope * slope, damp_ref.shape)

    def tiles(beside_ref, spills):
        for tile in range(step_rows // 8):
            here = slice(tile * 8, tile * 8 + 8)

            def at_row(first):
                return pl.ds(pl.multiple_of(first, 8), 8)

            first = (step + first_step) * step_rows + tile * 8
            half = jnp.where(first >= half_rows, 1, 0)
            way = par_ref[1 + half]
            rows = at_row(first)
            other_rows = at_row(first + (1 - 2 * half) * half_rows)
            coef = coef_ref[rows, :]

            def factor(at):
                return jnp.broadcast_to(coef[:, at : at + 1], shape)

            keep, by_row, by_col = factor(C_KEEP), factor(C_ROW), factor(C_COL)
            east, north, one, damp = factor(C_EAST), factor(C_NORTH), factor(C_ONE), factor(C_DAMP)
            s_east, s_north = factor(C_S_EAST), factor(C_S_NORTH)
            t_east, t_north = factor(C_T_EAST), factor(C_T_NORTH)
            sides = (rows, other_rows) if spills else (rows,)
            lists = [ref[which, :] for ref in list_refs for which in sides]
            places = list(range(4))
            places += [4 + 2 * at + side for at in range(owners - 2) for side in range(len(sides))]
            for block in range(blocks):
                at = slice(block * LANES, (block + 1) * LANES)
                lanes, code = idx_ref[2 * half, :, at], idx_ref[2 * half + 1, :, at]
                has_beside = idx_ref[4, :, at]
                own, beside = g_ref[here, at], beside_ref[here, at]
                sources = [own, near_block(g_ref, here, block, way)]
                sources += [beside, near_block(beside_ref, here, block, way)]
                row_value = row_neighbour(code, lanes, sources + lists, places)
                turning = near_block(beside_ref, here, block, turn)
                col_value = lane_take(jnp.where(edge, turning, beside), turned)
                col_value = jnp.where(has_beside > 0, col_value, 0.0)
                value = keep * own + by_row * row_value + by_col * col_value
                wind_east = jnp.broadcast_to(wind_ref[0:1, at], shape)
                wind_north = jnp.broadcast_to(wind_ref[1:2, at], shape)
                growth = jnp.maximum(east * wind_east + north * wind_north - one, 0.0)
                updated = value * jnp.exp(growth - damp * damp_ref[:, at])
                out_ref[here, at] = updated
                lifted = growth * value
                total_ref[0, :, at] += s_east * lifted
                total_ref[1, :, at] += s_north * lifted
                total_ref[2, :, at] += t_east * updated
                total_ref[3, :, at] += t_north * updated

    for (start, stop), beside_ref in zip(parts, beside_refs):
        for spills in (False, True):
            inside = (step >= start - first_step) & (step < stop - first_step)

            @pl.when(inside & ((spill_ref[0] > 0) == spills))
            def _():
                tiles(beside_ref, spills)

    @pl.when(step == pl.num_programs(0) - 1)
    def _():
        cpl = par_ref[4]
        for item in range(2):
            for block in range(blocks):
                at = slice(block * LANES, (block + 1) * LANES)
                pair = []
                for part in range(2):
                    value = jnp.sum(total_ref[2 * item + part, :, at], axis=0, keepdims=True)
                    if chained:
                        value = value + before_ref[2 * item + part, block : block + 1, :]
                    pair.append(value)
                where = slice(block, block + 1)
                if final:
                    sums_refs[0][item, where, :] = jnp.where(cpl == 0, pair[0], pair[1])
                    sums_refs[1][item, where, :] = jnp.where(cpl == 0, pair[1], pair[0])
                else:
                    sums_refs[0][2 * item, where, :] = pair[0]
                    sums_refs[0][2 * item + 1, where, :] = pair[1]


def pick_kernel(owners, atm_ref, ocean_ref, *refs):
    table_refs, (stress_ref, stokes_ref) = refs[:owners], refs[owners:]
    shift = owners.bit_length() - 1
    blocks = table_refs[0].shape[1]
    for item, (order_ref, out_ref) in enumerate(((atm_ref, stress_ref), (ocean_ref, stokes_ref))):
        point = order_ref[...]
        count = point.shape[1]
        slot = point >> shift
        row = (point & (owners - 1)) * blocks + (slot >> 7)
        lane = slot & (LANES - 1)
        rows = owners * blocks
        hot = jnp.where(lax.broadcasted_iota(I32, (rows, count), 0) == row, 1.0, 0.0).astype(BF16)
        table = jnp.concatenate([ref[item] for ref in table_refs], axis=0)
        table = jnp.transpose(table)
        found = times_hot(table, hot, ((1,), (0,)))
        pick = lax.broadcasted_iota(I32, (LANES, count), 0) == lane
        out_ref[...] = jnp.sum(jnp.where(pick, found, 0.0), axis=0, keepdims=True)


def coefficients(freq_local, dirs_local, pad_half, my_spec, my_cpl, freq_count, dir_count):
    freq = (my_spec * freq_local + jnp.arange(freq_local)).astype(F32)
    direction = (my_cpl * dirs_local + jnp.arange(dirs_local)).astype(F32)
    angles = 2.0 * math.pi * (direction + 0.5) / dir_count
    cosine, sine = jnp.cos(angles)[:, None], jnp.sin(angles)[:, None]
    speed = COURANT_MAX * jnp.power(1.1, -freq)[None, :]
    by_row, by_col = jnp.abs(speed * cosine), jnp.abs(speed * sine)
    sigma = (2.0 * math.pi * BASE_FREQ * jnp.power(1.1, freq))[None, :]
    sigma_top = 2.0 * math.pi * BASE_FREQ * 1.1 ** (freq_count - 1)
    inverse_speed = sigma / GRAVITY
    rate = GROWTH_RATE * sigma
    drift = jnp.power(1.1, 2.0 * (freq - (freq_count - 1)))[None, :]
    stress_scale = STRESS_GAIN / freq_count
    stokes_scale = STOKES_GAIN / math.sqrt(freq_count * dir_count)
    shape = (dirs_local, freq_local)
    columns = [
        1.0 - by_row - by_col,
        by_row,
        by_col,
        jnp.power(1.1, 0.4 * freq)[None, :] / (SLOPE_REF * freq_count * dir_count),
        rate * inverse_speed * cosine,
        rate * inverse_speed * sine,
        rate,
        sigma / sigma_top,
        stress_scale * cosine,
        stress_scale * sine,
        stokes_scale * drift * cosine,
        stokes_scale * drift * sine,
    ]
    table = jnp.stack([jnp.broadcast_to(column, shape) for column in columns], axis=-1)
    table = table.reshape(2, -1, len(columns))
    table = jnp.pad(table, ((0, 0), (0, pad_half), (0, 16 - len(columns))))
    return table.reshape(-1, 16)


def shape_of(*dims, kind=F32):
    return jax.ShapeDtypeStruct(dims, kind)


def call(kernel, inputs, outputs):
    return pl.pallas_call(
        kernel,
        in_specs=inputs,
        out_specs=[WHOLE] * len(outputs),
        out_shape=outputs,
        compiler_params=pltpu.CompilerParams(vmem_limit_bytes=VMEM_BYTES),
        cost_estimate=SHORT,
    )


def chunks_of(steps):
    ends = sorted({max(1, steps * part // 18) for part in CHUNK_ENDS} | {steps})
    return list(zip([0] + ends[:-1], ends))


def local(spec_deck, wind_deck, cell_sea, atm_order, ocean_order):
    owners = lax.axis_size("pts")
    spec_groups = lax.axis_size("spec")
    cpl_groups = lax.axis_size("cpl")
    groups = lax.axis_size("grp")
    my_pts = lax.axis_index("pts")
    my_spec = lax.axis_index("spec")
    my_cpl = lax.axis_index("cpl")
    assert cpl_groups == 2 and owners & (owners - 1) == 0
    freq_local, dirs_local, slots = spec_deck.shape
    freq_count = freq_local * spec_groups
    dir_count = dirs_local * cpl_groups
    blocks = slots // LANES
    half_rows = freq_local * dirs_local // 2
    pad_half = -half_rows % 8
    rows = 2 * (half_rows + pad_half)
    step_rows = 16 if (half_rows + pad_half) % 16 == 0 else 8
    steps = rows // step_rows

    field = jnp.transpose(spec_deck, (1, 0, 2)).reshape(2, half_rows, slots)
    if pad_half:
        field = jnp.pad(field, ((0, 0), (0, pad_half), (0, 0)))
    field = field.reshape(rows, slots)

    def around(values, distance=1):
        pairs = []
        for owner in range(owners):
            pairs.append((owner * 2, (owner + distance) % owners * 2))
            pairs.append((owner * 2 + 1, (owner - distance) % owners * 2 + 1))
        return lax.ppermute(values, ("pts", "cpl"), pairs)

    def chunk(values, at):
        return values[at[0] * step_rows : at[1] * step_rows]

    chunks = chunks_of(steps)
    def cut(values, at):
        size = (at[1] - at[0]) * step_rows
        if at[0] * step_rows % size:
            return chunk(values, at)
        return pl.pallas_call(
            copy_kernel,
            grid=(1,),
            in_specs=[pl.BlockSpec((size, slots), lambda i: (at[0] * step_rows // size, 0))],
            out_specs=WHOLE,
            out_shape=shape_of(size, slots),
            compiler_params=pltpu.CompilerParams(vmem_limit_bytes=VMEM_BYTES),
            cost_estimate=SHORT,
        )(values)

    first = cut(field, chunks[0])
    rest, first = lax.optimization_barrier((field, first))
    beside = [around(first), around(cut(rest, chunks[1]))]

    first_way = 2 * my_cpl - 1
    turn = jnp.where(
        (my_cpl == 0) & (my_pts == 0), -1, jnp.where((my_cpl == 1) & (my_pts == owners - 1), 1, 0)
    )
    par = jnp.stack([my_pts, first_way, -first_way, turn, my_cpl, -first_way]).astype(I32)
    coef = coefficients(
        freq_local, dirs_local, pad_half, my_spec, my_cpl, freq_count, dir_count
    )

    found = call(
        functools.partial(index_kernel, owners, [start * step_rows for start, _ in chunks[2:]]),
        [SCALARS, WHOLE, WHOLE, WHOLE],
        [
            shape_of(5, 8, slots, kind=I32),
            shape_of(owners * owners, cell_sea.shape[1]),
            shape_of(8, slots),
        ]
        + [shape_of(rows + 8, LANES)] * (owners - 2)
        + [
            shape_of((stop - start) * step_rows + (8 if at == 0 else 0), slots)
            for at, (start, stop) in enumerate(chunks[2:])
        ],
    )(par, cell_sea, coef, field)
    found, beside[0] = lax.optimization_barrier((found, beside[0]))
    (idx, counts, row_sums), lists = found[:3], found[3 : owners + 1]
    leaving = found[owners + 1 :]
    arrived = [around(values, 2 + at) for at, values in enumerate(lists)]
    pairs = jnp.sum(counts, axis=1).reshape(owners, owners)
    spills = jnp.where(jnp.max(pairs) > LANES, 1, 0).astype(I32).reshape(1)
    longest = jnp.max(pairs + pairs.T).reshape(1, 1)
    if groups == 2:
        longest = jnp.maximum(longest, lax.ppermute(longest, "grp", [(0, 1), (1, 0)]))
    else:
        longest = lax.pmax(longest, "grp")
    beside.append(around(leaving[0]))
    later = list(leaving[1:])
    later[0], beside[1] = lax.optimization_barrier((later[0], beside[1]))
    beside.append(around(later.pop(0)))
    later, arrived, beside[2], longest, spills = lax.optimization_barrier(
        (later, arrived, beside[2], longest, spills)
    )
    beside += [around(values) for values in later]

    (slope_part,) = call(
        slope_kernel, [SCALARS] + [WHOLE] * (owners + 1), [shape_of(1, slots)]
    )(par, idx, row_sums, beside[2], *arrived)

    slope = slope_part + lax.ppermute(slope_part, "cpl", [(0, 1), (1, 0)])
    if spec_groups == 2:
        slope = slope + lax.ppermute(slope, "spec", [(0, 1), (1, 0)])
    else:
        slope = lax.psum(slope, "spec")

    updated = sums = None
    for parts in [chunks[:3]] + [[at] for at in chunks[3:]]:
        ends = [(first * step_rows, end * step_rows) for first, end in parts]
        final = ends[-1][1] == rows
        block_rows = step_rows
        while all(end % (2 * block_rows) == 0 for part in ends for end in part) and block_rows < 32:
            block_rows *= 2
        parts = [(first // block_rows, end // block_rows) for first, end in ends]
        start, stop = parts[0][0], parts[-1][1]
        chained = start > 0
        in_rows = pl.BlockSpec(
            (block_rows, slots), functools.partial(lambda first, i: (first + i, 0), start)
        )
        near, beside = beside[: len(parts)], beside[len(parts) :]
        inputs = [par, spills, idx, wind_deck, slope, coef, field, *near, *arrived]
        specs = [SCALARS] * 2 + [WHOLE] * 4 + [in_rows]
        for first, end in parts:
            within = lambda skipped, most, i: (jnp.clip(i - skipped, 0, most), 0)
            within = functools.partial(within, first - start, end - first - 1)
            specs.append(pl.BlockSpec((block_rows, slots), within))
        specs += [WHOLE] * len(arrived)
        aliases = {}
        if chained:
            aliases = {len(inputs): 0}
            inputs += [updated, sums]
            specs += [pl.BlockSpec(memory_space=pl.ANY), WHOLE]
        sum_shapes = [(2, blocks, LANES)] * 2 if final else [(4, blocks, LANES)]
        updated, *sums = pl.pallas_call(
            functools.partial(step_kernel, owners, parts, rows // 2, chained, final),
            grid=(stop - start,),
            in_specs=specs,
            out_specs=[in_rows] + [WHOLE] * len(sum_shapes),
            out_shape=[pltpu.HBM((rows, slots), F32)] + [shape_of(*dims) for dims in sum_shapes],
            scratch_shapes=[pltpu.VMEM((4, 8, slots), F32), pltpu.VMEM((8, slots), F32)],
            input_output_aliases=aliases,
            compiler_params=pltpu.CompilerParams(vmem_limit_bytes=VMEM_BYTES),
            cost_estimate=SHORT,
        )(*inputs)
        if not final:
            sums = sums[0]

    mine, others = sums
    if spec_groups == 2:
        peers = spec_groups * cpl_groups
        mine = sum(
            lax.ppermute(values, ("spec", "cpl"), [(i, i ^ turned) for i in range(peers)])
            for values, turned in ((mine, 2), (others, 3), (others, 1))
        ) + mine
    else:
        mine = lax.psum(mine + lax.ppermute(others, "cpl", [(0, 1), (1, 0)]), "spec")
    if owners == 4:
        tables = [mine] + [
            lax.ppermute(mine, "pts", [(i, i ^ turned) for i in range(owners)])
            for turned in range(1, owners)
        ]
        looked = lambda order: (order ^ my_pts)[None, :]
    else:
        gathered = lax.all_gather(mine, "pts", axis=0)
        tables = [gathered[owner] for owner in range(owners)]
        looked = lambda order: order[None, :]
    count = atm_order.shape[0]
    stress_atm, stokes_ocn = call(
        functools.partial(pick_kernel, owners),
        [WHOLE] * (2 + owners),
        [shape_of(1, count)] * 2,
    )(looked(atm_order), looked(ocean_order), *tables)

    def by_direction(values):
        return jnp.transpose(values, (1, 0, 2)).reshape(dirs_local * freq_local, slots)

    def general_way():
        spectra, stress, stokes = general(spec_deck, wind_deck, cell_sea, atm_order, ocean_order)
        return by_direction(spectra), stress, stokes

    if pad_half:
        updated = updated.reshape(2, half_rows + pad_half, slots)[:, :half_rows]
        updated = updated.reshape(2 * half_rows, slots)
    updated, stress_atm, stokes_ocn = lax.cond(
        longest[0, 0] > 2 * LANES, general_way, lambda: (updated, stress_atm, stokes_ocn)
    )
    updated = jnp.transpose(updated.reshape(dirs_local, freq_local, slots), (1, 0, 2))
    return updated, stress_atm, stokes_ocn


def solution(mesh):
    return jax.shard_map(
        local,
        mesh=mesh,
        in_specs=(
            P("spec", "cpl", ("grp", "pts")),
            P(None, ("grp", "pts")),
            P("grp", None),
            P(("grp", "pts", "spec")),
            P(("grp", "pts", "spec")),
        ),
        out_specs=(
            P("spec", "cpl", ("grp", "pts")),
            P("cpl", ("grp", "pts", "spec")),
            P("cpl", ("grp", "pts", "spec")),
        ),
        check_vma=False,
    )
```

```python
import functools
import math

import jax
import jax.numpy as jnp
from jax import lax
from jax.experimental import pallas as pl
from jax.experimental.pallas import tpu as pltpu
from jax.sharding import PartitionSpec as P

COURANT_MAX = 0.68
BASE_FREQ = 0.035
GRAVITY = 9.81
GROWTH_RATE = 0.02
SLOPE_REF = 0.09
STRESS_GAIN = 64.0
STOKES_GAIN = 64.0
LANES = 128
F32 = jnp.float32
BF16 = jnp.bfloat16
I32 = jnp.int32
WHOLE = pl.BlockSpec(memory_space=pltpu.VMEM)
SHORT = pl.CostEstimate(flops=1000, bytes_accessed=1000, transcendentals=0)
SCALARS = pl.BlockSpec(memory_space=pltpu.SMEM)


def passed_along(shard, axis, by):
    devices = lax.axis_size(axis)
    pairs = [(i, i + by) for i in range(devices) if 0 <= i + by < devices]
    return lax.ppermute(shard, axis, pairs)


def upwind(extended, mask_rows, courant_east, courant_north):
    middle = extended[:, :, 1:-1]
    prior_row = extended[:, :, :-2]
    next_row = extended[:, :, 2:]
    side_pad = jnp.pad(middle, ((0, 0), (0, 0), (0, 0), (1, 1)))
    prior_col = side_pad[..., :-2]
    next_col = side_pad[..., 2:]
    advanced = (
        middle
        - jnp.maximum(courant_east, 0.0) * (middle - prior_row)
        - jnp.maximum(-courant_east, 0.0) * (middle - next_row)
        - jnp.maximum(courant_north, 0.0) * (middle - prior_col)
        - jnp.maximum(-courant_north, 0.0) * (middle - next_col)
    )
    return advanced * mask_rows


def general(spec_deck, wind_deck, cell_sea, atm_order, ocean_order):
    owners = lax.axis_size("pts")
    spec_groups = lax.axis_size("spec")
    cpl_groups = lax.axis_size("cpl")
    my_pts = lax.axis_index("pts")
    my_spec = lax.axis_index("spec")
    my_cpl = lax.axis_index("cpl")
    freq_local, dirs_local, slots_local = spec_deck.shape
    grid_rows, grid_cols = cell_sea.shape
    freq_count = freq_local * spec_groups
    dir_count = dirs_local * cpl_groups
    sea_mask = cell_sea >= 0
    row_counts = jnp.sum(sea_mask.astype(jnp.int32), axis=1)
    before_row = jnp.concatenate([jnp.zeros((1,), jnp.int32), jnp.cumsum(row_counts)])
    tile_freq = my_spec * freq_local + jnp.arange(freq_local)
    height = 2 * (grid_rows // owners)
    capacity = (slots_local + grid_cols) // owners + 1
    targets = jnp.arange(owners + 1, dtype=jnp.int32) * slots_local
    row_starts = jnp.sum((before_row[None, :] < targets[:, None]).astype(jnp.int32), axis=1)
    width_cells = height * grid_cols
    bounds = jnp.take(before_row, row_starts)
    starts = bounds[:-1]
    my_row = jnp.take(row_starts, my_pts)
    my_height = jnp.take(row_starts, my_pts + 1) - my_row
    first_slot = -((jnp.arange(owners, dtype=jnp.int32)[None, :] - starts[:, None]) // owners)
    slot_range = jnp.arange(capacity, dtype=jnp.int32)
    own_first = jnp.take(first_slot, my_pts, axis=1)
    picked = jnp.clip(own_first[:, None] + slot_range[None, :], 0, slots_local - 1).reshape(-1)
    outgoing = jnp.take(spec_deck, picked, axis=2)
    arrived = lax.all_to_all(outgoing, "pts", split_axis=2, concat_axis=2, tiled=True)
    freq_here = arrived.shape[0]
    padded_map = jnp.concatenate([cell_sea, jnp.full((height, grid_cols), -1, jnp.int32)], axis=0)
    strip_map = lax.dynamic_slice_in_dim(padded_map, my_row, height, 0)
    row_valid = jnp.arange(height) < my_height
    strip_sea = ((strip_map >= 0) & row_valid[:, None]).reshape(-1)
    strip_map = strip_map.reshape(-1)
    safe_index = jnp.maximum(strip_map, 0)
    source = safe_index % owners
    strip_first = jnp.take(first_slot, my_pts, axis=0)
    where_from = jnp.where(
        strip_sea, source * capacity + safe_index // owners - jnp.take(strip_first, source), 0
    )
    wave_field = jnp.take(arrived, where_from, axis=2) * strip_sea.astype(jnp.float32)
    wave_field = wave_field.reshape(freq_here, dirs_local, height, grid_cols)
    freq_index = tile_freq.astype(jnp.float32)
    dir_index = (my_cpl * dirs_local + jnp.arange(dirs_local)).astype(jnp.float32)
    angles = 2.0 * math.pi * (dir_index + 0.5) / dir_count
    dir_cosine = jnp.cos(angles)
    dir_sine = jnp.sin(angles)
    speeds = COURANT_MAX * jnp.power(1.1, -freq_index)
    courant_east = (speeds[:, None] * dir_cosine[None, :])[:, :, None, None]
    courant_north = (speeds[:, None] * dir_sine[None, :])[:, :, None, None]
    strip_mask = strip_sea.astype(jnp.float32).reshape(height, grid_cols)
    last_row = lax.dynamic_slice_in_dim(wave_field, my_height - 1, 1, 2)
    from_above = passed_along(last_row, "pts", 1)
    from_below = passed_along(wave_field[:, :, :1], "pts", -1)
    extended = jnp.concatenate([from_above, wave_field, jnp.zeros_like(from_below)], axis=2)
    extended = lax.dynamic_update_slice_in_dim(extended, from_below, my_height + 1, 2)
    wave_field = upwind(extended, strip_mask, courant_east, courant_north)
    flat_field = wave_field.reshape(freq_here, dirs_local, width_cells)
    strip_start = jnp.take(starts, my_pts)
    inverse = (
        jnp.zeros((width_cells,), jnp.int32)
        .at[jnp.where(strip_sea, strip_map - strip_start, width_cells)]
        .set(jnp.arange(width_cells, dtype=jnp.int32), mode="drop")
    )
    wanted = (strip_first[:, None] + slot_range[None, :]) * owners + jnp.arange(
        owners, dtype=jnp.int32
    )[:, None]
    cells_out = jnp.take(inverse, jnp.clip(wanted - strip_start, 0, width_cells - 1).reshape(-1))
    leaving = jnp.take(flat_field, cells_out, axis=2)
    returned = lax.all_to_all(leaving, "pts", split_axis=2, concat_axis=2, tiled=True)
    slot_index = jnp.arange(slots_local, dtype=jnp.int32)
    points = slot_index * owners + my_pts
    strip_of = jnp.sum((starts[None, 1:] <= points[:, None]).astype(jnp.int32), axis=1)
    offset = slot_index - jnp.take(own_first, strip_of)
    position = strip_of * capacity + offset
    propagated = jnp.take(returned, position, axis=2)
    band_freq = (my_spec * freq_local + jnp.arange(freq_local)).astype(jnp.float32)
    sigma_freq = 2.0 * math.pi * BASE_FREQ * jnp.power(1.1, band_freq)
    phase_speed = GRAVITY / sigma_freq
    slope_weight = jnp.power(1.1, 0.4 * band_freq)
    slope_part = jnp.sum(propagated * slope_weight[:, None, None], axis=(0, 1))
    slope_total = lax.psum(slope_part, ("spec", "cpl")) / (SLOPE_REF * freq_count * dir_count)
    wind_along = (
        wind_deck[0][None, None, :] * dir_cosine[None, :, None]
        + wind_deck[1][None, None, :] * dir_sine[None, :, None]
    )
    growth = (
        GROWTH_RATE
        * sigma_freq[:, None, None]
        * jnp.maximum(wind_along / phase_speed[:, None, None] - 1.0, 0.0)
    )
    sigma_top = 2.0 * math.pi * BASE_FREQ * 1.1 ** (freq_count - 1)
    damping = (sigma_freq / sigma_top)[:, None, None] * (slope_total * slope_total)[None, None, :]
    updated = propagated * jnp.exp(growth - damping)
    lifted = growth * propagated
    drift_part = updated * jnp.power(1.1, 2.0 * (band_freq - (freq_count - 1)))[:, None, None]
    stress_scale = STRESS_GAIN / freq_count
    stokes_scale = STOKES_GAIN / math.sqrt(freq_count * dir_count)
    coupled_part = jnp.stack(
        [
            stress_scale * jnp.sum(lifted * dir_cosine[None, :, None], axis=(0, 1)),
            stress_scale * jnp.sum(lifted * dir_sine[None, :, None], axis=(0, 1)),
            stokes_scale * jnp.sum(drift_part * dir_cosine[None, :, None], axis=(0, 1)),
            stokes_scale * jnp.sum(drift_part * dir_sine[None, :, None], axis=(0, 1)),
        ]
    )
    coupled_total = lax.psum(coupled_part, ("spec", "cpl"))
    coupled_all = lax.all_gather(coupled_total, "pts", axis=1, tiled=True)
    atm_col = atm_order % owners * slots_local + atm_order // owners
    ocean_col = ocean_order % owners * slots_local + ocean_order // owners
    stress_atm = jnp.take(lax.dynamic_slice_in_dim(coupled_all, my_cpl, 1, 0), atm_col, axis=1)
    stokes_ocn = jnp.take(
        lax.dynamic_slice_in_dim(coupled_all, 2 + my_cpl, 1, 0), ocean_col, axis=1
    )
    return (updated, stress_atm, stokes_ocn)


C_KEEP, C_ROW, C_COL, C_SLOPE, C_EAST, C_NORTH, C_ONE, C_DAMP = range(8)
C_S_EAST, C_S_NORTH, C_T_EAST, C_T_NORTH = range(8, 12)
CHUNK_ENDS = (2, 6, 8, 12, 16)
VMEM_BYTES = 24 * 1024 * 1024


def times_hot(value, one_hot, dims, parts=3):
    count = value.shape[0]
    pieces = []
    for _ in range(parts):
        pieces.append(value.astype(BF16).astype(F32))
        value = value - pieces[-1]
    stacked = jnp.concatenate(pieces, axis=0).astype(BF16)
    found = lax.dot_general(stacked, one_hot, (dims, ((), ())), preferred_element_type=F32)
    return sum(found[part * count : (part + 1) * count] for part in range(parts))


def index_kernel(owners, starts, par_ref, cell_ref, coef_ref, g_ref, idx_ref, count_ref, sum_ref, *refs):
    list_refs, chunk_refs = refs[: owners - 2], refs[owners - 2 :]
    slots = g_ref.shape[1]
    blocks = slots // LANES
    half_rows = g_ref.shape[0] // 2
    shift = owners.bit_length() - 1
    pts = par_ref[0]
    number = cell_ref[...].astype(F32)
    sea = number >= 0.0
    first = jnp.min(jnp.where(sea, number, 1e9), axis=1, keepdims=True)
    last = jnp.max(jnp.where(sea, number, -1.0), axis=1, keepdims=True)
    rank = jnp.where(sea, number - first + 1.0, 0.0)
    edge = jnp.full((1, number.shape[1]), -1.0, F32)
    above = jnp.concatenate([edge, number[:-1]], axis=0)
    below = jnp.concatenate([number[1:], edge], axis=0)
    to_above = jnp.where(sea & (above >= 0.0), number - above, 0.0)
    to_below = jnp.where(sea & (below >= 0.0), below - number, 0.0)
    ids = cell_ref[...] & (owners - 1)
    above_ids = above.astype(I32) & (owners - 1)
    crossing = (to_above > 0.0) & (ids != above_ids)
    pair = jnp.where(crossing, above_ids * owners + ids, -1)

    @pl.loop(0, owners * owners)
    def _(which):
        count_ref[pl.ds(which, 1), :] = jnp.sum(
            jnp.where(pair == which, 1.0, 0.0), axis=0, keepdims=True
        )

    cols = number.shape[1]
    column = lax.broadcasted_iota(I32, number.shape, 1)
    left = jnp.where(column == 0, -1.0, pltpu.roll(number, 1, 1))
    right = jnp.where(column == cols - 1, -1.0, pltpu.roll(number, cols - 1, 1))
    beside = jnp.where(par_ref[4] == 0, left, right)
    beside = jnp.where(sea & (beside >= 0.0), 1.0, 0.0)

    slot = lax.broadcasted_iota(I32, (1, slots), 1)
    point = slot * owners + pts
    pointf = point.astype(F32)
    in_row = (first <= pointf) & (pointf <= last)
    row_hot = jnp.where(in_row, 1.0, 0.0).astype(BF16)
    row_first = jnp.sum(jnp.where(in_row, first, 0.0), axis=0, keepdims=True)

    def of_row(values):
        return jnp.dot(
            jnp.transpose(values).astype(BF16), row_hot, preferred_element_type=F32
        )

    here = of_row(rank) == (pointf - row_first + 1.0)

    def of_point(values):
        return jnp.sum(jnp.where(here, of_row(values), 0.0), axis=0, keepdims=True)

    step_above = of_point(to_above).astype(I32)
    step_below = of_point(to_below).astype(I32)
    has_beside = of_point(beside).astype(I32)

    groups = max(8, owners)
    group = lax.broadcasted_iota(I32, (groups, slots), 0)
    codes, masks = [], []
    for half in range(2):
        up = par_ref[1 + half] < 0
        for sends in range(2):
            minus = up if sends == 0 else jnp.logical_not(up)
            step = jnp.where(minus, step_above, step_below)
            other = jnp.where(minus, point - step_above, point + step_below)
            owner = other & (owners - 1)
            away = ((pts - owner) if sends == 0 else (owner - pts)) * par_ref[5]
            away = jnp.where(step > 0, away & (owners - 1), -1)
            codes.append((away, other >> shift))
            masks.append(jnp.where(group == away, 1.0, 0.0))
    mask = jnp.concatenate(masks, axis=0)
    before = jnp.where(
        lax.broadcasted_iota(I32, (LANES, LANES), 0) < lax.broadcasted_iota(I32, (LANES, LANES), 1),
        1.0,
        0.0,
    ).astype(BF16)
    carry = jnp.zeros((mask.shape[0], 1), F32)
    counts = []
    for block in range(blocks):
        part = mask[:, block * LANES : (block + 1) * LANES]
        inside = jnp.dot(part.astype(BF16), before, preferred_element_type=F32)
        counts.append((inside + carry) * part)
        carry = carry + jnp.sum(part, axis=1, keepdims=True)
    counts = jnp.concatenate(counts, axis=1)
    sum_ref[...] = jnp.zeros_like(sum_ref)
    for half in range(2):
        rows = slice(half * half_rows, (half + 1) * half_rows)
        weight = coef_ref[rows, C_SLOPE : C_SLOPE + 1]
        weighted = g_ref[rows, :] * weight
        for at, column_of in ((0, C_KEEP), (1 + half, C_ROW), (3, C_COL)):
            sum_ref[at : at + 1, :] += jnp.sum(
                weighted * coef_ref[rows, column_of : column_of + 1], axis=0, keepdims=True
            )
    entry = lax.broadcasted_iota(I32, (2 * LANES, slots), 0)
    keys = []
    for half in range(2):
        receive, send = [
            jnp.sum(
                counts[(2 * half + sends) * groups : (2 * half + sends + 1) * groups],
                axis=0,
                keepdims=True,
            ).astype(I32)
            for sends in range(2)
        ]
        away, other_slot = codes[2 * half]
        spilled = receive >= LANES
        place = jnp.where(spilled, jnp.maximum(2 * LANES - 1 - receive, 0), receive)
        other_block = jnp.where((other_slot >> 7) == (slot >> 7), 0, 1)
        code = jnp.where(away <= 1, 1 + 2 * away + other_block, 1 + 2 * away + jnp.where(spilled, 1, 0))
        lane = jnp.where(away <= 1, other_slot & (LANES - 1), place)
        idx_ref[2 * half] = jnp.broadcast_to(jnp.where(away < 0, 0, lane), (8, slots))
        idx_ref[2 * half + 1] = jnp.broadcast_to(jnp.where(away < 0, 0, code), (8, slots))
        away, _ = codes[2 * half + 1]
        place = jnp.where(send >= LANES, 3 * LANES - 1 - send, send)
        place = jnp.where(send >= 2 * LANES, -1, place)
        key = jnp.where((away > 1) & (place >= 0), (away - 2) * 2 * LANES + place, -1)
        keys.append(key)
    for at, list_ref in enumerate(list_refs):
        for half in range(2):
            one_hot = jnp.where(entry == keys[half] - at * 2 * LANES, 1.0, 0.0).astype(BF16)
            rows = slice(half * half_rows, (half + 1) * half_rows)
            packed = times_hot(g_ref[rows, :], one_hot, ((1,), (1,)), 2)
            sums = times_hot(sum_ref[...], one_hot, ((1,), (1,)))[1 + half : 2 + half]
            other = slice((1 - half) * half_rows, (2 - half) * half_rows)
            own_row = slice(2 * half_rows + half, 2 * half_rows + half + 1)
            other_row = slice(2 * half_rows + 1 - half, 2 * half_rows + 2 - half)
            if half == 0:
                list_ref[rows, :] = packed[:, :LANES]
                list_ref[other, :] = packed[:, LANES:]
                list_ref[own_row, :] = sums[:, :LANES]
                list_ref[other_row, :] = sums[:, LANES:]
            else:
                list_ref[rows, :] += packed[:, :LANES]
                list_ref[other, :] += packed[:, LANES:]
                list_ref[own_row, :] += sums[:, :LANES]
                list_ref[other_row, :] += sums[:, LANES:]
    chunk_refs[0][-8:, :] = sum_ref[...]
    for start, chunk_ref in zip(starts, chunk_refs):
        count = chunk_ref.shape[0] - (8 if start == starts[0] else 0)
        chunk_ref[:count, :] = g_ref[start : start + count, :]
    for list_ref in list_refs:
        list_ref[2 * half_rows + 2 :, :] = jnp.zeros((6, LANES), F32)
    idx_ref[4] = jnp.broadcast_to(has_beside, (8, slots))


def copy_kernel(in_ref, out_ref):
    out_ref[...] = in_ref[...]


def lane_take(values, lanes):
    return jnp.take_along_axis(values, lanes, axis=1)


def row_neighbour(code, lanes, sources, places=range(4)):
    value = jnp.zeros(code.shape, F32)
    for place, source in zip(places, sources):
        value = jnp.where(code == 1 + place, lane_take(source, lanes), value)
    return value


def near_block(ref, rows, block, step):
    which = jnp.clip(block + step, 0, ref.shape[1] // LANES - 1)
    return ref[rows, pl.ds(pl.multiple_of(which * LANES, LANES), LANES)]


def turned_lanes(turn):
    lane = lax.broadcasted_iota(I32, (8, LANES), 1)
    lanes = (lane + turn) & (LANES - 1)
    return lanes, (lane + turn) != lanes


def slope_kernel(par_ref, idx_ref, sum_ref, beside_ref, *refs):
    list_refs, slope_ref = refs[:-1], refs[-1]
    shape = (8, LANES)
    turn = par_ref[3]
    beside_lanes, beyond = turned_lanes(turn)
    every, last = slice(0, 8), slice(beside_ref.shape[0] - 8, beside_ref.shape[0])
    lists = [ref[-8:, :] for ref in list_refs]
    for block in range(sum_ref.shape[1] // LANES):
        at = slice(block * LANES, (block + 1) * LANES)
        own, beside = sum_ref[:, at], beside_ref[last, at]
        slope = own[0:1]
        for half in range(2):
            lanes, code = idx_ref[2 * half, :, at], idx_ref[2 * half + 1, :, at]
            way = par_ref[1 + half]
            sources = [own, near_block(sum_ref, every, block, way)]
            sources += [beside, near_block(beside_ref, last, block, way)]
            value = row_neighbour(code, lanes, sources)
            slope = slope + value[1 + half : 2 + half]
            code = code - 4
            for values in lists:
                for row in (half, 1 - half):
                    value = jnp.where(code == 1, lane_take(values, lanes), 0.0)
                    slope = slope + value[row : row + 1]
                    code = code - 1
        column = jnp.where(
            beyond,
            lane_take(near_block(beside_ref, last, block, turn), beside_lanes),
            lane_take(beside, beside_lanes),
        )
        slope_ref[:, at] = slope + jnp.where(idx_ref[4, 0:1, at] > 0, column[3:4], 0.0)


def step_kernel(owners, parts, half_rows, chained, final, par_ref, spill_ref, idx_ref, wind_ref, slope_ref, coef_ref, g_ref, *refs):
    beside_refs, refs = refs[: len(parts)], refs[len(parts) :]
    list_refs, refs = refs[: owners - 2], refs[owners - 2 :]
    if chained:
        _, before_ref, refs = refs[0], refs[1], refs[2:]
    out_ref, sums_refs, total_ref, damp_ref = refs[0], refs[1:-2], refs[-2], refs[-1]
    blocks = g_ref.shape[1] // LANES
    shape = (8, LANES)
    step = pl.program_id(0)
    step_rows = out_ref.shape[0]
    first_step = parts[0][0]
    turn = par_ref[3]
    lane = lax.broadcasted_iota(I32, shape, 1)
    turned = (lane + turn) & (LANES - 1)
    edge = lane == jnp.where(turn < 0, LANES - 1, jnp.where(turn > 0, 0, -1))

    @pl.when(step == 0)
    def _():
        total_ref[...] = jnp.zeros_like(total_ref)
        slope = slope_ref[...]
        damp_ref[...] = jnp.broadcast_to(slope * slope, damp_ref.shape)

    def tiles(beside_ref, spills):
        for tile in range(step_rows // 8):
            here = slice(tile * 8, tile * 8 + 8)

            def at_row(first):
                return pl.ds(pl.multiple_of(first, 8), 8)

            first = (step + first_step) * step_rows + tile * 8
            half = jnp.where(first >= half_rows, 1, 0)
            way = par_ref[1 + half]
            rows = at_row(first)
            other_rows = at_row(first + (1 - 2 * half) * half_rows)
            coef = coef_ref[rows, :]

            def factor(at):
                return jnp.broadcast_to(coef[:, at : at + 1], shape)

            keep, by_row, by_col = factor(C_KEEP), factor(C_ROW), factor(C_COL)
            east, north, one, damp = factor(C_EAST), factor(C_NORTH), factor(C_ONE), factor(C_DAMP)
            s_east, s_north = factor(C_S_EAST), factor(C_S_NORTH)
            t_east, t_north = factor(C_T_EAST), factor(C_T_NORTH)
            sides = (rows, other_rows) if spills else (rows,)
            lists = [ref[which, :] for ref in list_refs for which in sides]
            places = list(range(4))
            places += [4 + 2 * at + side for at in range(owners - 2) for side in range(len(sides))]
            for block in range(blocks):
                at = slice(block * LANES, (block + 1) * LANES)
                lanes, code = idx_ref[2 * half, :, at], idx_ref[2 * half + 1, :, at]
                has_beside = idx_ref[4, :, at]
                own, beside = g_ref[here, at], beside_ref[here, at]
                sources = [own, near_block(g_ref, here, block, way)]
                sources += [beside, near_block(beside_ref, here, block, way)]
                row_value = row_neighbour(code, lanes, sources + lists, places)
                turning = near_block(beside_ref, here, block, turn)
                col_value = lane_take(jnp.where(edge, turning, beside), turned)
                col_value = jnp.where(has_beside > 0, col_value, 0.0)
                value = keep * own + by_row * row_value + by_col * col_value
                wind_east = jnp.broadcast_to(wind_ref[0:1, at], shape)
                wind_north = jnp.broadcast_to(wind_ref[1:2, at], shape)
                growth = jnp.maximum(east * wind_east + north * wind_north - one, 0.0)
                updated = value * jnp.exp(growth - damp * damp_ref[:, at])
                out_ref[here, at] = updated
                lifted = growth * value
                total_ref[0, :, at] += s_east * lifted
                total_ref[1, :, at] += s_north * lifted
                total_ref[2, :, at] += t_east * updated
                total_ref[3, :, at] += t_north * updated

    for (start, stop), beside_ref in zip(parts, beside_refs):
        for spills in (False, True):
            inside = (step >= start - first_step) & (step < stop - first_step)

            @pl.when(inside & ((spill_ref[0] > 0) == spills))
            def _():
                tiles(beside_ref, spills)

    @pl.when(step == pl.num_programs(0) - 1)
    def _():
        cpl = par_ref[4]
        for item in range(2):
            for block in range(blocks):
                at = slice(block * LANES, (block + 1) * LANES)
                pair = []
                for part in range(2):
                    value = jnp.sum(total_ref[2 * item + part, :, at], axis=0, keepdims=True)
                    if chained:
                        value = value + before_ref[2 * item + part, block : block + 1, :]
                    pair.append(value)
                where = slice(block, block + 1)
                if final:
                    sums_refs[0][item, where, :] = jnp.where(cpl == 0, pair[0], pair[1])
                    sums_refs[1][item, where, :] = jnp.where(cpl == 0, pair[1], pair[0])
                else:
                    sums_refs[0][2 * item, where, :] = pair[0]
                    sums_refs[0][2 * item + 1, where, :] = pair[1]


def pick_kernel(owners, atm_ref, ocean_ref, *refs):
    table_refs, (stress_ref, stokes_ref) = refs[:owners], refs[owners:]
    shift = owners.bit_length() - 1
    blocks = table_refs[0].shape[1]
    for item, (order_ref, out_ref) in enumerate(((atm_ref, stress_ref), (ocean_ref, stokes_ref))):
        point = order_ref[...]
        count = point.shape[1]
        slot = point >> shift
        row = (point & (owners - 1)) * blocks + (slot >> 7)
        lane = slot & (LANES - 1)
        rows = owners * blocks
        hot = jnp.where(lax.broadcasted_iota(I32, (rows, count), 0) == row, 1.0, 0.0).astype(BF16)
        table = jnp.concatenate([ref[item] for ref in table_refs], axis=0)
        table = jnp.transpose(table)
        found = times_hot(table, hot, ((1,), (0,)))
        pick = lax.broadcasted_iota(I32, (LANES, count), 0) == lane
        out_ref[...] = jnp.sum(jnp.where(pick, found, 0.0), axis=0, keepdims=True)


def coefficients(freq_local, dirs_local, pad_half, my_spec, my_cpl, freq_count, dir_count):
    freq = (my_spec * freq_local + jnp.arange(freq_local)).astype(F32)
    direction = (my_cpl * dirs_local + jnp.arange(dirs_local)).astype(F32)
    angles = 2.0 * math.pi * (direction + 0.5) / dir_count
    cosine, sine = jnp.cos(angles)[:, None], jnp.sin(angles)[:, None]
    speed = COURANT_MAX * jnp.power(1.1, -freq)[None, :]
    by_row, by_col = jnp.abs(speed * cosine), jnp.abs(speed * sine)
    sigma = (2.0 * math.pi * BASE_FREQ * jnp.power(1.1, freq))[None, :]
    sigma_top = 2.0 * math.pi * BASE_FREQ * 1.1 ** (freq_count - 1)
    inverse_speed = sigma / GRAVITY
    rate = GROWTH_RATE * sigma
    drift = jnp.power(1.1, 2.0 * (freq - (freq_count - 1)))[None, :]
    stress_scale = STRESS_GAIN / freq_count
    stokes_scale = STOKES_GAIN / math.sqrt(freq_count * dir_count)
    shape = (dirs_local, freq_local)
    columns = [
        1.0 - by_row - by_col,
        by_row,
        by_col,
        jnp.power(1.1, 0.4 * freq)[None, :] / (SLOPE_REF * freq_count * dir_count),
        rate * inverse_speed * cosine,
        rate * inverse_speed * sine,
        rate,
        sigma / sigma_top,
        stress_scale * cosine,
        stress_scale * sine,
        stokes_scale * drift * cosine,
        stokes_scale * drift * sine,
    ]
    table = jnp.stack([jnp.broadcast_to(column, shape) for column in columns], axis=-1)
    table = table.reshape(2, -1, len(columns))
    table = jnp.pad(table, ((0, 0), (0, pad_half), (0, 16 - len(columns))))
    return table.reshape(-1, 16)


def shape_of(*dims, kind=F32):
    return jax.ShapeDtypeStruct(dims, kind)


def call(kernel, inputs, outputs):
    return pl.pallas_call(
        kernel,
        in_specs=inputs,
        out_specs=[WHOLE] * len(outputs),
        out_shape=outputs,
        compiler_params=pltpu.CompilerParams(vmem_limit_bytes=VMEM_BYTES),
        cost_estimate=SHORT,
    )


def chunks_of(steps):
    ends = sorted({max(1, steps * part // 18) for part in CHUNK_ENDS} | {steps})
    return list(zip([0] + ends[:-1], ends))


def local(spec_deck, wind_deck, cell_sea, atm_order, ocean_order):
    owners = lax.axis_size("pts")
    spec_groups = lax.axis_size("spec")
    cpl_groups = lax.axis_size("cpl")
    groups = lax.axis_size("grp")
    my_pts = lax.axis_index("pts")
    my_spec = lax.axis_index("spec")
    my_cpl = lax.axis_index("cpl")
    assert cpl_groups == 2 and owners & (owners - 1) == 0
    freq_local, dirs_local, slots = spec_deck.shape
    freq_count = freq_local * spec_groups
    dir_count = dirs_local * cpl_groups
    blocks = slots // LANES
    half_rows = freq_local * dirs_local // 2
    pad_half = -half_rows % 8
    rows = 2 * (half_rows + pad_half)
    step_rows = 16 if (half_rows + pad_half) % 16 == 0 else 8
    steps = rows // step_rows

    field = jnp.transpose(spec_deck, (1, 0, 2)).reshape(2, half_rows, slots)
    if pad_half:
        field = jnp.pad(field, ((0, 0), (0, pad_half), (0, 0)))
    field = field.reshape(rows, slots)

    def around(values, distance=1):
        pairs = []
        for owner in range(owners):
            pairs.append((owner * 2, (owner + distance) % owners * 2))
            pairs.append((owner * 2 + 1, (owner - distance) % owners * 2 + 1))
        return lax.ppermute(values, ("pts", "cpl"), pairs)

    def chunk(values, at):
        return values[at[0] * step_rows : at[1] * step_rows]

    chunks = chunks_of(steps)
    def cut(values, at):
        size = (at[1] - at[0]) * step_rows
        if at[0] * step_rows % size:
            return chunk(values, at)
        return pl.pallas_call(
            copy_kernel,
            grid=(1,),
            in_specs=[pl.BlockSpec((size, slots), lambda i: (at[0] * step_rows // size, 0))],
            out_specs=WHOLE,
            out_shape=shape_of(size, slots),
            compiler_params=pltpu.CompilerParams(vmem_limit_bytes=VMEM_BYTES),
            cost_estimate=SHORT,
        )(values)

    first = cut(field, chunks[0])
    rest, first = lax.optimization_barrier((field, first))
    beside = [around(first), around(cut(rest, chunks[1]))]

    first_way = 2 * my_cpl - 1
    turn = jnp.where(
        (my_cpl == 0) & (my_pts == 0), -1, jnp.where((my_cpl == 1) & (my_pts == owners - 1), 1, 0)
    )
    par = jnp.stack([my_pts, first_way, -first_way, turn, my_cpl, -first_way]).astype(I32)
    coef = coefficients(
        freq_local, dirs_local, pad_half, my_spec, my_cpl, freq_count, dir_count
    )

    found = call(
        functools.partial(index_kernel, owners, [start * step_rows for start, _ in chunks[2:]]),
        [SCALARS, WHOLE, WHOLE, WHOLE],
        [
            shape_of(5, 8, slots, kind=I32),
            shape_of(owners * owners, cell_sea.shape[1]),
            shape_of(8, slots),
        ]
        + [shape_of(rows + 8, LANES)] * (owners - 2)
        + [
            shape_of((stop - start) * step_rows + (8 if at == 0 else 0), slots)
            for at, (start, stop) in enumerate(chunks[2:])
        ],
    )(par, cell_sea, coef, field)
    found, beside[0] = lax.optimization_barrier((found, beside[0]))
    (idx, counts, row_sums), lists = found[:3], found[3 : owners + 1]
    leaving = found[owners + 1 :]
    arrived = [around(values, 2 + at) for at, values in enumerate(lists)]
    pairs = jnp.sum(counts, axis=1).reshape(owners, owners)
    spills = jnp.where(jnp.max(pairs) > LANES, 1, 0).astype(I32).reshape(1)
    longest = jnp.max(pairs + pairs.T).reshape(1, 1)
    if groups == 2:
        longest = jnp.maximum(longest, lax.ppermute(longest, "grp", [(0, 1), (1, 0)]))
    else:
        longest = lax.pmax(longest, "grp")
    beside.append(around(leaving[0]))
    later = list(leaving[1:])
    later[0], beside[1] = lax.optimization_barrier((later[0], beside[1]))
    beside.append(around(later.pop(0)))
    later, arrived, beside[2], longest, spills = lax.optimization_barrier(
        (later, arrived, beside[2], longest, spills)
    )
    beside += [around(values) for values in later]

    (slope_part,) = call(
        slope_kernel, [SCALARS] + [WHOLE] * (owners + 1), [shape_of(1, slots)]
    )(par, idx, row_sums, beside[2], *arrived)

    slope = slope_part + lax.ppermute(slope_part, "cpl", [(0, 1), (1, 0)])
    if spec_groups == 2:
        slope = slope + lax.ppermute(slope, "spec", [(0, 1), (1, 0)])
    else:
        slope = lax.psum(slope, "spec")

    updated = sums = None
    for parts in [chunks[:3]] + [[at] for at in chunks[3:]]:
        ends = [(first * step_rows, end * step_rows) for first, end in parts]
        final = ends[-1][1] == rows
        block_rows = step_rows
        while all(end % (2 * block_rows) == 0 for part in ends for end in part) and block_rows < 32:
            block_rows *= 2
        parts = [(first // block_rows, end // block_rows) for first, end in ends]
        start, stop = parts[0][0], parts[-1][1]
        chained = start > 0
        in_rows = pl.BlockSpec(
            (block_rows, slots), functools.partial(lambda first, i: (first + i, 0), start)
        )
        near, beside = beside[: len(parts)], beside[len(parts) :]
        inputs = [par, spills, idx, wind_deck, slope, coef, field, *near, *arrived]
        specs = [SCALARS] * 2 + [WHOLE] * 4 + [in_rows]
        for first, end in parts:
            within = lambda skipped, most, i: (jnp.clip(i - skipped, 0, most), 0)
            within = functools.partial(within, first - start, end - first - 1)
            specs.append(pl.BlockSpec((block_rows, slots), within))
        specs += [WHOLE] * len(arrived)
        aliases = {}
        if chained:
            aliases = {len(inputs): 0}
            inputs += [updated, sums]
            specs += [pl.BlockSpec(memory_space=pl.ANY), WHOLE]
        sum_shapes = [(2, blocks, LANES)] * 2 if final else [(4, blocks, LANES)]
        updated, *sums = pl.pallas_call(
            functools.partial(step_kernel, owners, parts, rows // 2, chained, final),
            grid=(stop - start,),
            in_specs=specs,
            out_specs=[in_rows] + [WHOLE] * len(sum_shapes),
            out_shape=[pltpu.HBM((rows, slots), F32)] + [shape_of(*dims) for dims in sum_shapes],
            scratch_shapes=[pltpu.VMEM((4, 8, slots), F32), pltpu.VMEM((8, slots), F32)],
            input_output_aliases=aliases,
            compiler_params=pltpu.CompilerParams(vmem_limit_bytes=VMEM_BYTES),
            cost_estimate=SHORT,
        )(*inputs)
        if not final:
            sums = sums[0]

    mine, others = sums
    if spec_groups == 2:
        peers = spec_groups * cpl_groups
        mine = sum(
            lax.ppermute(values, ("spec", "cpl"), [(i, i ^ turned) for i in range(peers)])
            for values, turned in ((mine, 2), (others, 3), (others, 1))
        ) + mine
    else:
        mine = lax.psum(mine + lax.ppermute(others, "cpl", [(0, 1), (1, 0)]), "spec")
    if owners == 4:
        tables = [mine] + [
            lax.ppermute(mine, "pts", [(i, i ^ turned) for i in range(owners)])
            for turned in range(1, owners)
        ]
        looked = lambda order: (order ^ my_pts)[None, :]
    else:
        gathered = lax.all_gather(mine, "pts", axis=0)
        tables = [gathered[owner] for owner in range(owners)]
        looked = lambda order: order[None, :]
    count = atm_order.shape[0]
    stress_atm, stokes_ocn = call(
        functools.partial(pick_kernel, owners),
        [WHOLE] * (2 + owners),
        [shape_of(1, count)] * 2,
    )(looked(atm_order), looked(ocean_order), *tables)

    def by_direction(values):
        return jnp.transpose(values, (1, 0, 2)).reshape(dirs_local * freq_local, slots)

    def general_way():
        spectra, stress, stokes = general(spec_deck, wind_deck, cell_sea, atm_order, ocean_order)
        return by_direction(spectra), stress, stokes

    if pad_half:
        updated = updated.reshape(2, half_rows + pad_half, slots)[:, :half_rows]
        updated = updated.reshape(2 * half_rows, slots)
    updated, stress_atm, stokes_ocn = lax.cond(
        longest[0, 0] > 2 * LANES, general_way, lambda: (updated, stress_atm, stokes_ocn)
    )
    updated = jnp.transpose(updated.reshape(dirs_local, freq_local, slots), (1, 0, 2))
    return updated, stress_atm, stokes_ocn


def solution(mesh):
    return jax.shard_map(
        local,
        mesh=mesh,
        in_specs=(
            P("spec", "cpl", ("grp", "pts")),
            P(None, ("grp", "pts")),
            P("grp", None),
            P(("grp", "pts", "spec")),
            P(("grp", "pts", "spec")),
        ),
        out_specs=(
            P("spec", "cpl", ("grp", "pts")),
            P("cpl", ("grp", "pts", "spec")),
            P("cpl", ("grp", "pts", "spec")),
        ),
        check_vma=False,
    )
```
